32 devices in a mesh: uly: 4 (over y, x), blk: 8 (over z, core).
Axes of the slice: x: 2, y: 2, z: 4, core: 2. Of those that a mesh axis runs over, the one named last changes fastest.
Arguments:
- block_input: bfloat16 [4096, 2048], P(('uly', 'blk')), may hold values from -6 to 6
- cotangent: bfloat16 [4096, 2048], P(('uly', 'blk')), may hold values from -6 to 6
- lengths: int32 [8], replicated, may hold values from 1 to 2048, 3584 in all
- seq_order: int32 [8], replicated, may hold values from 0 to 7, each once
- norm_attn: bfloat16 [2048], P(('uly', 'blk')), may hold values from 0.5 to 1.5
- w_query: bfloat16 [2048, 2048], P(('uly', 'blk')), may hold values from -0.15625 to 0.15625
- w_key: bfloat16 [2048, 2048], P(('uly', 'blk')), may hold values from -0.15625 to 0.15625
- w_value: bfloat16 [2048, 2048], P(('uly', 'blk')), may hold values from -0.125 to 0.125
- w_out: bfloat16 [2048, 2048], P(('uly', 'blk')), may hold values from -1.5 to 1.5
- norm_ffn: bfloat16 [2048], P(('uly', 'blk')), may hold values from 0.5 to 1.5
- w_gate: bfloat16 [2048, 8192], P('blk', 'uly'), may hold values from -0.125 to 0.125
- w_up: bfloat16 [2048, 8192], P('blk', 'uly'), may hold values from -0.125 to 0.125
- w_down: bfloat16 [8192, 2048], P('uly', 'blk'), may hold values from -0.0625 to 0.0625
Outputs:
- output: bfloat16 [4096, 2048], P(('uly', 'blk'))
- input_grad: float32 [4096, 2048], P(('uly', 'blk'))
- grad_norm_attn: float32 [2048], P(('uly', 'blk'))
- grad_query: float32 [2048, 2048], P(('uly', 'blk'))
- grad_key: float32 [2048, 2048], P(('uly', 'blk'))
- grad_value: float32 [2048, 2048], P(('uly', 'blk'))
- grad_out: float32 [2048, 2048], P(('uly', 'blk'))
- grad_norm_ffn: float32 [2048], P(('uly', 'blk'))
- grad_gate: float32 [2048, 8192], P('blk', 'uly')
- grad_up: float32 [2048, 8192], P('blk', 'uly')
- grad_down: float32 [8192, 2048], P('uly', 'blk')
The draws below stay inside these ranges and needn't reach their ends.
Inputs may be any that keep to these rules, and one draw needn't show every extreme that they name: 8 lengths that sum to 3584; the longest is exactly 2048. `seq_order`: a permutation of the 8 sequences.
All inputs are finite; a program needn't handle non-finite values.
Results may differ from the reference program's by a relative error of at most 0.017.
Values may be sent and summed in bfloat16 or wider, within the bound.
No kernel may reach another device: no remote copies, remote signals or barrier semaphores. Data moves between devices by JAX's collectives and lax.ppermute only.
A program may use at most 512 MiB of HBM per device.

```python
import math
import jax
import jax.numpy as jnp
import numpy as np
from jax import lax

D = 2048
HEADS = 16
HD = 128
FF = 8192
TOK_DEV = 128
NSEQ = 8
PACK = 4096
MAXLEN = 2048
USED = 3584
N_ULY = 4


def block_scale(rng, shape, shards, smallest, largest):
    loudness = 1.0
    for dim, blocks in shards:
        heights = jax.random.uniform(jax.random.fold_in(jax.random.fold_in(rng, 6), dim), (blocks,), jnp.float32, smallest / len(shards), largest / len(shards))
        loudness = loudness * jnp.repeat(jnp.exp(heights), shape[dim] // blocks).reshape((-1,) + (1,) * (len(shape) - 1 - dim))
    return loudness


def profile(count, total, most, slope):
    portions = [(1 << 20) // math.isqrt(rank ** slope) + 1 for rank in range(2, count + 1)]
    rest, given = total - most - (count - 1), [1] * (count - 1)
    while rest > 0:
        candidates = [i for i in range(count - 1) if given[i] < most]
        mass, left = sum([portions[i] for i in candidates]), rest
        for i in candidates:
            more = min(most - given[i], max(1, left * portions[i] // mass), rest)
            given[i] = given[i] + more
            rest = rest - more
    return np.array([most] + given)


def ragged_sizes(rng, amount, total, limit, slope):
    if amount == 2:
        one = jax.random.randint(rng, (), max(1, total - limit), min(limit, total - 1) + 1)
        return jnp.stack([one, total - one])
    tallies = jnp.asarray(profile(amount, total, limit, slope), jnp.int32)
    couples = (amount - 1) // 2
    source_of, receiver = tallies[1:1 + 2 * couples:2], tallies[2:2 + 2 * couples:2]
    slack = jnp.minimum(source_of - 1, limit - receiver)
    passed = jax.random.randint(jax.random.fold_in(rng, 1), (couples,), 0, 1 << 20) % (slack + 1)
    tallies = tallies.at[1:1 + 2 * couples:2].set(source_of - passed).at[2:2 + 2 * couples:2].set(receiver + passed)
    return tallies[jax.random.permutation(jax.random.fold_in(rng, 2), amount)]


def scatter_about(key, dims, deviation, most, pieces=(), held_as=jnp.bfloat16):
    level = block_scale(key, dims, pieces, -0.22, 0.18) if pieces else 1.0
    result = jax.random.normal(key, dims, jnp.float32) * deviation * level
    return jnp.minimum(jnp.maximum(result, -most), most).astype(held_as)


def setup_inputs(seed: int = 0) -> dict:
    splits = jax.random.split(jax.random.key(seed), 14)
    block_input = scatter_about(splits[0], (PACK, D), 1.0, 6.0, ((0, 32),))
    cotangent = scatter_about(splits[1], (PACK, D), 1.0, 6.0, ((0, 32),))
    lengths = ragged_sizes(splits[2], NSEQ, USED, MAXLEN, 1).astype(jnp.int32)
    seq_order = jax.random.permutation(splits[3], NSEQ).astype(jnp.int32)
    norm_attn = jnp.clip(1.0 + 0.1 * jax.random.normal(splits[4], (D,), jnp.float32), 0.5, 1.5).astype(jnp.bfloat16)
    w_query = scatter_about(splits[5], (D, D), (D * 2 // 3) ** -0.5, 0.15625, ((0, 32),))
    w_key = scatter_about(splits[6], (D, D), (D * 2 // 3) ** -0.5, 0.15625, ((0, 32),))
    w_value = scatter_about(splits[7], (D, D), D ** -0.5, 0.125, ((0, 32),))
    w_out = scatter_about(splits[8], (D, D), 16 ** -0.5, 1.5, ((0, 32),))
    norm_ffn = jnp.clip(1.0 + 0.1 * jax.random.normal(splits[9], (D,), jnp.float32), 0.5, 1.5).astype(jnp.bfloat16)
    w_gate = scatter_about(splits[10], (D, FF), D ** -0.5, 0.125, ((0, 8), (1, 4)))
    w_up = scatter_about(splits[11], (D, FF), D ** -0.5, 0.125, ((0, 8), (1, 4)))
    w_down = scatter_about(splits[12], (FF, D), FF ** -0.5, 0.0625, ((0, 4), (1, 8)))
    return dict(block_input=block_input, cotangent=cotangent, lengths=lengths, seq_order=seq_order, norm_attn=norm_attn, w_query=w_query, w_key=w_key, w_value=w_value, w_out=w_out, norm_ffn=norm_ffn, w_gate=w_gate, w_up=w_up, w_down=w_down)


@jax.custom_vjp
def low(v):
    return lax.optimization_barrier(v.astype(jnp.bfloat16)).astype(jnp.float32)

@jax.custom_vjp
def low_back(v):
    return v

def low_keep(v):
    return (low(v), None)

def low_pass(kept, grad):
    return (grad,)

def back_keep(v):
    return (v, None)

def back_low(kept, grad):
    return (low(grad),)
low.defvjp(low_keep, low_pass)
low_back.defvjp(back_keep, back_low)
norm_eps = 1e-05
rope_base = 10000.0
score_bias = -math.log(4096.0)

def seq_bounds(lengths, seq_order):
    seq_count = lengths.shape[0]
    labels = jnp.arange(seq_count, dtype=jnp.int32)
    picked = lax.optimization_barrier(jnp.sum(jnp.where(seq_order[:, None] == labels[None, :], lengths[None, :], 0), axis=1, dtype=jnp.int32))
    seq_ends = jnp.cumsum(picked, dtype=jnp.int32)
    return (seq_ends - picked, seq_ends)

def locate(row_ids, seq_starts, seq_ends):
    inside = (row_ids[:, None] >= seq_starts[None, :]) & (row_ids[:, None] < seq_ends[None, :])
    segment = lax.optimization_barrier(jnp.sum((row_ids[:, None] >= seq_ends[None, :]).astype(jnp.int32), axis=1, dtype=jnp.int32))
    offset = lax.optimization_barrier(jnp.sum(jnp.where(inside, seq_starts[None, :], 0), axis=1, dtype=jnp.int32))
    return (segment, row_ids - offset)

def rope_tables(position, head_dim):
    half_dim = head_dim // 2
    frequency = rope_base ** (-jnp.arange(half_dim, dtype=jnp.float32) * 2.0 / head_dim)
    angles = position.astype(jnp.float32)[:, None] * frequency[None, :]
    return (jnp.cos(angles)[:, None, :], jnp.sin(angles)[:, None, :])

def rotate(values, cos_table, sin_table):
    half_dim = values.shape[-1] // 2
    leading = values[..., :half_dim]
    trailing = values[..., half_dim:]
    return jnp.concatenate([leading * cos_table - trailing * sin_table, trailing * cos_table + leading * sin_table], axis=-1)

def allowed(query_seg, query_pos, key_seg, key_pos, seq_count):
    return (query_seg[:, None] == key_seg[None, :]) & (query_seg[:, None] < seq_count) & (key_pos[None, :] <= query_pos[:, None])

def rms_norm(values, gain):
    return values * lax.rsqrt(lax.optimization_barrier(jnp.mean(values * values, axis=-1, keepdims=True)) + norm_eps) * gain

def matmul(left, right):
    return jnp.dot(left, right, precision=lax.Precision.HIGHEST, preferred_element_type=jnp.float32)

def reference(block_input, cotangent, lengths, seq_order, norm_attn, w_query, w_key, w_value, w_out, norm_ffn, w_gate, w_up, w_down):
    seq_starts, seq_ends = seq_bounds(lengths, seq_order)
    row_ids = jnp.arange(PACK, dtype=jnp.int32)
    segment, position = locate(row_ids, seq_starts, seq_ends)
    cos_table, sin_table = rope_tables(position, HD)
    head_scale = 1.0 / math.sqrt(HD)
    block_rows = TOK_DEV * N_ULY
    block_count = PACK // block_rows

    def attention(queries, keys, values):

        def one_head(head_args):
            q_head, k_head, v_head = head_args

            def one_block(block_args):
                q_block, block_index = block_args
                row_seg = lax.dynamic_slice_in_dim(segment, block_index * block_rows, block_rows)
                row_pos = lax.dynamic_slice_in_dim(position, block_index * block_rows, block_rows)
                scores = low_back(matmul(q_block, k_head.T) * head_scale + score_bias)
                key_mask = allowed(row_seg, row_pos, segment, position, NSEQ)
                weights = low(jnp.where(key_mask, jax.nn.sigmoid(scores), 0.0))
                return matmul(weights, v_head)
            out_blocks = lax.map(jax.checkpoint(one_block), (q_head.reshape(block_count, block_rows, HD), jnp.arange(block_count, dtype=jnp.int32)))
            return out_blocks.reshape(PACK, HD)
        stacked = lax.map(jax.checkpoint(one_head), (jnp.transpose(queries, (1, 0, 2)), jnp.transpose(keys, (1, 0, 2)), jnp.transpose(values, (1, 0, 2))))
        return jnp.transpose(stacked, (1, 0, 2)).reshape(PACK, HEADS * HD)

    def forward(input_f, gain_attn, query_w, key_w, value_w, out_w, gain_ffn, gate_w, up_w, down_w):
        hidden_one = low(rms_norm(input_f, gain_attn))
        queries = low(rotate(low_back(matmul(hidden_one, query_w)).reshape(PACK, HEADS, HD), cos_table, sin_table))
        keys = low(rotate(low_back(matmul(hidden_one, key_w)).reshape(PACK, HEADS, HD), cos_table, sin_table))
        values = low(low_back(matmul(hidden_one, value_w))).reshape(PACK, HEADS, HD)
        attended = low(low_back(attention(queries, keys, values)))
        resid = input_f + low_back(matmul(attended, out_w))
        hidden_two = low(rms_norm(resid, gain_ffn))
        gate_act = low_back(matmul(hidden_two, gate_w))
        up_act = low_back(matmul(hidden_two, up_w))
        inner = low(jax.nn.silu(gate_act) * up_act)
        return resid + low_back(matmul(inner, down_w))
    primals = [block_input.astype(jnp.float32), norm_attn.astype(jnp.float32), w_query.astype(jnp.float32), w_key.astype(jnp.float32), w_value.astype(jnp.float32), w_out.astype(jnp.float32), norm_ffn.astype(jnp.float32), w_gate.astype(jnp.float32), w_up.astype(jnp.float32), w_down.astype(jnp.float32)]
    output_f, pullback = jax.vjp(forward, *primals)
    gradients = pullback(cotangent.astype(jnp.float32))
    return (output_f.astype(jnp.bfloat16), gradients[0], gradients[1], gradients[2], gradients[3], gradients[4], gradients[5], gradients[6], gradients[7], gradients[8], gradients[9])
```

```python
import functools
import math

import jax
import jax.numpy as jnp
from jax import lax
from jax.experimental import pallas as pl
from jax.experimental.pallas import tpu as pltpu
from jax.sharding import PartitionSpec as P

HEADS = 16
HD = 128
BOTH = ("uly", "blk")
LONGEST = {4096: 2048, 16384: 4096}
LOG2E = math.log2(math.e)

norm_eps = 1e-05
rope_base = 10000.0
score_bias = -math.log(4096.0)
head_scale = 1.0 / math.sqrt(HD)

BQ = 256
BK = 512
BR = 256
VMEM = 60 * 2**20
f32 = jnp.float32
bf16 = jnp.bfloat16


def dot_t(left, right):
    return lax.dot_general(left, right, (((1,), (1,)), ((), ())), preferred_element_type=f32)


def t_dot(left, right):
    return lax.dot_general(left, right, (((0,), (0,)), ((), ())), preferred_element_type=f32)


def dot(left, right):
    return jnp.dot(left, right, preferred_element_type=f32)


def qkv_kernel(x_ref, gain_ref, w_ref, cos_ref, sin_ref, h_ref, q_ref, kv_ref):
    x = x_ref[...].astype(f32)
    inv = lax.rsqrt(jnp.mean(x * x, axis=-1, keepdims=True) + norm_eps)
    h = (x * inv * gain_ref[...]).astype(bf16)
    h_ref[...] = h
    acc = dot(h, w_ref[...])
    cos, sin = cos_ref[...], sin_ref[...]
    width = q_ref.shape[1]
    for s in range(0, width, HD):
        t = acc[:, s : s + HD]
        q_ref[:, s : s + HD] = (t * cos + pltpu.roll(t, HD // 2, 1) * sin).astype(bf16)
        t = acc[:, width + s : width + s + HD]
        kv_ref[:, s : s + HD] = (t * cos + pltpu.roll(t, HD // 2, 1) * sin).astype(bf16)
    kv_ref[:, width:] = acc[:, 2 * width :].astype(bf16)


def qkv_call(x, gain, w, cos, sin):
    rows, dim = x.shape
    width = w.shape[1] // 3
    block = lambda cols: pl.BlockSpec((BR, cols), lambda i: (i, 0))
    whole = lambda shape: pl.BlockSpec(shape, lambda i: (0, 0))
    return pl.pallas_call(
        qkv_kernel,
        grid=(rows // BR,),
        in_specs=[block(dim), whole((1, dim)), whole(w.shape), block(HD), block(HD)],
        out_specs=[block(dim), block(width), block(2 * width)],
        out_shape=[
            jax.ShapeDtypeStruct((rows, dim), bf16),
            jax.ShapeDtypeStruct((rows, width), bf16),
            jax.ShapeDtypeStruct((rows, 2 * width), bf16),
        ],
        compiler_params=pltpu.CompilerParams(vmem_limit_bytes=VMEM),
        cost_estimate=pl.CostEstimate(
            flops=2 * rows * dim * 3 * width, bytes_accessed=16 * 2**20, transcendentals=0
        ),
    )(x, gain, w, cos, sin)


def attn_fwd_kernel(count_kv, lo_ref, q_ref, start_ref, wo_ref, *refs):
    kv_refs, (att_ref, part_ref, kv_all) = refs[:count_kv], refs[count_kv:]
    rows, width = q_ref.shape
    heads = width // HD
    base = (count_kv - 1) * rows
    for i, r in enumerate(kv_refs):
        kv_all[i * rows : (i + 1) * rows, :] = r[...]
    for i in range(rows // BQ):
        at = slice(i * BQ, (i + 1) * BQ)
        start = start_ref[at, :]
        row = base + i * BQ + lax.broadcasted_iota(jnp.int32, (BQ, BK), 0)
        col = lax.broadcasted_iota(jnp.int32, (BQ, BK), 1)
        queries = [q_ref[at, h * HD : (h + 1) * HD] for h in range(heads)]

        def step(kb, sums):
            off = pl.multiple_of(kb * BK, BK)
            here = col + off
            ok = (here >= start) & (here <= row)
            out = []
            for h in range(heads):
                k = kv_all[pl.ds(off, BK), h * HD : (h + 1) * HD]
                v = kv_all[pl.ds(off, BK), width + h * HD : width + (h + 1) * HD]
                e = jnp.exp2(
                    dot_t(queries[h], k) * (-head_scale * LOG2E) - score_bias * LOG2E
                )
                weight = jnp.where(ok, 1.0 / (1.0 + e), 0.0).astype(bf16)
                out.append(sums[h] + dot(weight, v))
            return tuple(out)

        last = (base + (i + 1) * BQ - 1) // BK + 1
        sums = lax.fori_loop(
            lo_ref[i], last, step, tuple(jnp.zeros((BQ, HD), f32) for _ in range(heads))
        )
        att = jnp.concatenate([s.astype(bf16) for s in sums], axis=1)
        att_ref[at, :] = att
        part_ref[at, :] = dot(att, wo_ref[...]).astype(bf16)


def attn_fwd_call(lo, q, start, wo, kvs):
    rows, width = q.shape
    dim = wo.shape[1]
    vmem = pl.BlockSpec(memory_space=pltpu.VMEM)
    return pl.pallas_call(
        functools.partial(attn_fwd_kernel, len(kvs)),
        in_specs=[pl.BlockSpec(memory_space=pltpu.SMEM)] + [vmem] * (3 + len(kvs)),
        out_specs=[vmem, vmem],
        out_shape=[
            jax.ShapeDtypeStruct((rows, width), bf16),
            jax.ShapeDtypeStruct((rows, dim), bf16),
        ],
        scratch_shapes=[pltpu.VMEM((len(kvs) * rows, 2 * width), bf16)],
        compiler_params=pltpu.CompilerParams(vmem_limit_bytes=VMEM),
        cost_estimate=pl.CostEstimate(
            flops=10 * 10**9, bytes_accessed=12 * 2**20, transcendentals=4 * 10**6
        ),
    )(lo, q, start, wo, *kvs)


def attn_bwd_kernel(count_kv, lo_ref, q_ref, ga_ref, start_ref, wo_ref, cos_ref, sin_ref, *refs):
    kv_refs = refs[:count_kv]
    gq_ref, own_ref = refs[count_kv : count_kv + 2]
    rem_refs = refs[count_kv + 2 : 2 * count_kv + 1]
    kv_all, gkv = refs[2 * count_kv + 1 :]
    rows, width = q_ref.shape
    heads = width // HD
    base = (count_kv - 1) * rows
    for i, r in enumerate(kv_refs):
        kv_all[i * rows : (i + 1) * rows, :] = r[...]
        gkv[i * rows : (i + 1) * rows, :] = jnp.zeros((rows, 2 * width), f32)
    for i in range(rows // BQ):
        at = slice(i * BQ, (i + 1) * BQ)
        start = start_ref[:, at]
        row = base + i * BQ + lax.broadcasted_iota(jnp.int32, (BK, BQ), 1)
        col = lax.broadcasted_iota(jnp.int32, (BK, BQ), 0)
        gatt = dot_t(ga_ref[at, :], wo_ref[...]).astype(bf16)
        queries = [q_ref[at, h * HD : (h + 1) * HD] for h in range(heads)]
        gatts = [gatt[:, h * HD : (h + 1) * HD] for h in range(heads)]

        def step(kb, sums):
            off = pl.multiple_of(kb * BK, BK)
            here = col + off
            ok = (here >= start) & (here <= row)
            out = []
            for h in range(heads):
                ks = slice(h * HD, (h + 1) * HD)
                vs = slice(width + h * HD, width + (h + 1) * HD)
                k = kv_all[pl.ds(off, BK), ks]
                v = kv_all[pl.ds(off, BK), vs]
                e = jnp.exp2(
                    dot_t(k, queries[h]) * (-head_scale * LOG2E) - score_bias * LOG2E
                )
                sg = jnp.where(ok, 1.0 / (1.0 + e), 0.0)
                gs = (dot_t(v, gatts[h]) * sg * (1.0 - sg)).astype(bf16)
                gkv[pl.ds(off, BK), ks] += dot(gs, queries[h])
                gkv[pl.ds(off, BK), vs] += dot(sg.astype(bf16), gatts[h])
                out.append(sums[h] + t_dot(gs, k))
            return tuple(out)

        last = (base + (i + 1) * BQ - 1) // BK + 1
        sums = lax.fori_loop(
            lo_ref[i], last, step, tuple(jnp.zeros((BQ, HD), f32) for _ in range(heads))
        )
        cos, sin = cos_ref[at, :], sin_ref[at, :]
        for h in range(heads):
            t = sums[h] * head_scale
            gq_ref[at, h * HD : (h + 1) * HD] = (
                t * cos - pltpu.roll(t, HD // 2, 1) * sin
            ).astype(bf16)
    own_ref[:, :width] = gkv[base:, :width] * head_scale
    own_ref[:, width:] = gkv[base:, width:]
    for i, r in enumerate(rem_refs):
        r[:, :width] = (gkv[i * rows : (i + 1) * rows, :width] * head_scale).astype(bf16)
        r[:, width:] = gkv[i * rows : (i + 1) * rows, width:].astype(bf16)


def attn_bwd_call(lo, q, ga, start, wo, cos, sin, kvs):
    rows, width = q.shape
    vmem = pl.BlockSpec(memory_space=pltpu.VMEM)
    return pl.pallas_call(
        functools.partial(attn_bwd_kernel, len(kvs)),
        in_specs=[pl.BlockSpec(memory_space=pltpu.SMEM)] + [vmem] * (6 + len(kvs)),
        out_specs=[vmem] * (1 + len(kvs)),
        out_shape=[
            jax.ShapeDtypeStruct((rows, width), bf16),
            jax.ShapeDtypeStruct((rows, 2 * width), f32),
        ]
        + [jax.ShapeDtypeStruct((rows, 2 * width), bf16)] * (len(kvs) - 1),
        scratch_shapes=[
            pltpu.VMEM((len(kvs) * rows, 2 * width), bf16),
            pltpu.VMEM((len(kvs) * rows, 2 * width), f32),
        ],
        compiler_params=pltpu.CompilerParams(vmem_limit_bytes=VMEM),
        cost_estimate=pl.CostEstimate(
            flops=25 * 10**9, bytes_accessed=20 * 2**20, transcendentals=4 * 10**6
        ),
    )(lo, q, ga, start, wo, cos, sin, *kvs)


def ffn_kernel(places, blocks, h_ref, c_ref, *refs):
    count = len(places[0])
    sources = refs[: 3 * count]
    outs = refs[3 * count : 3 * count + 3 * blocks]
    y_ref, gh_ref = refs[3 * count + 3 * blocks : 3 * count + 3 * blocks + 2]
    wg, wu, wd, gates, ups, inners, sem = refs[3 * count + 3 * blocks + 2 :]
    inner_refs, gg_refs, gu_refs = outs[:blocks], outs[blocks : 2 * blocks], outs[2 * blocks :]
    width = wg.shape[1] // blocks

    def copies(which):
        found = []
        for p, (j, row) in enumerate(places[which]):
            src = sources[which * count + p]
            held = (wg, wu, wd)[which]
            if which < 2:
                dst = held.at[pl.ds(row, src.shape[0]), pl.ds(j * width, width)]
            else:
                dst = held.at[pl.ds(j * width + row, src.shape[0]), :]
            found.append(pltpu.make_async_copy(src, dst, sem.at[which, p]))
        return found

    first = pl.program_id(0) == 0

    @pl.when(first)
    def _():
        for which in range(3):
            for c in copies(which):
                c.start()
        for which in range(3):
            for c in copies(which):
                c.wait()

    h, c = h_ref[...], c_ref[...]
    for j in range(blocks):
        cols = slice(j * width, (j + 1) * width)
        gate = dot(h, wg[:, cols])
        up = dot(h, wu[:, cols])
        grad = dot_t(c, wd[cols, :])
        sig = 1.0 / (1.0 + jnp.exp2(gate * -LOG2E))
        act = gate * sig
        inner = (act * up).astype(bf16)
        gg = (grad * up * sig * (1.0 + gate * (1.0 - sig))).astype(bf16)
        gu = (grad * act).astype(bf16)
        inner_refs[j][...] = inner
        gg_refs[j][...] = gg
        gu_refs[j][...] = gu
        inners[:, cols] = inner
        gates[:, cols] = gg
        ups[:, cols] = gu
    gh_ref[...] = (dot_t(gates[...], wg[...]) + dot_t(ups[...], wu[...])).astype(bf16)
    y_ref[...] = dot(inners[...], wd[...]).astype(bf16)


def ffn_call(h, cot, gate, up, down):
    rows, dim = h.shape
    blocks = len(gate)
    width = gate[0][0].shape[1]
    if width % HD:
        merge = lambda parts: jnp.concatenate(parts, axis=0)
        gate = [[jnp.concatenate([merge(g) for g in gate], axis=1)]]
        up = [[jnp.concatenate([merge(g) for g in up], axis=1)]]
        down = [[jnp.concatenate([merge(g) for g in down], axis=0)]]
        joined, blocks, width = blocks, 1, width * blocks
    else:
        joined = 0
    places, sources = [], []
    for weight in (gate, up, down):
        place = []
        for j, parts in enumerate(weight):
            row = 0
            for part in parts:
                place.append((j, row))
                sources.append(part)
                row += part.shape[0]
        places.append(tuple(place))
    count = len(places[0])
    hidden = blocks * width
    block = lambda cols: pl.BlockSpec((BR, cols), lambda i: (i, 0))
    result = pl.pallas_call(
        functools.partial(ffn_kernel, tuple(places), blocks),
        grid=(rows // BR,),
        in_specs=[block(dim), block(dim)] + [pl.BlockSpec(memory_space=pl.ANY)] * len(sources),
        out_specs=[block(width)] * (3 * blocks) + [block(dim)] * 2,
        out_shape=[jax.ShapeDtypeStruct((rows, width), bf16)] * (3 * blocks)
        + [jax.ShapeDtypeStruct((rows, dim), bf16)] * 2,
        scratch_shapes=[
            pltpu.VMEM((dim, hidden), bf16),
            pltpu.VMEM((dim, hidden), bf16),
            pltpu.VMEM((hidden, dim), bf16),
            pltpu.VMEM((BR, hidden), bf16),
            pltpu.VMEM((BR, hidden), bf16),
            pltpu.VMEM((BR, hidden), bf16),
            pltpu.SemaphoreType.DMA((3, count)),
        ],
        compiler_params=pltpu.CompilerParams(vmem_limit_bytes=VMEM),
        cost_estimate=pl.CostEstimate(
            flops=12 * rows * dim * hidden, bytes_accessed=36 * 2**20, transcendentals=10**6
        ),
    )(h, cot, *sources)
    inner, gg, gu = result[:blocks], result[blocks : 2 * blocks], result[2 * blocks : 3 * blocks]
    if joined:
        split = lambda a: jnp.split(a[0], joined, axis=1)
        inner, gg, gu = split(inner), split(gg), split(gu)
    return inner, gg, gu, result[-2], result[-1]


def xor_permute(x, count, flip):
    return lax.ppermute(x, "uly", [(i, i ^ flip) for i in range(count)])


def gather_uly(x, count):
    if count != 4:
        return [[x]] + [[xor_permute(x, count, j)] for j in range(1, count)]
    half = x.shape[0] // 2
    one, two = xor_permute(x, count, 1), xor_permute(x, count, 2)
    low = xor_permute(one[:half], count, 2)
    high = xor_permute(two[half:], count, 1)
    return [[x], [one], [two], [low, high]]


def in_order(pieces, index):
    rows = sum(p.shape[0] for p in pieces[0])
    out = jnp.zeros((len(pieces) * rows,) + pieces[0][0].shape[1:], pieces[0][0].dtype)
    for j, parts in enumerate(pieces):
        at = (index ^ j) * rows
        for part in parts:
            out = lax.dynamic_update_slice_in_dim(out, part, at, 0)
            at = at + part.shape[0]
    return out


def scatter_uly(own, others, count):
    got = [xor_permute(block, count, j + 1) for j, block in enumerate(others)]
    for block in got:
        own = own + block.astype(f32)
    return own


def rms_stats(values):
    scale_inv = lax.rsqrt(jnp.mean(values * values, axis=-1, keepdims=True) + norm_eps)
    return (values * scale_inv, scale_inv)


def norm_back(grad_normed, normed, scale_inv, gain):
    scaled = grad_normed * gain
    return scale_inv * (scaled - normed * jnp.mean(scaled * normed, axis=-1, keepdims=True))


def body(
    block_input,
    cotangent,
    lengths,
    seq_order,
    norm_attn,
    w_query,
    w_key,
    w_value,
    w_out,
    norm_ffn,
    w_gate,
    w_up,
    w_down,
):
    count_uly = lax.axis_size("uly")
    count_blk = lax.axis_size("blk")
    devices = count_uly * count_blk
    uly_index = lax.axis_index("uly")
    tok_rows, dim = block_input.shape
    group = count_blk * tok_rows
    part = dim // count_blk
    rows_w = w_query.shape[0]
    longest = LONGEST.get(devices * tok_rows, devices * tok_rows)
    back = min(count_uly - 1, -(-(longest - 1) // group))

    labels = jnp.arange(lengths.shape[0], dtype=jnp.int32)
    picked = jnp.sum(
        jnp.where(seq_order[:, None] == labels[None, :], lengths[None, :], 0), axis=1
    )
    ends = jnp.sum(jnp.where(labels[None, :] <= labels[:, None], picked[None, :], 0), axis=1)
    starts = ends - picked
    row_ids = uly_index * group + jnp.arange(group, dtype=jnp.int32)
    inside = (row_ids[:, None] >= starts[None, :]) & (row_ids[:, None] < ends[None, :])
    seq_start = jnp.sum(jnp.where(inside, starts[None, :], 0), axis=1)
    position = row_ids - seq_start
    used = jnp.any(inside, axis=1)
    shift = (uly_index - back) * group
    begin = jnp.where(used, seq_start - shift, 1 << 30).astype(jnp.int32)
    firsts = begin[::BQ]
    ends_kb = (back * group + jnp.arange(group // BQ, dtype=jnp.int32) * BQ + BQ - 1) // BK + 1
    low_kb = jnp.minimum(firsts // BK, ends_kb).astype(jnp.int32)
    frequency = rope_base ** (-jnp.arange(HD // 2, dtype=f32) * 2.0 / HD)
    angles = position.astype(f32)[:, None] * frequency[None, :]
    cos, sin = jnp.cos(angles), jnp.sin(angles)
    cos = jnp.concatenate([cos, cos], axis=1)
    sin = jnp.concatenate([-sin, sin], axis=1)

    group_in = lax.all_gather(block_input, "blk", axis=0, tiled=True)
    gains = jnp.concatenate([norm_attn, norm_ffn])
    gains = lax.all_to_all(
        jnp.broadcast_to(gains[None], (devices, gains.shape[0])), BOTH, 0, 0, tiled=True
    )
    gain_attn = gains[:, :rows_w].reshape(1, dim).astype(f32)
    gain_ffn = gains[:, rows_w:].reshape(1, dim).astype(f32)
    qkv = jnp.stack([w.reshape(rows_w, count_blk, part) for w in (w_query, w_key, w_value)], axis=1)
    qkv = qkv.transpose(2, 0, 1, 3).reshape(count_blk * rows_w, 3 * part)
    qkv = lax.all_to_all(qkv, "blk", 0, 0, tiled=True)
    w_qkv = in_order(gather_uly(qkv, count_uly), uly_index)
    owner = [
        (i, (i % count_uly) * count_blk + i // count_uly) for i in range(devices)
    ]
    wo = lax.ppermute(w_out, BOTH, owner)
    wo = in_order(gather_uly(wo, count_uly), uly_index)

    hidden_one, query, kv = qkv_call(group_in, gain_attn, w_qkv, cos, sin)
    kvs = [
        lax.ppermute(kv, "uly", [(i, i + s) for i in range(count_uly - s)])
        for s in range(back, 0, -1)
    ] + [kv]

    group_cot = lax.all_gather(cotangent, "blk", axis=0, tiled=True)
    gate = gather_uly(lax.all_to_all(w_gate, "blk", 1, 0, tiled=True), count_uly)
    up = gather_uly(lax.all_to_all(w_up, "blk", 1, 0, tiled=True), count_uly)
    down = gather_uly(lax.all_to_all(w_down, "blk", 0, 1, tiled=True), count_uly)

    attended, out_part = attn_fwd_call(low_kb, query, begin[:, None], wo, kvs)
    input_f = block_input.astype(f32)
    resid = input_f + lax.psum_scatter(out_part, "blk", scatter_dimension=0, tiled=True).astype(f32)
    normed_two, inv_two = rms_stats(resid)
    hidden_two = (normed_two * gain_ffn).astype(bf16)
    group_hidden = lax.all_gather(hidden_two, "blk", axis=0, tiled=True)

    inner, gg, gu, y_part, gh_part = ffn_call(group_hidden, group_cot, gate, up, down)
    grad_h2 = lax.psum_scatter(gh_part, "blk", scatter_dimension=0, tiled=True).astype(f32)
    output = (
        resid + lax.psum_scatter(y_part, "blk", scatter_dimension=0, tiled=True).astype(f32)
    ).astype(bf16)
    grad_resid = cotangent.astype(f32) + norm_back(grad_h2, normed_two, inv_two, gain_ffn)
    gain_part = jnp.sum(grad_h2 * normed_two, axis=0).reshape(devices, rows_w)
    grad_gain_ffn = jnp.sum(
        lax.all_to_all(gain_part, BOTH, 0, 0, tiled=True).reshape(devices, rows_w), axis=0
    )
    group_gattn = lax.all_gather(grad_resid.astype(bf16), "blk", axis=0, tiled=True)

    def summed(term, lefts, rights):
        parts = [term(left, right) for left, right in zip(lefts, rights)]
        return scatter_uly(parts[0], [p.astype(bf16) for p in parts[1:]], count_uly).astype(bf16)

    hiddens, cots = [group_hidden] * count_uly, [group_cot] * count_uly
    grad_gate = lax.all_to_all(summed(t_dot, hiddens, gg), "blk", 0, 1, tiled=True).astype(f32)
    grad_up = lax.all_to_all(summed(t_dot, hiddens, gu), "blk", 0, 1, tiled=True).astype(f32)
    grad_down = lax.all_to_all(summed(t_dot, inner, cots), "blk", 1, 0, tiled=True).astype(f32)

    def split_rows(whole):
        rows = whole.shape[0] // count_uly
        pick = lambda j: lax.dynamic_slice_in_dim(whole, (uly_index ^ j) * rows, rows, 0)
        return scatter_uly(
            pick(0), [pick(j).astype(bf16) for j in range(1, count_uly)], count_uly
        ).astype(bf16)

    grad_out = lax.ppermute(
        split_rows(t_dot(attended, group_gattn)), BOTH, [(j, i) for i, j in owner]
    ).astype(f32)

    gq, gkv, *sent = attn_bwd_call(
        low_kb, query, group_gattn, begin[None, :], wo, cos, sin, kvs
    )
    for s, block in zip(range(back, 0, -1), sent):
        gkv = gkv + lax.ppermute(
            block, "uly", [(i, i - s) for i in range(s, count_uly)]
        ).astype(f32)
    gk = gkv[:, :part].reshape(group, part // HD, HD)
    gk = gk * cos[:, None, :] - jnp.roll(gk, HD // 2, axis=2) * sin[:, None, :]
    gqkv = jnp.concatenate(
        [gq, gk.reshape(group, part).astype(bf16), gkv[:, part:].astype(bf16)], axis=1
    )
    gh1_part = dot_t(gqkv, w_qkv).astype(bf16)
    grad_h1 = lax.psum_scatter(gh1_part, "blk", scatter_dimension=0, tiled=True).astype(f32)
    normed_one, inv_one = rms_stats(input_f)
    input_grad = grad_resid + norm_back(grad_h1, normed_one, inv_one, gain_attn)
    grads = split_rows(t_dot(hidden_one, gqkv))
    grads = lax.all_to_all(grads, "blk", 0, 0, tiled=True).astype(f32)
    grads = grads.reshape(count_blk, rows_w, 3, part).transpose(2, 1, 0, 3).reshape(3, rows_w, dim)
    grad_gain_attn = (
        jnp.sum(
            grads[0] * w_query.astype(f32)
            + grads[1] * w_key.astype(f32)
            + grads[2] * w_value.astype(f32),
            axis=1,
        )
        / norm_attn.astype(f32)
    )
    return (
        output,
        input_grad,
        grad_gain_attn,
        grads[0],
        grads[1],
        grads[2],
        grad_out,
        grad_gain_ffn,
        grad_gate,
        grad_up,
        grad_down,
    )


def solution(mesh):
    rows = P(("uly", "blk"), None)
    vector = P(("uly", "blk"))
    weights = (vector, rows, rows, rows, rows, vector, P("blk", "uly"), P("blk", "uly"), P("uly", "blk"))
    return jax.shard_map(
        body,
        mesh=mesh,
        in_specs=(rows, rows, P(), P()) + weights,
        out_specs=(rows, rows) + weights,
        check_vma=False,
    )
```

```python
import functools
import math

import jax
import jax.numpy as jnp
from jax import lax
from jax.experimental import pallas as pl
from jax.experimental.pallas import tpu as pltpu
from jax.sharding import PartitionSpec as P

HEADS = 16
HD = 128
BOTH = ("uly", "blk")
LONGEST = {4096: 2048, 16384: 4096}
LOG2E = math.log2(math.e)

norm_eps = 1e-05
rope_base = 10000.0
score_bias = -math.log(4096.0)
head_scale = 1.0 / math.sqrt(HD)

BQ = 512
BK = 512
BR = 256
VMEM = 60 * 2**20
f32 = jnp.float32
bf16 = jnp.bfloat16


def dot_t(left, right):
    return lax.dot_general(left, right, (((1,), (1,)), ((), ())), preferred_element_type=f32)


def t_dot(left, right):
    return lax.dot_general(left, right, (((0,), (0,)), ((), ())), preferred_element_type=f32)


def dot(left, right):
    return jnp.dot(left, right, preferred_element_type=f32)


def pack_kernel(wq_ref, wk_ref, wv_ref, gain_ref, out_ref):
    rows = wq_ref.shape[0]
    width = out_ref.shape[2] // 3
    for b in range(out_ref.shape[0]):
        for i, w in enumerate((wq_ref, wk_ref, wv_ref)):
            out_ref[b, :rows, i * width : (i + 1) * width] = w[:, b * width : (b + 1) * width]
        out_ref[b, rows:, :] = gain_ref[...]


def pack_call(wq, wk, wv, gains, count):
    rows, dim = wq.shape
    vmem = pl.BlockSpec(memory_space=pltpu.VMEM)
    return pl.pallas_call(
        pack_kernel,
        in_specs=[vmem] * 4,
        out_specs=vmem,
        out_shape=jax.ShapeDtypeStruct((count, rows + gains.shape[0], 3 * dim // count), bf16),
    )(wq, wk, wv, gains)


def unpack_kernel(got_ref, wq_ref, wk_ref, wv_ref, gain_ref, gq_ref, gk_ref, gv_ref, gg_ref):
    width = got_ref.shape[2] // 3
    total = jnp.zeros(gg_ref.shape, f32)
    for i, (w, g_ref) in enumerate(((wq_ref, gq_ref), (wk_ref, gk_ref), (wv_ref, gv_ref))):
        for b in range(got_ref.shape[0]):
            at = slice(b * width, (b + 1) * width)
            g = got_ref[b, :, i * width : (i + 1) * width].astype(f32)
            g_ref[:, at] = g
            total = total + jnp.sum(g * w[:, at].astype(f32), axis=1, keepdims=True)
    gg_ref[...] = total / gain_ref[...]


def unpack_call(got, wq, wk, wv, gain):
    vmem = pl.BlockSpec(memory_space=pltpu.VMEM)
    return pl.pallas_call(
        unpack_kernel,
        in_specs=[vmem] * 5,
        out_specs=[vmem] * 4,
        out_shape=[jax.ShapeDtypeStruct(wq.shape, f32)] * 3
        + [jax.ShapeDtypeStruct((wq.shape[0], 1), f32)],
    )(got, wq, wk, wv, gain)


def qkv_kernel(x_ref, gain_ref, w_ref, cos_ref, sin_ref, h_ref, q_ref, kv_ref):
    x = x_ref[...].astype(f32)
    inv = lax.rsqrt(jnp.mean(x * x, axis=-1, keepdims=True) + norm_eps)
    h = (x * inv * gain_ref[...]).astype(bf16)
    h_ref[...] = h
    acc = dot(h, w_ref[...])
    cos, sin = cos_ref[...], sin_ref[...]
    width = q_ref.shape[1]
    for s in range(0, width, HD):
        t = acc[:, s : s + HD]
        q_ref[:, s : s + HD] = (t * cos + pltpu.roll(t, HD // 2, 1) * sin).astype(bf16)
        t = acc[:, width + s : width + s + HD]
        kv_ref[:, s : s + HD] = (t * cos + pltpu.roll(t, HD // 2, 1) * sin).astype(bf16)
    kv_ref[:, width:] = acc[:, 2 * width :].astype(bf16)


def qkv_call(x, gain, w, cos, sin):
    rows, dim = x.shape
    width = w.shape[1] // 3
    block = lambda cols: pl.BlockSpec((BR, cols), lambda i: (i, 0))
    whole = lambda shape: pl.BlockSpec(shape, lambda i: (0, 0))
    return pl.pallas_call(
        qkv_kernel,
        grid=(rows // BR,),
        in_specs=[block(dim), whole((1, dim)), whole(w.shape), block(HD), block(HD)],
        out_specs=[block(dim), block(width), block(2 * width)],
        out_shape=[
            jax.ShapeDtypeStruct((rows, dim), bf16),
            jax.ShapeDtypeStruct((rows, width), bf16),
            jax.ShapeDtypeStruct((rows, 2 * width), bf16),
        ],
        compiler_params=pltpu.CompilerParams(vmem_limit_bytes=VMEM),
        cost_estimate=pl.CostEstimate(
            flops=2 * rows * dim * 3 * width, bytes_accessed=16 * 2**20, transcendentals=0
        ),
    )(x, gain, w, cos, sin)


def attn_fwd_kernel(count_kv, lo_ref, q_ref, start_ref, *refs):
    kv_refs, (att_ref, kv_all) = refs[:count_kv], refs[count_kv:]
    rows, width = q_ref.shape
    heads = width // HD
    base = (count_kv - 1) * rows
    for i, r in enumerate(kv_refs):
        kv_all[i * rows : (i + 1) * rows, :] = r[...]
    for i in range(rows // BQ):
        at = slice(i * BQ, (i + 1) * BQ)
        start = start_ref[at, :]
        row = base + i * BQ + lax.broadcasted_iota(jnp.int32, (BQ, BK), 0)
        col = lax.broadcasted_iota(jnp.int32, (BQ, BK), 1)
        queries = [q_ref[at, h * HD : (h + 1) * HD] for h in range(heads)]

        def step(kb, sums):
            off = pl.multiple_of(kb * BK, BK)
            here = col + off
            ok = (here >= start) & (here <= row)
            out = []
            for h in range(heads):
                k = kv_all[pl.ds(off, BK), h * HD : (h + 1) * HD]
                v = kv_all[pl.ds(off, BK), width + h * HD : width + (h + 1) * HD]
                e = jnp.exp2(
                    dot_t(queries[h], k) * (-head_scale * LOG2E) - score_bias * LOG2E
                )
                weight = jnp.where(ok, 1.0 / (1.0 + e), 0.0).astype(bf16)
                out.append(sums[h] + dot(weight, v))
            return tuple(out)

        last = (base + (i + 1) * BQ - 1) // BK + 1
        sums = lax.fori_loop(
            lo_ref[i], last, step, tuple(jnp.zeros((BQ, HD), f32) for _ in range(heads))
        )
        att_ref[at, :] = jnp.concatenate([s.astype(bf16) for s in sums], axis=1)


def attn_fwd_call(lo, q, start, kvs):
    rows, width = q.shape
    vmem = pl.BlockSpec(memory_space=pltpu.VMEM)
    return pl.pallas_call(
        functools.partial(attn_fwd_kernel, len(kvs)),
        in_specs=[pl.BlockSpec(memory_space=pltpu.SMEM)] + [vmem] * (2 + len(kvs)),
        out_specs=vmem,
        out_shape=jax.ShapeDtypeStruct((rows, width), bf16),
        scratch_shapes=[pltpu.VMEM((len(kvs) * rows, 2 * width), bf16)],
        compiler_params=pltpu.CompilerParams(vmem_limit_bytes=VMEM),
        cost_estimate=pl.CostEstimate(
            flops=10 * 10**9, bytes_accessed=12 * 2**20, transcendentals=4 * 10**6
        ),
    )(lo, q, start, *kvs)


def project_kernel(count, places, at_ref, att_ref, x_ref, gain_ref, *refs):
    sources, (h_ref, own_ref, wo_out_ref, wo, att, sem) = refs[: len(places)], refs[len(places) :]
    uly, blk = at_ref[0], at_ref[1]
    heads, _, width = att_ref.shape
    dim = wo.shape[0]
    step = pl.program_id(0)

    @pl.when(step == 0)
    def _():
        copies = []
        for n, (source, (j, half, row)) in enumerate(zip(sources, places)):
            rows = source.shape[0]
            block = dim // count
            at = (uly ^ j) * block + row
            if half:
                core = lax.rem(blk, 2)
                at = at + (core if half == 1 else 1 - core) * (block // 2)
            to = wo.at[pl.ds(pl.multiple_of(at, rows), rows), :]
            copies.append(pltpu.make_async_copy(source, to, sem.at[n]))
        for c in copies:
            c.start()
        for c in copies:
            c.wait()
        wo_out_ref[...] = wo[pl.ds(pl.multiple_of(blk * width, width), width), :]

    for n in range(heads):
        att[:, n * width : (n + 1) * width] = att_ref[n]
    resid = x_ref[...].astype(f32) + dot(att[...], wo[...])
    inv = lax.rsqrt(jnp.mean(resid * resid, axis=-1, keepdims=True) + norm_eps)
    h_ref[...] = (resid * inv * gain_ref[...]).astype(bf16)
    own = own_ref.shape[0]
    for n in range(BR // own):

        @pl.when(step * (BR // own) + n == blk)
        def _():
            own_ref[...] = resid[n * own : (n + 1) * own, :]


def project_call(at, att, x, gain, sources, places, own, count):
    heads, rows, width = att.shape
    dim = x.shape[1]
    block = lambda cols: pl.BlockSpec((BR, cols), lambda i: (i, 0))
    whole = lambda *shape: pl.BlockSpec(shape, lambda i: (0, 0))
    return pl.pallas_call(
        functools.partial(project_kernel, count, places),
        grid=(rows // BR,),
        in_specs=[
            pl.BlockSpec(memory_space=pltpu.SMEM),
            pl.BlockSpec((heads, BR, width), lambda i: (0, i, 0)),
            block(dim),
            whole(1, dim),
        ]
        + [pl.BlockSpec(memory_space=pl.ANY)] * len(sources),
        out_specs=[block(dim), whole(own, dim), whole(width, dim)],
        out_shape=[
            jax.ShapeDtypeStruct((rows, dim), bf16),
            jax.ShapeDtypeStruct((own, dim), f32),
            jax.ShapeDtypeStruct((width, dim), bf16),
        ],
        scratch_shapes=[
            pltpu.VMEM((dim, dim), bf16),
            pltpu.VMEM((BR, dim), bf16),
            pltpu.SemaphoreType.DMA((len(places),)),
        ],
        compiler_params=pltpu.CompilerParams(vmem_limit_bytes=VMEM),
        cost_estimate=pl.CostEstimate(
            flops=2 * rows * dim * dim, bytes_accessed=24 * 2**20, transcendentals=0
        ),
    )(at, att, x, gain, *sources)


def attn_bwd_kernel(count_kv, lo_ref, q_ref, ga_ref, start_ref, wo_ref, cos_ref, sin_ref, *refs):
    kv_refs = refs[:count_kv]
    gq_ref, own_ref = refs[count_kv : count_kv + 2]
    rem_refs = refs[count_kv + 2 : 2 * count_kv + 1]
    kv_all, gkv = refs[2 * count_kv + 1 :]
    rows, width = q_ref.shape
    heads = width // HD
    base = (count_kv - 1) * rows
    for i, r in enumerate(kv_refs):
        kv_all[i * rows : (i + 1) * rows, :] = r[...]
        gkv[i * rows : (i + 1) * rows, :] = jnp.zeros((rows, 2 * width), f32)
    for i in range(rows // BQ):
        at = slice(i * BQ, (i + 1) * BQ)
        start = start_ref[:, at]
        row = base + i * BQ + lax.broadcasted_iota(jnp.int32, (BK, BQ), 1)
        col = lax.broadcasted_iota(jnp.int32, (BK, BQ), 0)
        gatt = dot_t(ga_ref[at, :], wo_ref[...]).astype(bf16)
        queries = [q_ref[at, h * HD : (h + 1) * HD] for h in range(heads)]
        gatts = [gatt[:, h * HD : (h + 1) * HD] for h in range(heads)]

        def step(kb, sums):
            off = pl.multiple_of(kb * BK, BK)
            here = col + off
            ok = (here >= start) & (here <= row)
            out = []
            for h in range(heads):
                ks = slice(h * HD, (h + 1) * HD)
                vs = slice(width + h * HD, width + (h + 1) * HD)
                k = kv_all[pl.ds(off, BK), ks]
                v = kv_all[pl.ds(off, BK), vs]
                e = jnp.exp2(
                    dot_t(k, queries[h]) * (-head_scale * LOG2E) - score_bias * LOG2E
                )
                sg = jnp.where(ok, 1.0 / (1.0 + e), 0.0)
                gs = (dot_t(v, gatts[h]) * sg * (1.0 - sg)).astype(bf16)
                gkv[pl.ds(off, BK), ks] += dot(gs, queries[h])
                gkv[pl.ds(off, BK), vs] += dot(sg.astype(bf16), gatts[h])
                out.append(sums[h] + t_dot(gs, k))
            return tuple(out)

        last = (base + (i + 1) * BQ - 1) // BK + 1
        sums = lax.fori_loop(
            lo_ref[i], last, step, tuple(jnp.zeros((BQ, HD), f32) for _ in range(heads))
        )
        cos, sin = cos_ref[at, :], sin_ref[at, :]
        for h in range(heads):
            t = sums[h] * head_scale
            gq_ref[at, h * HD : (h + 1) * HD] = (
                t * cos - pltpu.roll(t, HD // 2, 1) * sin
            ).astype(bf16)
    own_ref[:, :width] = gkv[base:, :width] * head_scale
    own_ref[:, width:] = gkv[base:, width:]
    for i, r in enumerate(rem_refs):
        r[:, :width] = (gkv[i * rows : (i + 1) * rows, :width] * head_scale).astype(bf16)
        r[:, width:] = gkv[i * rows : (i + 1) * rows, width:].astype(bf16)


def attn_bwd_call(lo, q, ga, start, wo, cos, sin, kvs):
    rows, width = q.shape
    vmem = pl.BlockSpec(memory_space=pltpu.VMEM)
    return pl.pallas_call(
        functools.partial(attn_bwd_kernel, len(kvs)),
        in_specs=[pl.BlockSpec(memory_space=pltpu.SMEM)] + [vmem] * (6 + len(kvs)),
        out_specs=[vmem] * (1 + len(kvs)),
        out_shape=[
            jax.ShapeDtypeStruct((rows, width), bf16),
            jax.ShapeDtypeStruct((rows, 2 * width), f32),
        ]
        + [jax.ShapeDtypeStruct((rows, 2 * width), bf16)] * (len(kvs) - 1),
        scratch_shapes=[
            pltpu.VMEM((len(kvs) * rows, 2 * width), bf16),
            pltpu.VMEM((len(kvs) * rows, 2 * width), f32),
        ],
        compiler_params=pltpu.CompilerParams(vmem_limit_bytes=VMEM),
        cost_estimate=pl.CostEstimate(
            flops=25 * 10**9, bytes_accessed=20 * 2**20, transcendentals=4 * 10**6
        ),
    )(lo, q, ga, start, wo, cos, sin, *kvs)


def gqkv_kernel(count, index_ref, h_ref, gq_ref, own_ref, cos_ref, sin_ref, w_ref, *refs):
    got, gh_ref, grad_refs, g_ref = refs[: -2 - count], refs[-2 - count], refs[-1 - count : -1], refs[-1]
    rows, width = gq_ref.shape
    for at in range(0, rows, BR):
        at = slice(at, at + BR)
        gkv = own_ref[at, :]
        for r in got:
            gkv = gkv + r[at, :].astype(f32)
        cos, sin = cos_ref[at, :], sin_ref[at, :]
        g_ref[at, :width] = gq_ref[at, :]
        for s in range(0, width, HD):
            t = gkv[:, s : s + HD]
            g_ref[at, width + s : width + s + HD] = (
                t * cos - pltpu.roll(t, HD // 2, 1) * sin
            ).astype(bf16)
        g_ref[at, 2 * width :] = gkv[:, width:].astype(bf16)
        gh_ref[at, :] = dot_t(g_ref[at, :], w_ref[...]).astype(bf16)
    size = h_ref.shape[1] // count
    for j in list(range(1, count)) + [0]:
        at = pl.multiple_of((index_ref[0] ^ j) * size, size)
        grad_refs[j][...] = t_dot(h_ref[:, pl.ds(at, size)], g_ref[...]).astype(grad_refs[j].dtype)


def gqkv_call(index, h, gq, own, got, cos, sin, w, count):
    rows, width = gq.shape
    dim = h.shape[1]
    size = dim // count
    vmem = pl.BlockSpec(memory_space=pltpu.VMEM)
    gh, *grads = pl.pallas_call(
        functools.partial(gqkv_kernel, count),
        in_specs=[pl.BlockSpec(memory_space=pltpu.SMEM)] + [vmem] * (6 + len(got)),
        out_specs=[vmem] * (1 + count),
        out_shape=[
            jax.ShapeDtypeStruct((rows, dim), bf16),
            jax.ShapeDtypeStruct((size, 3 * width), f32),
        ]
        + [jax.ShapeDtypeStruct((size, 3 * width), bf16)] * (count - 1),
        scratch_shapes=[pltpu.VMEM((rows, 3 * width), bf16)],
        compiler_params=pltpu.CompilerParams(vmem_limit_bytes=VMEM),
        cost_estimate=pl.CostEstimate(
            flops=12 * rows * width * dim, bytes_accessed=20 * 2**20, transcendentals=0
        ),
    )(index, h, gq, own, cos, sin, w, *got)
    return gh, grads


def ffn_kernel(places, blocks, groups, h_ref, c_ref, *refs):
    count = 1 + max(p[1] for p in places)
    sources = refs[:count]
    outs = refs[count : count + 3 * len(groups)]
    inner_ref, gh_ref, wg, wu, wd, gates, ups, sem = refs[count + 3 * len(groups) :]
    width = wg.shape[1] // blocks
    copies = [
        (which, pltpu.make_async_copy(sources[source].at[at], (wg, wu, wd)[which].at[to], sem.at[i]))
        for i, (which, source, at, to) in enumerate(places)
    ]
    first = pl.program_id(0) == 0

    def wait(weight):
        @pl.when(first)
        def _():
            for which, c in copies:
                if which == weight:
                    c.wait()

    @pl.when(first)
    def _():
        for weight in range(3):
            for which, c in copies:
                if which == weight:
                    c.start()

    wait(0)
    gate = dot(h_ref[...], wg[...])
    wait(1)
    up = dot(h_ref[...], wu[...])
    wait(2)
    grad = dot_t(c_ref[...], wd[...])
    sig = 1.0 / (1.0 + jnp.exp2(gate * -LOG2E))
    act = gate * sig
    inner = (act * up).astype(bf16)
    gg = (grad * up * sig * (1.0 + gate * (1.0 - sig))).astype(bf16)
    gu = (grad * act).astype(bf16)
    inner_ref[...] = inner
    gates[...] = gg
    ups[...] = gu
    for n, members in enumerate(groups):
        for m, j in enumerate(members):
            at, to = slice(j * width, (j + 1) * width), slice(m * width, (m + 1) * width)
            outs[n][:, to] = inner[:, at]
            outs[len(groups) + n][:, to] = gg[:, at]
            outs[2 * len(groups) + n][:, to] = gu[:, at]
    gh_ref[...] = (dot_t(gates[...], wg[...]) + dot_t(ups[...], wu[...])).astype(bf16)


def ffn_call(h, cot, sources, places, blocks, width, groups):
    rows, dim = h.shape
    hidden = blocks * width
    block = lambda cols: pl.BlockSpec((BR, cols), lambda i: (i, 0))
    sizes = [len(members) * width for members in groups] * 3 + [hidden, dim]
    result = pl.pallas_call(
        functools.partial(ffn_kernel, places, blocks, groups),
        grid=(rows // BR,),
        in_specs=[block(dim), block(dim)] + [pl.BlockSpec(memory_space=pl.ANY)] * len(sources),
        out_specs=[block(size) for size in sizes],
        out_shape=[jax.ShapeDtypeStruct((rows, size), bf16) for size in sizes],
        scratch_shapes=[
            pltpu.VMEM((dim, hidden), bf16),
            pltpu.VMEM((dim, hidden), bf16),
            pltpu.VMEM((hidden, dim), bf16),
            pltpu.VMEM((BR, hidden), bf16),
            pltpu.VMEM((BR, hidden), bf16),
            pltpu.SemaphoreType.DMA((len(places),)),
        ],
        compiler_params=pltpu.CompilerParams(vmem_limit_bytes=VMEM),
        cost_estimate=pl.CostEstimate(
            flops=10 * rows * dim * hidden, bytes_accessed=36 * 2**20, transcendentals=10**6
        ),
    )(h, cot, *sources)
    n = len(groups)
    down = [p for p in places if p[0] == 2]
    base = min(p[1] for p in down)
    y = down_call(result[-2], sources[base:], [(p[1] - base,) + p[2:] for p in down])
    return result[:n], result[n : 2 * n], result[2 * n : 3 * n], y, result[-1]


def down_kernel(places, inner_ref, *refs):
    sources, (y_ref, wd, sem) = refs[:-3], refs[-3:]

    @pl.when(pl.program_id(0) == 0)
    def _():
        copies = [
            pltpu.make_async_copy(sources[source].at[at], wd.at[to], sem.at[i])
            for i, (source, at, to) in enumerate(places)
        ]
        for c in copies:
            c.start()
        for c in copies:
            c.wait()

    y_ref[...] = dot(inner_ref[...], wd[...]).astype(bf16)


def down_call(inner, sources, places):
    rows, hidden = inner.shape
    dim = max(to[1].stop or 0 for _, _, to in places) or sources[0].shape[-1]
    block = lambda cols: pl.BlockSpec((BR, cols), lambda i: (i, 0))
    return pl.pallas_call(
        functools.partial(down_kernel, tuple(places)),
        grid=(rows // BR,),
        in_specs=[block(hidden)] + [pl.BlockSpec(memory_space=pl.ANY)] * len(sources),
        out_specs=block(dim),
        out_shape=jax.ShapeDtypeStruct((rows, dim), bf16),
        scratch_shapes=[
            pltpu.VMEM((hidden, dim), bf16),
            pltpu.SemaphoreType.DMA((len(places),)),
        ],
        compiler_params=pltpu.CompilerParams(vmem_limit_bytes=VMEM),
        cost_estimate=pl.CostEstimate(
            flops=2 * rows * dim * hidden, bytes_accessed=12 * 2**20, transcendentals=0
        ),
    )(inner, *sources)


PAIRS = ((0, 2), (1, 3), (2, 3), (0, 1))


def ffn_pieces(h, cot, gate_up, down, width):
    sources, places = [], []
    for pieces, kinds in ((gate_up, (0, 1)), (down, (2,))):
        for j, parts in enumerate(pieces):
            block = 0
            for part in parts:
                size = part.shape[2] if kinds == (2,) else part.shape[1] // 2
                for i in range(part.shape[0]):
                    rows = slice(block * size, (block + 1) * size)
                    cols = slice(j * width, (j + 1) * width)
                    for which in kinds:
                        at = (i, slice(which * size, (which + 1) * size)) if which < 2 else (i,)
                        to = (rows, cols) if which < 2 else (cols, rows)
                        places.append((which, len(sources), at, to))
                    block += 1
                sources.append(part)
    return ffn_call(h, cot, sources, tuple(places), len(down), width, PAIRS)


def ffn_plain(h, cot, gate_up, down):
    size = gate_up[0][0].shape[1] // 2
    merge = lambda parts: jnp.concatenate(parts, axis=0)
    flat = lambda p, at: merge(p)[:, at].reshape(-1, p[0].shape[-1])
    tall = lambda p: merge(p).transpose(1, 0, 2).reshape(p[0].shape[1], -1)
    sources = [
        jnp.concatenate([flat(p, slice(0, size)) for p in gate_up], axis=1),
        jnp.concatenate([flat(p, slice(size, 2 * size)) for p in gate_up], axis=1),
        jnp.concatenate([tall(p) for p in down], axis=0),
    ]
    every = (slice(None), slice(None))
    places = tuple((which, which, every, every) for which in range(3))
    return ffn_call(h, cot, sources, places, 1, sources[0].shape[1], ((0,),))


def xor_permute(x, count, flip):
    return lax.ppermute(x, "uly", [(i, i ^ flip) for i in range(count)])


def gather_uly(x, count):
    return gather_rest(gather_first(x, count), count)


def gather_first(x, count):
    return [x] + [xor_permute(x, count, j) for j in ((1, 2) if count == 4 else range(1, count))]


def gather_rest(blocks, count):
    if count != 4:
        return [[block] for block in blocks]
    x, one, two = blocks
    half = x.shape[0] // 2
    low = xor_permute(one[:half], count, 2)
    high = xor_permute(two[half:], count, 1)
    return [[x], [one], [two], [low, high]]


def in_order(pieces, index):
    rows = sum(p.shape[0] for p in pieces[0])
    out = jnp.zeros((len(pieces) * rows,) + pieces[0][0].shape[1:], pieces[0][0].dtype)
    for j, parts in enumerate(pieces):
        at = (index ^ j) * rows
        for part in parts:
            out = lax.dynamic_update_slice_in_dim(out, part, at, 0)
            at = at + part.shape[0]
    return out


def scatter_uly(own, others, count):
    got = [xor_permute(block, count, j + 1) for j, block in enumerate(others)]
    for block in got:
        own = own + block.astype(f32)
    return own


def after(x, *earlier):
    return lax.optimization_barrier((x,) + earlier)[0]


def rms_stats(values):
    scale_inv = lax.rsqrt(jnp.mean(values * values, axis=-1, keepdims=True) + norm_eps)
    return (values * scale_inv, scale_inv)


def norm_back(grad_normed, normed, scale_inv, gain):
    scaled = grad_normed * gain
    return scale_inv * (scaled - normed * jnp.mean(scaled * normed, axis=-1, keepdims=True))


def body(
    block_input,
    cotangent,
    lengths,
    seq_order,
    norm_attn,
    w_query,
    w_key,
    w_value,
    w_out,
    norm_ffn,
    w_gate,
    w_up,
    w_down,
):
    count_uly = lax.axis_size("uly")
    count_blk = lax.axis_size("blk")
    devices = count_uly * count_blk
    uly_index = lax.axis_index("uly")
    blk_index = lax.axis_index("blk")
    uly_at = uly_index.astype(jnp.int32).reshape(1)
    both_at = jnp.stack([uly_index, blk_index]).astype(jnp.int32)
    tok_rows, dim = block_input.shape
    group = count_blk * tok_rows
    part = dim // count_blk
    rows_w = w_query.shape[0]
    together = lax.optimization_barrier
    longest = LONGEST.get(devices * tok_rows, devices * tok_rows)
    back = min(count_uly - 1, -(-(longest - 1) // group))

    labels = jnp.arange(lengths.shape[0], dtype=jnp.int32)
    picked = jnp.sum(
        jnp.where(seq_order[:, None] == labels[None, :], lengths[None, :], 0), axis=1
    )
    ends = jnp.sum(jnp.where(labels[None, :] <= labels[:, None], picked[None, :], 0), axis=1)
    starts = ends - picked
    row_ids = uly_index * group + jnp.arange(group, dtype=jnp.int32)
    inside = (row_ids[:, None] >= starts[None, :]) & (row_ids[:, None] < ends[None, :])
    seq_start = jnp.sum(jnp.where(inside, starts[None, :], 0), axis=1)
    position = row_ids - seq_start
    used = jnp.any(inside, axis=1)
    shift = (uly_index - back) * group
    begin = jnp.where(used, seq_start - shift, 1 << 30).astype(jnp.int32)
    firsts = begin[::BQ]
    ends_kb = (back * group + jnp.arange(group // BQ, dtype=jnp.int32) * BQ + BQ - 1) // BK + 1
    low_kb = jnp.minimum(firsts // BK, ends_kb).astype(jnp.int32)
    frequency = rope_base ** (-jnp.arange(HD // 2, dtype=f32) * 2.0 / HD)
    angles = position.astype(f32)[:, None] * frequency[None, :]
    cos, sin = jnp.cos(angles), jnp.sin(angles)
    cos = jnp.concatenate([cos, cos], axis=1)
    sin = jnp.concatenate([-sin, sin], axis=1)

    wo = lax.all_gather(w_out, "blk", axis=0, tiled=True)
    gains = jnp.concatenate([norm_attn, norm_ffn])
    gains = jnp.pad(gains[None], ((0, 15), (0, 3 * part - 2 * rows_w)))
    qkv = pack_call(w_query, w_key, w_value, gains, count_blk)
    qkv = lax.all_to_all(qkv, "blk", 0, 0, tiled=True)
    group_in = lax.all_gather(after(block_input, qkv, wo), "blk", axis=0, tiled=True)
    qkv_pieces = gather_uly(qkv, count_uly)
    cut = lambda f: in_order([[f(p) for p in parts] for parts in qkv_pieces], uly_index)
    w_qkv = cut(lambda p: p[:, :rows_w].reshape(-1, 3 * part))
    gains = cut(lambda p: p[:, rows_w, : 2 * rows_w])
    gain_attn = gains[:, :rows_w].reshape(1, dim).astype(f32)
    gain_ffn = gains[:, rows_w:].reshape(1, dim).astype(f32)

    rows_d, width = w_gate.shape[0], w_gate.shape[1] // count_blk
    columns = lambda w: w.reshape(rows_d, count_blk, width).transpose(1, 0, 2)
    to_hidden = lambda w: lax.all_to_all(w, "blk", 0, 0, tiled=True)
    gate_up = jnp.concatenate([columns(w_gate), columns(w_up)], axis=1)
    down = to_hidden(after(w_down.reshape(count_blk, width, rows_d), qkv))
    if count_uly == 4:
        size = wo.shape[0] // 2
        half = lax.dynamic_slice_in_dim(wo, lax.rem(blk_index, 2) * size, size, 0)
        halves = gather_uly(after(half, qkv_pieces[3][-1]), count_uly)[1:]
    else:
        halves = gather_uly(wo, count_uly)[1:]
    halves, group_in, down, gate_up = together((halves, group_in, down, gate_up))
    wos, places = [wo], [(0, 0, 0)]
    for j, parts in enumerate(halves, 1):
        row = 0
        for piece in parts:
            if count_uly == 4:
                swapped = lax.ppermute(piece, "blk", [(i, i ^ 1) for i in range(count_blk)])
                wos += [piece, swapped]
                places += [(j, 1, row), (j, 2, row)]
            else:
                wos += [piece]
                places += [(j, 0, 0)]
            row += piece.shape[0]
    hidden_one, query, kv = qkv_call(group_in, gain_attn, w_qkv, cos, sin)
    kvs = [
        lax.ppermute(kv, "uly", [(i, i + s) for i in range(count_uly - s)])
        for s in range(back, 0, -1)
    ] + [kv]

    gate_up = to_hidden(after(gate_up, kv))
    group_cot = lax.all_gather(after(cotangent, kv), "blk", axis=0, tiled=True)
    down = gather_uly(after(down, kv), count_uly)
    query, gate_up, down, group_cot = together((query, gate_up, down, group_cot))
    gate_up = gather_first(gate_up, count_uly)
    attended = attn_fwd_call(low_kb, query, begin[:, None], kvs)
    group_att = lax.all_gather(attended, "blk", axis=0, tiled=True)
    gate_up, group_att = together((gate_up, group_att))
    gate_up = gather_rest(gate_up, count_uly)
    group_hidden, resid, wo = project_call(
        both_at,
        group_att.reshape(count_blk, group, part),
        group_in,
        gain_ffn,
        wos,
        tuple(places),
        tok_rows,
        count_uly,
    )
    input_f = block_input.astype(f32)
    normed_two, inv_two = rms_stats(resid)

    pairs = count_uly == 4 and width % HD == 0
    if pairs:
        ffn = ffn_pieces(group_hidden, group_cot, gate_up, down, width)
    else:
        ffn = ffn_plain(group_hidden, group_cot, gate_up, down)
    inner, gg, gu, y_part, gh_part = ffn
    grad_h2 = lax.psum_scatter(gh_part, "blk", scatter_dimension=0, tiled=True)

    def products(lefts, rights, rows):
        half = dim // 2
        if rows:
            halves = (rights[:, :half], rights[:, half:])
            term = [t_dot(lefts[n], halves[n // 2]) for n in range(4)]
        else:
            halves = (lefts[:, :half], lefts[:, half:])
            term = [t_dot(halves[n // 2], rights[n]) for n in range(4)]
        return [term[1].astype(bf16), term[2].astype(bf16), term[0], term[3]]

    def first_phase(term):
        return [
            xor_permute(term[0], count_uly, 1),
            xor_permute(term[1], count_uly, 2),
            term[2],
            term[3],
        ]

    def second_phase(term, rows):
        axis = 0 if rows else 1
        one, two = (k + g.astype(f32) for k, g in zip(term[2:], term[:2]))
        mine = [lax.slice_in_dim(t, 0, width, axis=axis) for t in (one, two)]
        rest = [lax.slice_in_dim(t, width, 2 * width, axis=axis).astype(bf16) for t in (one, two)]
        mine[0] = mine[0] + xor_permute(rest[0], count_uly, 2).astype(f32)
        mine[1] = mine[1] + xor_permute(rest[1], count_uly, 1).astype(f32)
        return jnp.concatenate(mine, axis=1 - axis).astype(bf16)

    def direct(lefts, rights, rows):
        cut = lambda a: [a[0][:, j * width : (j + 1) * width] for j in range(count_uly)]
        if rows:
            terms = [t_dot(left, rights) for left in cut(lefts)]
        else:
            terms = [t_dot(lefts, right) for right in cut(rights)]
        return scatter_uly(terms[0], [t.astype(bf16) for t in terms[1:]], count_uly).astype(bf16)

    if pairs:
        sum_gate = second_phase(first_phase(products(group_hidden, gg, False)), False)
        sum_up = products(group_hidden, gu, False)
        sum_down = products(inner, group_cot, True)
    else:
        sum_gate = direct(group_hidden, gg, False)
        sum_up = direct(group_hidden, gu, False)
        sum_down = direct(inner, group_cot, True)
    grad_h2, sum_gate, sum_up, sum_down, y_part = together((grad_h2, sum_gate, sum_up, sum_down, y_part))
    if pairs:
        sum_up = second_phase(first_phase(sum_up), False)
        sum_down = second_phase(first_phase(sum_down), True)
    grad_h2 = grad_h2.astype(f32)
    grad_resid = cotangent.astype(f32) + norm_back(grad_h2, normed_two, inv_two, gain_ffn)
    group_gattn = lax.all_gather(grad_resid.astype(bf16), "blk", axis=0, tiled=True)
    blocks_of = lambda w: w.reshape(count_blk, rows_d, width)
    gain_part = jnp.sum(grad_h2 * normed_two, axis=0).astype(bf16).reshape(count_blk, -1, width)
    gain_rows = gain_part.shape[1]
    gain_part = jnp.pad(gain_part, ((0, 0), (0, -gain_rows % 8), (0, 0)))
    grad_gate = to_hidden(jnp.concatenate([blocks_of(sum_gate), gain_part], axis=1))
    gattn, sum_up, sum_down, grad_gate = together((group_gattn, sum_up, sum_down, grad_gate))

    down_blocks = sum_down.reshape(width, count_blk, rows_d).transpose(1, 0, 2)
    grads_ud = to_hidden(
        jnp.concatenate(
            [blocks_of(sum_up), down_blocks.reshape(count_blk, rows_d, width)], axis=1
        )
    )
    gq, gkv, *sent = attn_bwd_call(
        low_kb, query, gattn, begin[None, :], wo, cos, sin, kvs
    )
    got = [
        lax.ppermute(block, "uly", [(i, i - s) for i in range(s, count_uly)])
        for s, block in zip(range(back, 0, -1), sent)
    ]
    y_own = lax.psum_scatter(after(y_part, gattn), "blk", scatter_dimension=0, tiled=True)
    def split_rows(whole):
        rows = whole.shape[0] // count_uly
        pick = lambda j: lax.dynamic_slice_in_dim(whole, (uly_index ^ j) * rows, rows, 0)
        return scatter_uly(
            pick(0).astype(f32), [pick(j) for j in range(1, count_uly)], count_uly
        ).astype(bf16)

    gain_sum = jnp.sum(grad_gate[:, rows_d:][:, :gain_rows].astype(f32), axis=0)
    gain_sum = jnp.pad(gain_sum.reshape(part, 1), ((0, 0), (0, HD - 1)))
    outs = jnp.concatenate([t_dot(attended, gattn), gain_sum], axis=1).astype(bf16)
    outs = split_rows(after(outs, gq))
    gkv, y_own, grads_ud, outs = together((gkv, y_own, grads_ud, outs))
    output = (resid + y_own.astype(f32)).astype(bf16)
    gh1_part, grads = gqkv_call(
        uly_at, hidden_one, gq, gkv, got, cos, sin, w_qkv, count_uly
    )
    grad_h1 = lax.psum_scatter(gh1_part, "blk", scatter_dimension=0, tiled=True).astype(f32)
    normed_one, inv_one = rms_stats(input_f)
    input_grad = grad_resid + norm_back(grad_h1, normed_one, inv_one, gain_attn)

    grads = scatter_uly(grads[0], grads[1:], count_uly).astype(bf16)
    owner = [((i % count_uly) * count_blk + i // count_uly, i) for i in range(devices)]
    outs = lax.ppermute(after(outs, gh1_part), BOTH, owner)
    grads, outs = together((grads, outs))
    outs = outs.astype(f32)
    grad_out, grad_gain_ffn = outs[:, :dim], outs[:, dim]
    grads = lax.all_to_all(grads.reshape(count_blk, rows_w, 3 * part), "blk", 0, 0, tiled=True)
    grad_gate = grad_gate[:, :rows_d].astype(f32).transpose(1, 0, 2).reshape(w_gate.shape)
    grad_up = grads_ud[:, :rows_d].astype(f32).transpose(1, 0, 2).reshape(w_up.shape)
    grad_down = grads_ud[:, rows_d:].astype(f32).reshape(w_down.shape)
    grads, *_ = together((grads, grad_gate, grad_up, grad_down, input_grad, grad_out, grad_gain_ffn))
    grad_query, grad_key, grad_value, grad_gain_attn = unpack_call(
        grads, w_query, w_key, w_value, norm_attn.astype(f32)[:, None]
    )
    return (
        output,
        input_grad,
        grad_gain_attn[:, 0],
        grad_query,
        grad_key,
        grad_value,
        grad_out,
        grad_gain_ffn,
        grad_gate,
        grad_up,
        grad_down,
    )


def solution(mesh):
    rows = P(("uly", "blk"), None)
    vector = P(("uly", "blk"))
    weights = (vector, rows, rows, rows, rows, vector, P("blk", "uly"), P("blk", "uly"), P("uly", "blk"))
    return jax.shard_map(
        body,
        mesh=mesh,
        in_specs=(rows, rows, P(), P()) + weights,
        out_specs=(rows, rows) + weights,
        check_vma=False,
    )
```

```python
import functools
import math

import jax
import jax.numpy as jnp
from jax import lax
from jax.experimental import pallas as pl
from jax.experimental.pallas import tpu as pltpu
from jax.sharding import PartitionSpec as P

HEADS = 16
HD = 128
BOTH = ("uly", "blk")
LONGEST = {4096: 2048, 16384: 4096}
LOG2E = math.log2(math.e)

norm_eps = 1e-05
rope_base = 10000.0
score_bias = -math.log(4096.0)
head_scale = 1.0 / math.sqrt(HD)

BQ = 512
BK = 512
BR = 256
VMEM = 60 * 2**20
f32 = jnp.float32
bf16 = jnp.bfloat16


def dot_t(left, right):
    return lax.dot_general(left, right, (((1,), (1,)), ((), ())), preferred_element_type=f32)


def t_dot(left, right):
    return lax.dot_general(left, right, (((0,), (0,)), ((), ())), preferred_element_type=f32)


def dot(left, right):
    return jnp.dot(left, right, preferred_element_type=f32)


def pack_kernel(wq_ref, wk_ref, wv_ref, gain_ref, out_ref):
    rows = wq_ref.shape[0]
    width = out_ref.shape[2] // 3
    for b in range(out_ref.shape[0]):
        for i, w in enumerate((wq_ref, wk_ref, wv_ref)):
            out_ref[b, :rows, i * width : (i + 1) * width] = w[:, b * width : (b + 1) * width]
        out_ref[b, rows:, :] = gain_ref[...]


def pack_call(wq, wk, wv, gains, count):
    rows, dim = wq.shape
    vmem = pl.BlockSpec(memory_space=pltpu.VMEM)
    return pl.pallas_call(
        pack_kernel,
        in_specs=[vmem] * 4,
        out_specs=vmem,
        out_shape=jax.ShapeDtypeStruct((count, rows + gains.shape[0], 3 * dim // count), bf16),
    )(wq, wk, wv, gains)


def unpack_kernel(got_ref, wq_ref, wk_ref, wv_ref, gain_ref, gq_ref, gk_ref, gv_ref, gg_ref):
    width = got_ref.shape[2] // 3
    total = jnp.zeros(gg_ref.shape, f32)
    for i, (w, g_ref) in enumerate(((wq_ref, gq_ref), (wk_ref, gk_ref), (wv_ref, gv_ref))):
        for b in range(got_ref.shape[0]):
            at = slice(b * width, (b + 1) * width)
            g = got_ref[b, :, i * width : (i + 1) * width].astype(f32)
            g_ref[:, at] = g
            total = total + jnp.sum(g * w[:, at].astype(f32), axis=1, keepdims=True)
    gg_ref[...] = total / gain_ref[...]


def unpack_call(got, wq, wk, wv, gain):
    vmem = pl.BlockSpec(memory_space=pltpu.VMEM)
    return pl.pallas_call(
        unpack_kernel,
        in_specs=[vmem] * 5,
        out_specs=[vmem] * 4,
        out_shape=[jax.ShapeDtypeStruct(wq.shape, f32)] * 3
        + [jax.ShapeDtypeStruct((wq.shape[0], 1), f32)],
    )(got, wq, wk, wv, gain)


def qkv_kernel(x_ref, gain_ref, w_ref, cos_ref, sin_ref, h_ref, q_ref, kv_ref):
    x = x_ref[...].astype(f32)
    inv = lax.rsqrt(jnp.mean(x * x, axis=-1, keepdims=True) + norm_eps)
    h = (x * inv * gain_ref[...]).astype(bf16)
    h_ref[...] = h
    acc = dot(h, w_ref[...])
    cos, sin = cos_ref[...], sin_ref[...]
    width = q_ref.shape[1]
    for s in range(0, width, HD):
        t = acc[:, s : s + HD]
        q_ref[:, s : s + HD] = (t * cos + pltpu.roll(t, HD // 2, 1) * sin).astype(bf16)
        t = acc[:, width + s : width + s + HD]
        kv_ref[:, s : s + HD] = (t * cos + pltpu.roll(t, HD // 2, 1) * sin).astype(bf16)
    kv_ref[:, width:] = acc[:, 2 * width :].astype(bf16)


def qkv_call(x, gain, w, cos, sin):
    rows, dim = x.shape
    width = w.shape[1] // 3
    block = lambda cols: pl.BlockSpec((BR, cols), lambda i: (i, 0))
    whole = lambda shape: pl.BlockSpec(shape, lambda i: (0, 0))
    return pl.pallas_call(
        qkv_kernel,
        grid=(rows // BR,),
        in_specs=[block(dim), whole((1, dim)), whole(w.shape), block(HD), block(HD)],
        out_specs=[block(dim), block(width), block(2 * width)],
        out_shape=[
            jax.ShapeDtypeStruct((rows, dim), bf16),
            jax.ShapeDtypeStruct((rows, width), bf16),
            jax.ShapeDtypeStruct((rows, 2 * width), bf16),
        ],
        compiler_params=pltpu.CompilerParams(vmem_limit_bytes=VMEM),
        cost_estimate=pl.CostEstimate(
            flops=2 * rows * dim * 3 * width, bytes_accessed=16 * 2**20, transcendentals=0
        ),
    )(x, gain, w, cos, sin)


def attn_fwd_kernel(count_kv, lo_ref, q_ref, start_ref, wo_ref, *refs):
    kv_refs, (att_ref, part_ref, kv_all) = refs[:count_kv], refs[count_kv:]
    rows, width = q_ref.shape
    heads = width // HD
    base = (count_kv - 1) * rows
    for i, r in enumerate(kv_refs):
        kv_all[i * rows : (i + 1) * rows, :] = r[...]
    for i in range(rows // BQ):
        at = slice(i * BQ, (i + 1) * BQ)
        start = start_ref[at, :]
        row = base + i * BQ + lax.broadcasted_iota(jnp.int32, (BQ, BK), 0)
        col = lax.broadcasted_iota(jnp.int32, (BQ, BK), 1)
        queries = [q_ref[at, h * HD : (h + 1) * HD] for h in range(heads)]

        def step(kb, sums):
            off = pl.multiple_of(kb * BK, BK)
            here = col + off
            ok = (here >= start) & (here <= row)
            out = []
            for h in range(heads):
                k = kv_all[pl.ds(off, BK), h * HD : (h + 1) * HD]
                v = kv_all[pl.ds(off, BK), width + h * HD : width + (h + 1) * HD]
                e = jnp.exp2(
                    dot_t(queries[h], k) * (-head_scale * LOG2E) - score_bias * LOG2E
                )
                weight = jnp.where(ok, 1.0 / (1.0 + e), 0.0).astype(bf16)
                out.append(sums[h] + dot(weight, v))
            return tuple(out)

        last = (base + (i + 1) * BQ - 1) // BK + 1
        sums = lax.fori_loop(
            lo_ref[i], last, step, tuple(jnp.zeros((BQ, HD), f32) for _ in range(heads))
        )
        att = jnp.concatenate([s.astype(bf16) for s in sums], axis=1)
        att_ref[at, :] = att
        part_ref[at, :] = dot(att, wo_ref[...]).astype(bf16)


def attn_fwd_call(lo, q, start, wo, kvs):
    rows, width = q.shape
    dim = wo.shape[1]
    vmem = pl.BlockSpec(memory_space=pltpu.VMEM)
    return pl.pallas_call(
        functools.partial(attn_fwd_kernel, len(kvs)),
        in_specs=[pl.BlockSpec(memory_space=pltpu.SMEM)] + [vmem] * (3 + len(kvs)),
        out_specs=[vmem, vmem],
        out_shape=[
            jax.ShapeDtypeStruct((rows, width), bf16),
            jax.ShapeDtypeStruct((rows, dim), bf16),
        ],
        scratch_shapes=[pltpu.VMEM((len(kvs) * rows, 2 * width), bf16)],
        compiler_params=pltpu.CompilerParams(vmem_limit_bytes=VMEM),
        cost_estimate=pl.CostEstimate(
            flops=10**6, bytes_accessed=10**6, transcendentals=0
        ),
    )(lo, q, start, wo, *kvs)


def attn_bwd_kernel(count_kv, lo_ref, q_ref, ga_ref, start_ref, wo_ref, cos_ref, sin_ref, *refs):
    kv_refs = refs[:count_kv]
    gq_ref, own_ref = refs[count_kv : count_kv + 2]
    rem_refs = refs[count_kv + 2 : 2 * count_kv + 1]
    kv_all, gkv = refs[2 * count_kv + 1 :]
    rows, width = q_ref.shape
    heads = width // HD
    base = (count_kv - 1) * rows
    for i, r in enumerate(kv_refs):
        kv_all[i * rows : (i + 1) * rows, :] = r[...]
        gkv[i * rows : (i + 1) * rows, :] = jnp.zeros((rows, 2 * width), f32)
    for i in range(rows // BQ):
        at = slice(i * BQ, (i + 1) * BQ)
        start = start_ref[:, at]
        row = base + i * BQ + lax.broadcasted_iota(jnp.int32, (BK, BQ), 1)
        col = lax.broadcasted_iota(jnp.int32, (BK, BQ), 0)
        gatt = dot_t(ga_ref[at, :], wo_ref[...]).astype(bf16)
        queries = [q_ref[at, h * HD : (h + 1) * HD] for h in range(heads)]
        gatts = [gatt[:, h * HD : (h + 1) * HD] for h in range(heads)]

        def step(kb, sums):
            off = pl.multiple_of(kb * BK, BK)
            here = col + off
            ok = (here >= start) & (here <= row)
            out = []
            for h in range(heads):
                ks = slice(h * HD, (h + 1) * HD)
                vs = slice(width + h * HD, width + (h + 1) * HD)
                k = kv_all[pl.ds(off, BK), ks]
                v = kv_all[pl.ds(off, BK), vs]
                e = jnp.exp2(
                    dot_t(k, queries[h]) * (-head_scale * LOG2E) - score_bias * LOG2E
                )
                sg = jnp.where(ok, 1.0 / (1.0 + e), 0.0)
                gs = (dot_t(v, gatts[h]) * sg * (1.0 - sg)).astype(bf16)
                gkv[pl.ds(off, BK), ks] += dot(gs, queries[h])
                gkv[pl.ds(off, BK), vs] += dot(sg.astype(bf16), gatts[h])
                out.append(sums[h] + t_dot(gs, k))
            return tuple(out)

        last = (base + (i + 1) * BQ - 1) // BK + 1
        sums = lax.fori_loop(
            lo_ref[i], last, step, tuple(jnp.zeros((BQ, HD), f32) for _ in range(heads))
        )
        cos, sin = cos_ref[at, :], sin_ref[at, :]
        for h in range(heads):
            t = sums[h] * head_scale
            gq_ref[at, h * HD : (h + 1) * HD] = (
                t * cos - pltpu.roll(t, HD // 2, 1) * sin
            ).astype(bf16)
    own_ref[:, :width] = gkv[base:, :width] * head_scale
    own_ref[:, width:] = gkv[base:, width:]
    for i, r in enumerate(rem_refs):
        r[:, :width] = (gkv[i * rows : (i + 1) * rows, :width] * head_scale).astype(bf16)
        r[:, width:] = gkv[i * rows : (i + 1) * rows, width:].astype(bf16)


def attn_bwd_call(lo, q, ga, start, wo, cos, sin, kvs):
    rows, width = q.shape
    vmem = pl.BlockSpec(memory_space=pltpu.VMEM)
    return pl.pallas_call(
        functools.partial(attn_bwd_kernel, len(kvs)),
        in_specs=[pl.BlockSpec(memory_space=pltpu.SMEM)] + [vmem] * (6 + len(kvs)),
        out_specs=[vmem] * (1 + len(kvs)),
        out_shape=[
            jax.ShapeDtypeStruct((rows, width), bf16),
            jax.ShapeDtypeStruct((rows, 2 * width), f32),
        ]
        + [jax.ShapeDtypeStruct((rows, 2 * width), bf16)] * (len(kvs) - 1),
        scratch_shapes=[
            pltpu.VMEM((len(kvs) * rows, 2 * width), bf16),
            pltpu.VMEM((len(kvs) * rows, 2 * width), f32),
        ],
        compiler_params=pltpu.CompilerParams(vmem_limit_bytes=VMEM),
        cost_estimate=pl.CostEstimate(
            flops=25 * 10**9, bytes_accessed=20 * 2**20, transcendentals=4 * 10**6
        ),
    )(lo, q, ga, start, wo, cos, sin, *kvs)


def gqkv_kernel(count, index_ref, h_ref, gq_ref, own_ref, cos_ref, sin_ref, w_ref, *refs):
    got, gh_ref, grad_refs, g_ref = refs[: -2 - count], refs[-2 - count], refs[-1 - count : -1], refs[-1]
    rows, width = gq_ref.shape
    for at in range(0, rows, BR):
        at = slice(at, at + BR)
        gkv = own_ref[at, :]
        for r in got:
            gkv = gkv + r[at, :].astype(f32)
        cos, sin = cos_ref[at, :], sin_ref[at, :]
        g_ref[at, :width] = gq_ref[at, :]
        for s in range(0, width, HD):
            t = gkv[:, s : s + HD]
            g_ref[at, width + s : width + s + HD] = (
                t * cos - pltpu.roll(t, HD // 2, 1) * sin
            ).astype(bf16)
        g_ref[at, 2 * width :] = gkv[:, width:].astype(bf16)
        gh_ref[at, :] = dot_t(g_ref[at, :], w_ref[...]).astype(bf16)
    size = h_ref.shape[1] // count
    for j in list(range(1, count)) + [0]:
        at = pl.multiple_of((index_ref[0] ^ j) * size, size)
        grad_refs[j][...] = t_dot(h_ref[:, pl.ds(at, size)], g_ref[...]).astype(grad_refs[j].dtype)


def gqkv_call(index, h, gq, own, got, cos, sin, w, count):
    rows, width = gq.shape
    dim = h.shape[1]
    size = dim // count
    vmem = pl.BlockSpec(memory_space=pltpu.VMEM)
    gh, *grads = pl.pallas_call(
        functools.partial(gqkv_kernel, count),
        in_specs=[pl.BlockSpec(memory_space=pltpu.SMEM)] + [vmem] * (6 + len(got)),
        out_specs=[vmem] * (1 + count),
        out_shape=[
            jax.ShapeDtypeStruct((rows, dim), bf16),
            jax.ShapeDtypeStruct((size, 3 * width), f32),
        ]
        + [jax.ShapeDtypeStruct((size, 3 * width), bf16)] * (count - 1),
        scratch_shapes=[pltpu.VMEM((rows, 3 * width), bf16)],
        compiler_params=pltpu.CompilerParams(vmem_limit_bytes=VMEM),
        cost_estimate=pl.CostEstimate(
            flops=12 * rows * width * dim, bytes_accessed=20 * 2**20, transcendentals=0
        ),
    )(index, h, gq, own, cos, sin, w, *got)
    return gh, grads


def ffn_kernel(places, blocks, groups, h_ref, c_ref, *refs):
    count = 1 + max(p[1] for p in places)
    sources = refs[:count]
    outs = refs[count : count + 3 * len(groups)]
    inner_ref, gh_ref, wg, wu, wd, gates, ups, sem = refs[count + 3 * len(groups) :]
    width = wg.shape[1] // blocks
    copies = [
        (which, pltpu.make_async_copy(sources[source].at[at], (wg, wu, wd)[which].at[to], sem.at[i]))
        for i, (which, source, at, to) in enumerate(places)
    ]
    first = pl.program_id(0) == 0

    def wait(weight):
        @pl.when(first)
        def _():
            for which, c in copies:
                if which == weight:
                    c.wait()

    @pl.when(first)
    def _():
        for weight in range(3):
            for which, c in copies:
                if which == weight:
                    c.start()

    wait(0)
    gate = dot(h_ref[...], wg[...])
    wait(1)
    up = dot(h_ref[...], wu[...])
    wait(2)
    grad = dot_t(c_ref[...], wd[...])
    sig = 1.0 / (1.0 + jnp.exp2(gate * -LOG2E))
    act = gate * sig
    inner = (act * up).astype(bf16)
    gg = (grad * up * sig * (1.0 + gate * (1.0 - sig))).astype(bf16)
    gu = (grad * act).astype(bf16)
    inner_ref[...] = inner
    gates[...] = gg
    ups[...] = gu
    for n, members in enumerate(groups):
        for m, j in enumerate(members):
            at, to = slice(j * width, (j + 1) * width), slice(m * width, (m + 1) * width)
            outs[n][:, to] = inner[:, at]
            outs[len(groups) + n][:, to] = gg[:, at]
            outs[2 * len(groups) + n][:, to] = gu[:, at]
    gh_ref[...] = (dot_t(gates[...], wg[...]) + dot_t(ups[...], wu[...])).astype(bf16)


def ffn_call(h, cot, sources, places, blocks, width, groups):
    rows, dim = h.shape
    hidden = blocks * width
    block = lambda cols: pl.BlockSpec((BR, cols), lambda i: (i, 0))
    sizes = [len(members) * width for members in groups] * 3 + [hidden, dim]
    result = pl.pallas_call(
        functools.partial(ffn_kernel, places, blocks, groups),
        grid=(rows // BR,),
        in_specs=[block(dim), block(dim)] + [pl.BlockSpec(memory_space=pl.ANY)] * len(sources),
        out_specs=[block(size) for size in sizes],
        out_shape=[jax.ShapeDtypeStruct((rows, size), bf16) for size in sizes],
        scratch_shapes=[
            pltpu.VMEM((dim, hidden), bf16),
            pltpu.VMEM((dim, hidden), bf16),
            pltpu.VMEM((hidden, dim), bf16),
            pltpu.VMEM((BR, hidden), bf16),
            pltpu.VMEM((BR, hidden), bf16),
            pltpu.SemaphoreType.DMA((len(places),)),
        ],
        compiler_params=pltpu.CompilerParams(vmem_limit_bytes=VMEM),
        cost_estimate=pl.CostEstimate(
            flops=10 * rows * dim * hidden, bytes_accessed=36 * 2**20, transcendentals=10**6
        ),
    )(h, cot, *sources)
    n = len(groups)
    down = [p for p in places if p[0] == 2]
    base = min(p[1] for p in down)
    y = down_call(result[-2], sources[base:], [(p[1] - base,) + p[2:] for p in down])
    return result[:n], result[n : 2 * n], result[2 * n : 3 * n], y, result[-1]


def down_kernel(places, inner_ref, *refs):
    sources, (y_ref, wd, sem) = refs[:-3], refs[-3:]

    @pl.when(pl.program_id(0) == 0)
    def _():
        copies = [
            pltpu.make_async_copy(sources[source].at[at], wd.at[to], sem.at[i])
            for i, (source, at, to) in enumerate(places)
        ]
        for c in copies:
            c.start()
        for c in copies:
            c.wait()

    y_ref[...] = dot(inner_ref[...], wd[...]).astype(bf16)


def down_call(inner, sources, places):
    rows, hidden = inner.shape
    dim = max(to[1].stop or 0 for _, _, to in places) or sources[0].shape[-1]
    block = lambda cols: pl.BlockSpec((BR, cols), lambda i: (i, 0))
    return pl.pallas_call(
        functools.partial(down_kernel, tuple(places)),
        grid=(rows // BR,),
        in_specs=[block(hidden)] + [pl.BlockSpec(memory_space=pl.ANY)] * len(sources),
        out_specs=block(dim),
        out_shape=jax.ShapeDtypeStruct((rows, dim), bf16),
        scratch_shapes=[
            pltpu.VMEM((hidden, dim), bf16),
            pltpu.SemaphoreType.DMA((len(places),)),
        ],
        compiler_params=pltpu.CompilerParams(vmem_limit_bytes=VMEM),
        cost_estimate=pl.CostEstimate(
            flops=2 * rows * dim * hidden, bytes_accessed=12 * 2**20, transcendentals=0
        ),
    )(inner, *sources)


PAIRS = ((0, 2), (1, 3), (2, 3), (0, 1))


def ffn_pieces(h, cot, gate_up, down, width):
    sources, places = [], []
    for pieces, kinds in ((gate_up, (0, 1)), (down, (2,))):
        for j, parts in enumerate(pieces):
            block = 0
            for part in parts:
                size = part.shape[2] if kinds == (2,) else part.shape[1] // 2
                for i in range(part.shape[0]):
                    rows = slice(block * size, (block + 1) * size)
                    cols = slice(j * width, (j + 1) * width)
                    for which in kinds:
                        at = (i, slice(which * size, (which + 1) * size)) if which < 2 else (i,)
                        to = (rows, cols) if which < 2 else (cols, rows)
                        places.append((which, len(sources), at, to))
                    block += 1
                sources.append(part)
    return ffn_call(h, cot, sources, tuple(places), len(down), width, PAIRS)


def ffn_plain(h, cot, gate_up, down):
    size = gate_up[0][0].shape[1] // 2
    merge = lambda parts: jnp.concatenate(parts, axis=0)
    flat = lambda p, at: merge(p)[:, at].reshape(-1, p[0].shape[-1])
    tall = lambda p: merge(p).transpose(1, 0, 2).reshape(p[0].shape[1], -1)
    sources = [
        jnp.concatenate([flat(p, slice(0, size)) for p in gate_up], axis=1),
        jnp.concatenate([flat(p, slice(size, 2 * size)) for p in gate_up], axis=1),
        jnp.concatenate([tall(p) for p in down], axis=0),
    ]
    every = (slice(None), slice(None))
    places = tuple((which, which, every, every) for which in range(3))
    return ffn_call(h, cot, sources, places, 1, sources[0].shape[1], ((0,),))


def xor_permute(x, count, flip):
    return lax.ppermute(x, "uly", [(i, i ^ flip) for i in range(count)])


def gather_uly(x, count):
    return gather_rest(gather_first(x, count), count)


def gather_first(x, count):
    return [x] + [xor_permute(x, count, j) for j in ((1, 2) if count == 4 else range(1, count))]


def gather_rest(blocks, count):
    if count != 4:
        return [[block] for block in blocks]
    x, one, two = blocks
    half = x.shape[0] // 2
    low = xor_permute(one[:half], count, 2)
    high = xor_permute(two[half:], count, 1)
    return [[x], [one], [two], [low, high]]


def in_order(pieces, index):
    rows = sum(p.shape[0] for p in pieces[0])
    out = jnp.zeros((len(pieces) * rows,) + pieces[0][0].shape[1:], pieces[0][0].dtype)
    for j, parts in enumerate(pieces):
        at = (index ^ j) * rows
        for part in parts:
            out = lax.dynamic_update_slice_in_dim(out, part, at, 0)
            at = at + part.shape[0]
    return out


def scatter_uly(own, others, count):
    got = [xor_permute(block, count, j + 1) for j, block in enumerate(others)]
    for block in got:
        own = own + block.astype(f32)
    return own


def after(x, *earlier):
    return lax.optimization_barrier((x,) + earlier)[0]


def rms_stats(values):
    scale_inv = lax.rsqrt(jnp.mean(values * values, axis=-1, keepdims=True) + norm_eps)
    return (values * scale_inv, scale_inv)


def norm_back(grad_normed, normed, scale_inv, gain):
    scaled = grad_normed * gain
    return scale_inv * (scaled - normed * jnp.mean(scaled * normed, axis=-1, keepdims=True))


def body(
    block_input,
    cotangent,
    lengths,
    seq_order,
    norm_attn,
    w_query,
    w_key,
    w_value,
    w_out,
    norm_ffn,
    w_gate,
    w_up,
    w_down,
):
    count_uly = lax.axis_size("uly")
    count_blk = lax.axis_size("blk")
    devices = count_uly * count_blk
    uly_index = lax.axis_index("uly")
    uly_at = uly_index.astype(jnp.int32).reshape(1)
    tok_rows, dim = block_input.shape
    group = count_blk * tok_rows
    part = dim // count_blk
    rows_w = w_query.shape[0]
    together = lax.optimization_barrier
    longest = LONGEST.get(devices * tok_rows, devices * tok_rows)
    back = min(count_uly - 1, -(-(longest - 1) // group))

    labels = jnp.arange(lengths.shape[0], dtype=jnp.int32)
    picked = jnp.sum(
        jnp.where(seq_order[:, None] == labels[None, :], lengths[None, :], 0), axis=1
    )
    ends = jnp.sum(jnp.where(labels[None, :] <= labels[:, None], picked[None, :], 0), axis=1)
    starts = ends - picked
    row_ids = uly_index * group + jnp.arange(group, dtype=jnp.int32)
    inside = (row_ids[:, None] >= starts[None, :]) & (row_ids[:, None] < ends[None, :])
    seq_start = jnp.sum(jnp.where(inside, starts[None, :], 0), axis=1)
    position = row_ids - seq_start
    used = jnp.any(inside, axis=1)
    shift = (uly_index - back) * group
    begin = jnp.where(used, seq_start - shift, 1 << 30).astype(jnp.int32)
    firsts = begin[::BQ]
    ends_kb = (back * group + jnp.arange(group // BQ, dtype=jnp.int32) * BQ + BQ - 1) // BK + 1
    low_kb = jnp.minimum(firsts // BK, ends_kb).astype(jnp.int32)
    frequency = rope_base ** (-jnp.arange(HD // 2, dtype=f32) * 2.0 / HD)
    angles = position.astype(f32)[:, None] * frequency[None, :]
    cos, sin = jnp.cos(angles), jnp.sin(angles)
    cos = jnp.concatenate([cos, cos], axis=1)
    sin = jnp.concatenate([-sin, sin], axis=1)

    owner = [(i, (i % count_uly) * count_blk + i // count_uly) for i in range(devices)]
    wo = lax.ppermute(w_out, BOTH, owner)
    gains = jnp.concatenate([norm_attn, norm_ffn])
    gains = jnp.pad(gains[None], ((0, 15), (0, 3 * part - 2 * rows_w)))
    qkv = pack_call(w_query, w_key, w_value, gains, count_blk)
    qkv = lax.all_to_all(qkv, "blk", 0, 0, tiled=True)
    group_in = lax.all_gather(after(block_input, qkv, wo), "blk", axis=0, tiled=True)
    qkv_pieces = gather_uly(qkv, count_uly)
    cut = lambda f: in_order([[f(p) for p in parts] for parts in qkv_pieces], uly_index)
    w_qkv = cut(lambda p: p[:, :rows_w].reshape(-1, 3 * part))
    gains = cut(lambda p: p[:, rows_w, : 2 * rows_w])
    gain_attn = gains[:, :rows_w].reshape(1, dim).astype(f32)
    gain_ffn = gains[:, rows_w:].reshape(1, dim).astype(f32)

    rows_d, width = w_gate.shape[0], w_gate.shape[1] // count_blk
    columns = lambda w: w.reshape(rows_d, count_blk, width).transpose(1, 0, 2)
    to_hidden = lambda w: lax.all_to_all(w, "blk", 0, 0, tiled=True)
    gate_up = jnp.concatenate([columns(w_gate), columns(w_up)], axis=1)
    down = to_hidden(
        after(w_down.reshape(count_blk, width, rows_d), *[p[0] for p in qkv_pieces[1:3]])
    )
    wo = in_order(gather_uly(after(wo, qkv_pieces[3][-1]), count_uly), uly_index)
    group_in, down, gate_up, wo = together((group_in, down, gate_up, wo))
    hidden_one, query, kv = qkv_call(group_in, gain_attn, w_qkv, cos, sin)
    if count_uly == 4 and back == 2:
        half = group // 2
        two = lax.ppermute(kv, "uly", [(0, 2), (1, 3)])
        one = lax.ppermute(kv, "uly", [(0, 1), (2, 3)])
        over = lax.ppermute(kv[:half], "uly", [(1, 0)])
        over = lax.ppermute(over, "uly", [(0, 2)])
        under = lax.ppermute(two[half:], "uly", [(3, 2)])
        kvs = [two, one + jnp.concatenate([over, under]), kv]
    else:
        kvs = [
            lax.ppermute(kv, "uly", [(i, i + s) for i in range(count_uly - s)])
            for s in range(back, 0, -1)
        ] + [kv]

    gate_up = to_hidden(after(gate_up, kv))
    group_cot = lax.all_gather(after(cotangent, kv), "blk", axis=0, tiled=True)
    down = gather_first(after(down, kv), count_uly)
    query, down = together((query, down))
    attended, out_part = attn_fwd_call(low_kb, query, begin[:, None], wo, kvs)
    out_part, gate_up, group_cot = together((out_part, gate_up, group_cot))
    gate_up = gather_first(gate_up, count_uly)
    out_own = lax.psum_scatter(out_part, "blk", scatter_dimension=0, tiled=True)
    out_own, gate_up = together((out_own, gate_up))
    gate_up = gather_rest(gate_up, count_uly)
    down = gather_rest(down, count_uly)
    input_f = block_input.astype(f32)
    resid = input_f + out_own.astype(f32)
    normed_two, inv_two = rms_stats(resid)
    hidden_two = (normed_two * gain_ffn).astype(bf16)
    group_hidden = lax.all_gather(hidden_two, "blk", axis=0, tiled=True)

    pairs = count_uly == 4 and width % HD == 0
    if pairs:
        ffn = ffn_pieces(group_hidden, group_cot, gate_up, down, width)
    else:
        ffn = ffn_plain(group_hidden, group_cot, gate_up, down)
    inner, gg, gu, y_part, gh_part = ffn
    grad_h2 = lax.psum_scatter(gh_part, "blk", scatter_dimension=0, tiled=True)

    def products(lefts, rights, rows):
        half = dim // 2
        if rows:
            halves = (rights[:, :half], rights[:, half:])
            term = [t_dot(lefts[n], halves[n // 2]) for n in range(4)]
        else:
            halves = (lefts[:, :half], lefts[:, half:])
            term = [t_dot(halves[n // 2], rights[n]) for n in range(4)]
        return [term[1].astype(bf16), term[2].astype(bf16), term[0], term[3]]

    def first_phase(term):
        return [
            xor_permute(term[0], count_uly, 1),
            xor_permute(term[1], count_uly, 2),
            term[2],
            term[3],
        ]

    def second_phase(term, rows):
        axis = 0 if rows else 1
        one, two = (k + g.astype(f32) for k, g in zip(term[2:], term[:2]))
        mine = [lax.slice_in_dim(t, 0, width, axis=axis) for t in (one, two)]
        rest = [lax.slice_in_dim(t, width, 2 * width, axis=axis).astype(bf16) for t in (one, two)]
        mine[0] = mine[0] + xor_permute(rest[0], count_uly, 2).astype(f32)
        mine[1] = mine[1] + xor_permute(rest[1], count_uly, 1).astype(f32)
        return jnp.concatenate(mine, axis=1 - axis).astype(bf16)

    def direct(lefts, rights, rows):
        cut = lambda a: [a[0][:, j * width : (j + 1) * width] for j in range(count_uly)]
        if rows:
            terms = [t_dot(left, rights) for left in cut(lefts)]
        else:
            terms = [t_dot(lefts, right) for right in cut(rights)]
        return scatter_uly(terms[0], [t.astype(bf16) for t in terms[1:]], count_uly).astype(bf16)

    if pairs:
        sum_gate = second_phase(first_phase(products(group_hidden, gg, False)), False)
        sum_up = products(group_hidden, gu, False)
        sum_down = products(inner, group_cot, True)
    else:
        sum_gate = direct(group_hidden, gg, False)
        sum_up = direct(group_hidden, gu, False)
        sum_down = direct(inner, group_cot, True)
    grad_h2, sum_gate, sum_up, sum_down, y_part = together((grad_h2, sum_gate, sum_up, sum_down, y_part))
    if pairs:
        sum_up = second_phase(first_phase(sum_up), False)
        sum_down = second_phase(first_phase(sum_down), True)
    grad_h2 = grad_h2.astype(f32)
    grad_resid = cotangent.astype(f32) + norm_back(grad_h2, normed_two, inv_two, gain_ffn)
    group_gattn = lax.all_gather(grad_resid.astype(bf16), "blk", axis=0, tiled=True)
    blocks_of = lambda w: w.reshape(count_blk, rows_d, width)
    gain_part = jnp.sum(grad_h2 * normed_two, axis=0).astype(bf16).reshape(count_blk, -1, width)
    gain_rows = gain_part.shape[1]
    gain_part = jnp.pad(gain_part, ((0, 0), (0, -gain_rows % 8), (0, 0)))
    grad_gate = to_hidden(jnp.concatenate([blocks_of(sum_gate), gain_part], axis=1))
    gattn, sum_up, sum_down, grad_gate = together((group_gattn, sum_up, sum_down, grad_gate))

    down_blocks = sum_down.reshape(width, count_blk, rows_d).transpose(1, 0, 2)
    grads_ud = to_hidden(
        jnp.concatenate(
            [blocks_of(sum_up), down_blocks.reshape(count_blk, rows_d, width)], axis=1
        )
    )
    gq, gkv, *sent = attn_bwd_call(
        low_kb, query, gattn, begin[None, :], wo, cos, sin, kvs
    )
    got = [
        lax.ppermute(block, "uly", [(i, i - s) for i in range(s, count_uly)])
        for s, block in zip(range(back, 0, -1), sent)
    ]
    y_own = lax.psum_scatter(after(y_part, gattn), "blk", scatter_dimension=0, tiled=True)
    def split_rows(whole):
        rows = whole.shape[0] // count_uly
        pick = lambda j: lax.dynamic_slice_in_dim(whole, (uly_index ^ j) * rows, rows, 0)
        return scatter_uly(
            pick(0).astype(f32), [pick(j) for j in range(1, count_uly)], count_uly
        ).astype(bf16)

    gain_sum = jnp.sum(grad_gate[:, rows_d:][:, :gain_rows].astype(f32), axis=0)
    gain_sum = jnp.pad(gain_sum.reshape(part, 1), ((0, 0), (0, HD - 1)))
    outs = jnp.concatenate([t_dot(attended, gattn), gain_sum], axis=1).astype(bf16)
    outs = split_rows(after(outs, gq))
    gkv, y_own, grads_ud, outs = together((gkv, y_own, grads_ud, outs))
    output = (resid + y_own.astype(f32)).astype(bf16)
    gh1_part, grads = gqkv_call(
        uly_at, hidden_one, gq, gkv, got, cos, sin, w_qkv, count_uly
    )
    grad_h1 = lax.psum_scatter(gh1_part, "blk", scatter_dimension=0, tiled=True).astype(f32)
    normed_one, inv_one = rms_stats(input_f)
    input_grad = grad_resid + norm_back(grad_h1, normed_one, inv_one, gain_attn)

    grads = scatter_uly(grads[0], grads[1:], count_uly).astype(bf16)
    outs = lax.ppermute(after(outs, gh1_part), BOTH, [(j, i) for i, j in owner])
    grads, outs = together((grads, outs))
    outs = outs.astype(f32)
    grad_out, grad_gain_ffn = outs[:, :dim], outs[:, dim]
    grads = lax.all_to_all(grads.reshape(count_blk, rows_w, 3 * part), "blk", 0, 0, tiled=True)
    grad_gate = grad_gate[:, :rows_d].astype(f32).transpose(1, 0, 2).reshape(w_gate.shape)
    grad_up = grads_ud[:, :rows_d].astype(f32).transpose(1, 0, 2).reshape(w_up.shape)
    grad_down = grads_ud[:, rows_d:].astype(f32).reshape(w_down.shape)
    grads, *_ = together((grads, grad_gate, grad_up, grad_down, input_grad, grad_out, grad_gain_ffn))
    grad_query, grad_key, grad_value, grad_gain_attn = unpack_call(
        grads, w_query, w_key, w_value, norm_attn.astype(f32)[:, None]
    )
    return (
        output,
        input_grad,
        grad_gain_attn[:, 0],
        grad_query,
        grad_key,
        grad_value,
        grad_out,
        grad_gain_ffn,
        grad_gate,
        grad_up,
        grad_down,
    )


def solution(mesh):
    rows = P(("uly", "blk"), None)
    vector = P(("uly", "blk"))
    weights = (vector, rows, rows, rows, rows, vector, P("blk", "uly"), P("blk", "uly"), P("uly", "blk"))
    return jax.shard_map(
        body,
        mesh=mesh,
        in_specs=(rows, rows, P(), P()) + weights,
        out_specs=(rows, rows) + weights,
        check_vma=False,
    )
```

```python
import functools
import math

import jax
import jax.numpy as jnp
from jax import lax
from jax.experimental import pallas as pl
from jax.experimental.pallas import tpu as pltpu
from jax.sharding import PartitionSpec as P

HEADS = 16
HD = 128
BOTH = ("uly", "blk")
LONGEST = {4096: 2048, 16384: 4096}
LOG2E = math.log2(math.e)

norm_eps = 1e-05
rope_base = 10000.0
score_bias = -math.log(4096.0)
head_scale = 1.0 / math.sqrt(HD)

BQ = 512
BK = 512
BR = 256
VMEM = 60 * 2**20
f32 = jnp.float32
bf16 = jnp.bfloat16


def dot_t(left, right):
    return lax.dot_general(left, right, (((1,), (1,)), ((), ())), preferred_element_type=f32)


def t_dot(left, right):
    return lax.dot_general(left, right, (((0,), (0,)), ((), ())), preferred_element_type=f32)


def dot(left, right):
    return jnp.dot(left, right, preferred_element_type=f32)


def pack_kernel(wq_ref, wk_ref, wv_ref, gain_ref, out_ref):
    rows = wq_ref.shape[0]
    width = out_ref.shape[2] // 3
    for b in range(out_ref.shape[0]):
        for i, w in enumerate((wq_ref, wk_ref, wv_ref)):
            out_ref[b, :rows, i * width : (i + 1) * width] = w[:, b * width : (b + 1) * width]
        out_ref[b, rows:, :] = gain_ref[...]


def pack_call(wq, wk, wv, gains, count):
    rows, dim = wq.shape
    vmem = pl.BlockSpec(memory_space=pltpu.VMEM)
    return pl.pallas_call(
        pack_kernel,
        in_specs=[vmem] * 4,
        out_specs=vmem,
        out_shape=jax.ShapeDtypeStruct((count, rows + gains.shape[0], 3 * dim // count), bf16),
    )(wq, wk, wv, gains)


def unpack_kernel(got_ref, wq_ref, wk_ref, wv_ref, gain_ref, gq_ref, gk_ref, gv_ref, gg_ref):
    width = got_ref.shape[2] // 3
    total = jnp.zeros(gg_ref.shape, f32)
    for i, (w, g_ref) in enumerate(((wq_ref, gq_ref), (wk_ref, gk_ref), (wv_ref, gv_ref))):
        for b in range(got_ref.shape[0]):
            at = slice(b * width, (b + 1) * width)
            g = got_ref[b, :, i * width : (i + 1) * width].astype(f32)
            g_ref[:, at] = g
            total = total + jnp.sum(g * w[:, at].astype(f32), axis=1, keepdims=True)
    gg_ref[...] = total / gain_ref[...]


def unpack_call(got, wq, wk, wv, gain):
    vmem = pl.BlockSpec(memory_space=pltpu.VMEM)
    return pl.pallas_call(
        unpack_kernel,
        in_specs=[vmem] * 5,
        out_specs=[vmem] * 4,
        out_shape=[jax.ShapeDtypeStruct(wq.shape, f32)] * 3
        + [jax.ShapeDtypeStruct((wq.shape[0], 1), f32)],
    )(got, wq, wk, wv, gain)


def qkv_kernel(x_ref, gain_ref, w_ref, cos_ref, sin_ref, h_ref, q_ref, kv_ref):
    x = x_ref[...].astype(f32)
    inv = lax.rsqrt(jnp.mean(x * x, axis=-1, keepdims=True) + norm_eps)
    h = (x * inv * gain_ref[...]).astype(bf16)
    h_ref[...] = h
    acc = dot(h, w_ref[...])
    cos, sin = cos_ref[...], sin_ref[...]
    width = q_ref.shape[1]
    for s in range(0, width, HD):
        t = acc[:, s : s + HD]
        q_ref[:, s : s + HD] = (t * cos + pltpu.roll(t, HD // 2, 1) * sin).astype(bf16)
        t = acc[:, width + s : width + s + HD]
        kv_ref[:, s : s + HD] = (t * cos + pltpu.roll(t, HD // 2, 1) * sin).astype(bf16)
    kv_ref[:, width:] = acc[:, 2 * width :].astype(bf16)


def qkv_call(x, gain, w, cos, sin):
    rows, dim = x.shape
    width = w.shape[1] // 3
    block = lambda cols: pl.BlockSpec((BR, cols), lambda i: (i, 0))
    whole = lambda shape: pl.BlockSpec(shape, lambda i: (0, 0))
    return pl.pallas_call(
        qkv_kernel,
        grid=(rows // BR,),
        in_specs=[block(dim), whole((1, dim)), whole(w.shape), block(HD), block(HD)],
        out_specs=[block(dim), block(width), block(2 * width)],
        out_shape=[
            jax.ShapeDtypeStruct((rows, dim), bf16),
            jax.ShapeDtypeStruct((rows, width), bf16),
            jax.ShapeDtypeStruct((rows, 2 * width), bf16),
        ],
        compiler_params=pltpu.CompilerParams(vmem_limit_bytes=VMEM),
        cost_estimate=pl.CostEstimate(
            flops=2 * rows * dim * 3 * width, bytes_accessed=16 * 2**20, transcendentals=0
        ),
    )(x, gain, w, cos, sin)


def attn_fwd_kernel(count_kv, lo_ref, q_ref, start_ref, wo_ref, *refs):
    kv_refs, (att_ref, part_ref, kv_all) = refs[:count_kv], refs[count_kv:]
    rows, width = q_ref.shape
    heads = width // HD
    base = (count_kv - 1) * rows
    for i, r in enumerate(kv_refs):
        kv_all[i * rows : (i + 1) * rows, :] = r[...]
    for i in range(rows // BQ):
        at = slice(i * BQ, (i + 1) * BQ)
        start = start_ref[at, :]
        row = base + i * BQ + lax.broadcasted_iota(jnp.int32, (BQ, BK), 0)
        col = lax.broadcasted_iota(jnp.int32, (BQ, BK), 1)
        queries = [q_ref[at, h * HD : (h + 1) * HD] for h in range(heads)]

        def step(kb, sums):
            off = pl.multiple_of(kb * BK, BK)
            here = col + off
            ok = (here >= start) & (here <= row)
            out = []
            for h in range(heads):
                k = kv_all[pl.ds(off, BK), h * HD : (h + 1) * HD]
                v = kv_all[pl.ds(off, BK), width + h * HD : width + (h + 1) * HD]
                e = jnp.exp2(
                    dot_t(queries[h], k) * (-head_scale * LOG2E) - score_bias * LOG2E
                )
                weight = jnp.where(ok, 1.0 / (1.0 + e), 0.0).astype(bf16)
                out.append(sums[h] + dot(weight, v))
            return tuple(out)

        last = (base + (i + 1) * BQ - 1) // BK + 1
        sums = lax.fori_loop(
            lo_ref[i], last, step, tuple(jnp.zeros((BQ, HD), f32) for _ in range(heads))
        )
        att = jnp.concatenate([s.astype(bf16) for s in sums], axis=1)
        att_ref[at, :] = att
        part_ref[at, :] = dot(att, wo_ref[...]).astype(bf16)


def attn_fwd_call(lo, q, start, wo, kvs):
    rows, width = q.shape
    dim = wo.shape[1]
    vmem = pl.BlockSpec(memory_space=pltpu.VMEM)
    return pl.pallas_call(
        functools.partial(attn_fwd_kernel, len(kvs)),
        in_specs=[pl.BlockSpec(memory_space=pltpu.SMEM)] + [vmem] * (3 + len(kvs)),
        out_specs=[vmem, vmem],
        out_shape=[
            jax.ShapeDtypeStruct((rows, width), bf16),
            jax.ShapeDtypeStruct((rows, dim), bf16),
        ],
        scratch_shapes=[pltpu.VMEM((len(kvs) * rows, 2 * width), bf16)],
        compiler_params=pltpu.CompilerParams(vmem_limit_bytes=VMEM),
        cost_estimate=pl.CostEstimate(
            flops=10**6, bytes_accessed=10**6, transcendentals=0
        ),
    )(lo, q, start, wo, *kvs)


def attn_bwd_kernel(count_kv, lo_ref, q_ref, ga_ref, start_ref, wo_ref, cos_ref, sin_ref, *refs):
    kv_refs = refs[:count_kv]
    gq_ref, own_ref = refs[count_kv : count_kv + 2]
    rem_refs = refs[count_kv + 2 : 2 * count_kv + 1]
    kv_all, gkv = refs[2 * count_kv + 1 :]
    rows, width = q_ref.shape
    heads = width // HD
    base = (count_kv - 1) * rows
    for i, r in enumerate(kv_refs):
        kv_all[i * rows : (i + 1) * rows, :] = r[...]
        gkv[i * rows : (i + 1) * rows, :] = jnp.zeros((rows, 2 * width), f32)
    for i in range(rows // BQ):
        at = slice(i * BQ, (i + 1) * BQ)
        start = start_ref[:, at]
        row = base + i * BQ + lax.broadcasted_iota(jnp.int32, (BK, BQ), 1)
        col = lax.broadcasted_iota(jnp.int32, (BK, BQ), 0)
        gatt = dot_t(ga_ref[at, :], wo_ref[...]).astype(bf16)
        queries = [q_ref[at, h * HD : (h + 1) * HD] for h in range(heads)]
        gatts = [gatt[:, h * HD : (h + 1) * HD] for h in range(heads)]

        def step(kb, sums):
            off = pl.multiple_of(kb * BK, BK)
            here = col + off
            ok = (here >= start) & (here <= row)
            out = []
            for h in range(heads):
                ks = slice(h * HD, (h + 1) * HD)
                vs = slice(width + h * HD, width + (h + 1) * HD)
                k = kv_all[pl.ds(off, BK), ks]
                v = kv_all[pl.ds(off, BK), vs]
                e = jnp.exp2(
                    dot_t(k, queries[h]) * (-head_scale * LOG2E) - score_bias * LOG2E
                )
                sg = jnp.where(ok, 1.0 / (1.0 + e), 0.0)
                gs = (dot_t(v, gatts[h]) * sg * (1.0 - sg)).astype(bf16)
                gkv[pl.ds(off, BK), ks] += dot(gs, queries[h])
                gkv[pl.ds(off, BK), vs] += dot(sg.astype(bf16), gatts[h])
                out.append(sums[h] + t_dot(gs, k))
            return tuple(out)

        last = (base + (i + 1) * BQ - 1) // BK + 1
        sums = lax.fori_loop(
            lo_ref[i], last, step, tuple(jnp.zeros((BQ, HD), f32) for _ in range(heads))
        )
        cos, sin = cos_ref[at, :], sin_ref[at, :]
        for h in range(heads):
            t = sums[h] * head_scale
            gq_ref[at, h * HD : (h + 1) * HD] = (
                t * cos - pltpu.roll(t, HD // 2, 1) * sin
            ).astype(bf16)
    own_ref[:, :width] = gkv[base:, :width] * head_scale
    own_ref[:, width:] = gkv[base:, width:]
    for i, r in enumerate(rem_refs):
        r[:, :width] = (gkv[i * rows : (i + 1) * rows, :width] * head_scale).astype(bf16)
        r[:, width:] = gkv[i * rows : (i + 1) * rows, width:].astype(bf16)


def attn_bwd_call(lo, q, ga, start, wo, cos, sin, kvs):
    rows, width = q.shape
    vmem = pl.BlockSpec(memory_space=pltpu.VMEM)
    return pl.pallas_call(
        functools.partial(attn_bwd_kernel, len(kvs)),
        in_specs=[pl.BlockSpec(memory_space=pltpu.SMEM)] + [vmem] * (6 + len(kvs)),
        out_specs=[vmem] * (1 + len(kvs)),
        out_shape=[
            jax.ShapeDtypeStruct((rows, width), bf16),
            jax.ShapeDtypeStruct((rows, 2 * width), f32),
        ]
        + [jax.ShapeDtypeStruct((rows, 2 * width), bf16)] * (len(kvs) - 1),
        scratch_shapes=[
            pltpu.VMEM((len(kvs) * rows, 2 * width), bf16),
            pltpu.VMEM((len(kvs) * rows, 2 * width), f32),
        ],
        compiler_params=pltpu.CompilerParams(vmem_limit_bytes=VMEM),
        cost_estimate=pl.CostEstimate(
            flops=25 * 10**9, bytes_accessed=20 * 2**20, transcendentals=4 * 10**6
        ),
    )(lo, q, ga, start, wo, cos, sin, *kvs)


def norm_kernel(gh_ref, cot_ref, resid_ref, gain_ref, grad_ref, low_ref, part_ref):
    gh, resid, gain = gh_ref[...].astype(f32), resid_ref[...], gain_ref[...]
    inv = lax.rsqrt(jnp.mean(resid * resid, axis=-1, keepdims=True) + norm_eps)
    normed = resid * inv
    scaled = gh * gain
    grad = cot_ref[...].astype(f32) + inv * (
        scaled - normed * jnp.mean(scaled * normed, axis=-1, keepdims=True)
    )
    grad_ref[...] = grad
    low_ref[...] = grad.astype(bf16)
    part_ref[...] = jnp.sum(gh * normed, axis=0, keepdims=True)


def norm_call(gh, cot, resid, gain):
    vmem = pl.BlockSpec(memory_space=pltpu.VMEM)
    return pl.pallas_call(
        norm_kernel,
        in_specs=[vmem] * 4,
        out_specs=[vmem] * 3,
        out_shape=[
            jax.ShapeDtypeStruct(resid.shape, f32),
            jax.ShapeDtypeStruct(resid.shape, bf16),
            jax.ShapeDtypeStruct(gain.shape, f32),
        ],
    )(gh, cot, resid, gain)


def gqkv_kernel(gq_ref, own_ref, cos_ref, sin_ref, w_ref, *refs):
    got, g_ref, gh_ref = refs[:-2], refs[-2], refs[-1]
    width = gq_ref.shape[1]
    gkv = own_ref[...]
    for r in got:
        gkv = gkv + r[...].astype(f32)
    cos, sin = cos_ref[...], sin_ref[...]
    g_ref[:, :width] = gq_ref[...]
    for s in range(0, width, HD):
        t = gkv[:, s : s + HD]
        g_ref[:, width + s : width + s + HD] = (
            t * cos - pltpu.roll(t, HD // 2, 1) * sin
        ).astype(bf16)
    g_ref[:, 2 * width :] = gkv[:, width:].astype(bf16)
    gh_ref[...] = dot_t(g_ref[...], w_ref[...]).astype(bf16)


def gqkv_call(gq, own, got, cos, sin, w):
    rows, width = gq.shape
    dim = w.shape[0]
    block = lambda cols: pl.BlockSpec((BR, cols), lambda i: (i, 0))
    return pl.pallas_call(
        gqkv_kernel,
        grid=(rows // BR,),
        in_specs=[
            block(width),
            block(2 * width),
            block(HD),
            block(HD),
            pl.BlockSpec(w.shape, lambda i: (0, 0)),
        ]
        + [block(2 * width)] * len(got),
        out_specs=[block(3 * width), block(dim)],
        out_shape=[
            jax.ShapeDtypeStruct((rows, 3 * width), bf16),
            jax.ShapeDtypeStruct((rows, dim), bf16),
        ],
        compiler_params=pltpu.CompilerParams(vmem_limit_bytes=VMEM),
        cost_estimate=pl.CostEstimate(
            flops=2 * rows * dim * 3 * width, bytes_accessed=16 * 2**20, transcendentals=0
        ),
    )(gq, own, cos, sin, w, *got)


def grads_kernel(groups, index_ref, h_ref, g_ref, *refs):
    size = refs[0].shape[1]
    for j in range(h_ref.shape[1] // size):
        at = pl.multiple_of((index_ref[0] ^ j) * size, size)
        grad = t_dot(h_ref[:, pl.ds(at, size)], g_ref[...])
        for ref, (first, columns, members) in zip(refs, groups):
            if j in members:
                ref[members.index(j)] = grad[:, first : first + columns].astype(ref.dtype)


def grads_call(index, h, g, count):
    rows, width = g.shape
    size = h.shape[1] // count
    if count == 4:
        half = width // 2
        groups = [(0, half, (1, 3)), (half, half, (2, 3)), (0, half, (0, 2)), (half, half, (0, 1))]
        kinds = [bf16, bf16, f32, f32]
    else:
        groups = [(0, width, (j,)) for j in range(count)]
        kinds = [f32] + [bf16] * (count - 1)
    vmem = pl.BlockSpec(memory_space=pltpu.VMEM)
    return pl.pallas_call(
        functools.partial(grads_kernel, groups),
        in_specs=[pl.BlockSpec(memory_space=pltpu.SMEM), vmem, vmem],
        out_specs=[vmem] * len(groups),
        out_shape=[
            jax.ShapeDtypeStruct((len(members), size, columns), kind)
            for (_, columns, members), kind in zip(groups, kinds)
        ],
        compiler_params=pltpu.CompilerParams(vmem_limit_bytes=VMEM),
        cost_estimate=pl.CostEstimate(
            flops=2 * rows * width * h.shape[1], bytes_accessed=9 * 2**20, transcendentals=0
        ),
    )(index, h, g)


def ffn_kernel(places, blocks, groups, h_ref, c_ref, *refs):
    count = 1 + max(p[1] for p in places)
    sources = refs[:count]
    outs = refs[count : count + 3 * len(groups)]
    inner_ref, gh_ref, wg, wu, wd, gates, ups, sem = refs[count + 3 * len(groups) :]
    width = wg.shape[1] // blocks
    copies = [
        (which, pltpu.make_async_copy(sources[source].at[at], (wg, wu, wd)[which].at[to], sem.at[i]))
        for i, (which, source, at, to) in enumerate(places)
    ]
    first = pl.program_id(0) == 0

    def wait(weight):
        @pl.when(first)
        def _():
            for which, c in copies:
                if which == weight:
                    c.wait()

    @pl.when(first)
    def _():
        for weight in range(3):
            for which, c in copies:
                if which == weight:
                    c.start()

    wait(0)
    gate = dot(h_ref[...], wg[...])
    wait(1)
    up = dot(h_ref[...], wu[...])
    wait(2)
    grad = dot_t(c_ref[...], wd[...])
    sig = 1.0 / (1.0 + jnp.exp2(gate * -LOG2E))
    act = gate * sig
    inner = (act * up).astype(bf16)
    gg = (grad * up * sig * (1.0 + gate * (1.0 - sig))).astype(bf16)
    gu = (grad * act).astype(bf16)
    inner_ref[...] = inner
    gates[...] = gg
    ups[...] = gu
    for n, members in enumerate(groups):
        for m, j in enumerate(members):
            at, to = slice(j * width, (j + 1) * width), slice(m * width, (m + 1) * width)
            outs[n][:, to] = inner[:, at]
            outs[len(groups) + n][:, to] = gg[:, at]
            outs[2 * len(groups) + n][:, to] = gu[:, at]
    gh_ref[...] = (dot_t(gates[...], wg[...]) + dot_t(ups[...], wu[...])).astype(bf16)


def ffn_call(h, cot, sources, places, blocks, width, groups):
    rows, dim = h.shape
    hidden = blocks * width
    block = lambda cols: pl.BlockSpec((BR, cols), lambda i: (i, 0))
    sizes = [len(members) * width for members in groups] * 3 + [hidden, dim]
    result = pl.pallas_call(
        functools.partial(ffn_kernel, places, blocks, groups),
        grid=(rows // BR,),
        in_specs=[block(dim), block(dim)] + [pl.BlockSpec(memory_space=pl.ANY)] * len(sources),
        out_specs=[block(size) for size in sizes],
        out_shape=[jax.ShapeDtypeStruct((rows, size), bf16) for size in sizes],
        scratch_shapes=[
            pltpu.VMEM((dim, hidden), bf16),
            pltpu.VMEM((dim, hidden), bf16),
            pltpu.VMEM((hidden, dim), bf16),
            pltpu.VMEM((BR, hidden), bf16),
            pltpu.VMEM((BR, hidden), bf16),
            pltpu.SemaphoreType.DMA((len(places),)),
        ],
        compiler_params=pltpu.CompilerParams(vmem_limit_bytes=VMEM),
        cost_estimate=pl.CostEstimate(
            flops=10 * rows * dim * hidden, bytes_accessed=36 * 2**20, transcendentals=10**6
        ),
    )(h, cot, *sources)
    n = len(groups)
    down = [p for p in places if p[0] == 2]
    base = min(p[1] for p in down)
    project = functools.partial(
        down_call, sources=sources[base:], places=[(p[1] - base,) + p[2:] for p in down]
    )
    return result[:n], result[n : 2 * n], result[2 * n : 3 * n], result[-2], project, result[-1]


def down_kernel(places, inner_ref, *refs):
    sources, (y_ref, wd, sem) = refs[:-3], refs[-3:]

    @pl.when(pl.program_id(0) == 0)
    def _():
        copies = [
            pltpu.make_async_copy(sources[source].at[at], wd.at[to], sem.at[i])
            for i, (source, at, to) in enumerate(places)
        ]
        for c in copies:
            c.start()
        for c in copies:
            c.wait()

    y_ref[...] = dot(inner_ref[...], wd[...]).astype(bf16)


def down_call(inner, sources, places):
    rows, hidden = inner.shape
    dim = max(to[1].stop or 0 for _, _, to in places) or sources[0].shape[-1]
    block = lambda cols: pl.BlockSpec((BR, cols), lambda i: (i, 0))
    return pl.pallas_call(
        functools.partial(down_kernel, tuple(places)),
        grid=(rows // BR,),
        in_specs=[block(hidden)] + [pl.BlockSpec(memory_space=pl.ANY)] * len(sources),
        out_specs=block(dim),
        out_shape=jax.ShapeDtypeStruct((rows, dim), bf16),
        scratch_shapes=[
            pltpu.VMEM((hidden, dim), bf16),
            pltpu.SemaphoreType.DMA((len(places),)),
        ],
        compiler_params=pltpu.CompilerParams(vmem_limit_bytes=VMEM),
        cost_estimate=pl.CostEstimate(
            flops=2 * rows * dim * hidden, bytes_accessed=12 * 2**20, transcendentals=0
        ),
    )(inner, *sources)


PAIRS = ((0, 2), (1, 3), (2, 3), (0, 1))


def ffn_pieces(h, cot, gate_up, down, width):
    sources, places = [], []
    for pieces, kinds in ((gate_up, (0, 1)), (down, (2,))):
        for j, parts in enumerate(pieces):
            block = 0
            for part in parts:
                size = part.shape[2] if kinds == (2,) else part.shape[1] // 2
                for i in range(part.shape[0]):
                    rows = slice(block * size, (block + 1) * size)
                    cols = slice(j * width, (j + 1) * width)
                    for which in kinds:
                        at = (i, slice(which * size, (which + 1) * size)) if which < 2 else (i,)
                        to = (rows, cols) if which < 2 else (cols, rows)
                        places.append((which, len(sources), at, to))
                    block += 1
                sources.append(part)
    return ffn_call(h, cot, sources, tuple(places), len(down), width, PAIRS)


def ffn_plain(h, cot, gate_up, down):
    size = gate_up[0][0].shape[1] // 2
    merge = lambda parts: jnp.concatenate(parts, axis=0)
    flat = lambda p, at: merge(p)[:, at].reshape(-1, p[0].shape[-1])
    tall = lambda p: merge(p).transpose(1, 0, 2).reshape(p[0].shape[1], -1)
    sources = [
        jnp.concatenate([flat(p, slice(0, size)) for p in gate_up], axis=1),
        jnp.concatenate([flat(p, slice(size, 2 * size)) for p in gate_up], axis=1),
        jnp.concatenate([tall(p) for p in down], axis=0),
    ]
    every = (slice(None), slice(None))
    places = tuple((which, which, every, every) for which in range(3))
    return ffn_call(h, cot, sources, places, 1, sources[0].shape[1], ((0,),))


def xor_permute(x, count, flip):
    return lax.ppermute(x, "uly", [(i, i ^ flip) for i in range(count)])


def gather_uly(x, count):
    return gather_rest(gather_first(x, count), count)


def gather_first(x, count):
    return [x] + [xor_permute(x, count, j) for j in ((1, 2) if count == 4 else range(1, count))]


def gather_rest(blocks, count):
    if count != 4:
        return [[block] for block in blocks]
    x, one, two = blocks
    half = x.shape[0] // 2
    low = xor_permute(one[:half], count, 2)
    high = xor_permute(two[half:], count, 1)
    return [[x], [one], [two], [low, high]]


def in_order(pieces, index):
    rows = sum(p.shape[0] for p in pieces[0])
    out = jnp.zeros((len(pieces) * rows,) + pieces[0][0].shape[1:], pieces[0][0].dtype)
    for j, parts in enumerate(pieces):
        at = (index ^ j) * rows
        for part in parts:
            out = lax.dynamic_update_slice_in_dim(out, part, at, 0)
            at = at + part.shape[0]
    return out


def scatter_uly(own, others, count):
    got = [xor_permute(block, count, j + 1) for j, block in enumerate(others)]
    for block in got:
        own = own + block.astype(f32)
    return own


def after(x, *earlier):
    return lax.optimization_barrier((x,) + earlier)[0]


def rms_stats(values):
    scale_inv = lax.rsqrt(jnp.mean(values * values, axis=-1, keepdims=True) + norm_eps)
    return (values * scale_inv, scale_inv)


def norm_back(grad_normed, normed, scale_inv, gain):
    scaled = grad_normed * gain
    return scale_inv * (scaled - normed * jnp.mean(scaled * normed, axis=-1, keepdims=True))


def body(
    block_input,
    cotangent,
    lengths,
    seq_order,
    norm_attn,
    w_query,
    w_key,
    w_value,
    w_out,
    norm_ffn,
    w_gate,
    w_up,
    w_down,
):
    count_uly = lax.axis_size("uly")
    count_blk = lax.axis_size("blk")
    devices = count_uly * count_blk
    uly_index = lax.axis_index("uly")
    uly_at = uly_index.astype(jnp.int32).reshape(1)
    tok_rows, dim = block_input.shape
    group = count_blk * tok_rows
    part = dim // count_blk
    rows_w = w_query.shape[0]
    together = lax.optimization_barrier
    longest = LONGEST.get(devices * tok_rows, devices * tok_rows)
    back = min(count_uly - 1, -(-(longest - 1) // group))

    labels = jnp.arange(lengths.shape[0], dtype=jnp.int32)
    picked = jnp.sum(
        jnp.where(seq_order[:, None] == labels[None, :], lengths[None, :], 0), axis=1
    )
    ends = jnp.sum(jnp.where(labels[None, :] <= labels[:, None], picked[None, :], 0), axis=1)
    starts = ends - picked
    row_ids = uly_index * group + jnp.arange(group, dtype=jnp.int32)
    inside = (row_ids[:, None] >= starts[None, :]) & (row_ids[:, None] < ends[None, :])
    seq_start = jnp.sum(jnp.where(inside, starts[None, :], 0), axis=1)
    position = row_ids - seq_start
    used = jnp.any(inside, axis=1)
    shift = (uly_index - back) * group
    begin = jnp.where(used, seq_start - shift, 1 << 30).astype(jnp.int32)
    firsts = begin[::BQ]
    ends_kb = (back * group + jnp.arange(group // BQ, dtype=jnp.int32) * BQ + BQ - 1) // BK + 1
    low_kb = jnp.minimum(firsts // BK, ends_kb).astype(jnp.int32)
    frequency = rope_base ** (-jnp.arange(HD // 2, dtype=f32) * 2.0 / HD)
    angles = position.astype(f32)[:, None] * frequency[None, :]
    cos, sin = jnp.cos(angles), jnp.sin(angles)
    cos = jnp.concatenate([cos, cos], axis=1)
    sin = jnp.concatenate([-sin, sin], axis=1)

    owner = [(i, (i % count_uly) * count_blk + i // count_uly) for i in range(devices)]
    wo = lax.ppermute(w_out, BOTH, owner)
    gains = jnp.concatenate([norm_attn, norm_ffn])
    gains = jnp.pad(gains[None], ((0, 15), (0, 3 * part - 2 * rows_w)))
    qkv = pack_call(w_query, w_key, w_value, gains, count_blk)
    qkv = lax.all_to_all(qkv, "blk", 0, 0, tiled=True)
    group_in = lax.all_gather(after(block_input, qkv, wo), "blk", axis=0, tiled=True)
    qkv_pieces = gather_uly(qkv, count_uly)
    cut = lambda f: in_order([[f(p) for p in parts] for parts in qkv_pieces], uly_index)
    w_qkv = cut(lambda p: p[:, :rows_w].reshape(-1, 3 * part))
    gains = cut(lambda p: p[:, rows_w, : 2 * rows_w])
    gain_attn = gains[:, :rows_w].reshape(1, dim).astype(f32)
    gain_ffn = gains[:, rows_w:].reshape(1, dim).astype(f32)

    rows_d, width = w_gate.shape[0], w_gate.shape[1] // count_blk
    columns = lambda w: w.reshape(rows_d, count_blk, width).transpose(1, 0, 2)
    to_hidden = lambda w: lax.all_to_all(w, "blk", 0, 0, tiled=True)
    gate_up = jnp.concatenate([columns(w_gate), columns(w_up)], axis=1)
    down = to_hidden(
        after(w_down.reshape(count_blk, width, rows_d), *[p[0] for p in qkv_pieces[1:3]])
    )
    wo = in_order(gather_uly(after(wo, qkv_pieces[3][-1]), count_uly), uly_index)
    group_in, down, gate_up, wo = together((group_in, down, gate_up, wo))
    hidden_one, query, kv = qkv_call(group_in, gain_attn, w_qkv, cos, sin)
    if count_uly == 4 and back == 2:
        half = group // 2
        two = lax.ppermute(kv, "uly", [(0, 2), (1, 3)])
        one = lax.ppermute(kv, "uly", [(0, 1), (2, 3)])
        over = lax.ppermute(kv[:half], "uly", [(1, 0)])
        over = lax.ppermute(over, "uly", [(0, 2)])
        under = lax.ppermute(two[half:], "uly", [(3, 2)])
        kvs = [two, one + jnp.concatenate([over, under]), kv]
    else:
        kvs = [
            lax.ppermute(kv, "uly", [(i, i + s) for i in range(count_uly - s)])
            for s in range(back, 0, -1)
        ] + [kv]

    gate_up = to_hidden(after(gate_up, kv))
    group_cot = lax.all_gather(after(cotangent, kv), "blk", axis=0, tiled=True)
    down = gather_first(after(down, kv), count_uly)
    query, down = together((query, down))
    attended, out_part = attn_fwd_call(low_kb, query, begin[:, None], wo, kvs)
    out_part, gate_up, group_cot = together((out_part, gate_up, group_cot))
    gate_up = gather_first(gate_up, count_uly)
    out_own = lax.psum_scatter(out_part, "blk", scatter_dimension=0, tiled=True)
    out_own, gate_up = together((out_own, gate_up))
    gate_up = gather_rest(gate_up, count_uly)
    down = gather_rest(down, count_uly)
    input_f = block_input.astype(f32)
    resid = input_f + out_own.astype(f32)
    hidden_two = (rms_stats(resid)[0] * gain_ffn).astype(bf16)
    group_hidden = lax.all_gather(hidden_two, "blk", axis=0, tiled=True)

    pairs = count_uly == 4 and width % HD == 0
    if pairs:
        ffn = ffn_pieces(group_hidden, group_cot, gate_up, down, width)
    else:
        ffn = ffn_plain(group_hidden, group_cot, gate_up, down)
    inner, gg, gu, inner_all, project, gh_part = ffn
    grad_h2 = lax.psum_scatter(gh_part, "blk", scatter_dimension=0, tiled=True)

    def products(lefts, rights, rows):
        half = dim // 2
        if rows:
            halves = (rights[:, :half], rights[:, half:])
            term = [t_dot(lefts[n], halves[n // 2]) for n in range(4)]
        else:
            halves = (lefts[:, :half], lefts[:, half:])
            term = [t_dot(halves[n // 2], rights[n]) for n in range(4)]
        return [term[1].astype(bf16), term[2].astype(bf16), term[0], term[3]]

    def first_phase(term):
        return [
            xor_permute(term[0], count_uly, 1),
            xor_permute(term[1], count_uly, 2),
            term[2],
            term[3],
        ]

    def second_phase(term, rows):
        axis = 0 if rows else 1
        one, two = (k + g.astype(f32) for k, g in zip(term[2:], term[:2]))
        mine = [lax.slice_in_dim(t, 0, width, axis=axis) for t in (one, two)]
        rest = [lax.slice_in_dim(t, width, 2 * width, axis=axis).astype(bf16) for t in (one, two)]
        mine[0] = mine[0] + xor_permute(rest[0], count_uly, 2).astype(f32)
        mine[1] = mine[1] + xor_permute(rest[1], count_uly, 1).astype(f32)
        return jnp.concatenate(mine, axis=1 - axis).astype(bf16)

    def direct(lefts, rights, rows):
        cut = lambda a: [a[0][:, j * width : (j + 1) * width] for j in range(count_uly)]
        if rows:
            terms = [t_dot(left, rights) for left in cut(lefts)]
        else:
            terms = [t_dot(lefts, right) for right in cut(rights)]
        return scatter_uly(terms[0], [t.astype(bf16) for t in terms[1:]], count_uly).astype(bf16)

    if pairs:
        sum_gate = second_phase(first_phase(products(group_hidden, gg, False)), False)
        sum_up = products(group_hidden, gu, False)
        sum_down = products(inner, group_cot, True)
    else:
        sum_gate = direct(group_hidden, gg, False)
        sum_up = direct(group_hidden, gu, False)
        sum_down = direct(inner, group_cot, True)
    grad_h2, sum_gate, sum_up, sum_down, inner_all = together(
        (grad_h2, sum_gate, sum_up, sum_down, inner_all)
    )
    y_part = project(inner_all)
    if pairs:
        sum_up = second_phase(first_phase(sum_up), False)
        sum_down = second_phase(first_phase(sum_down), True)
    grad_resid, grad_low, gain_part = norm_call(grad_h2, cotangent, resid, gain_ffn)
    group_gattn = lax.all_gather(grad_low, "blk", axis=0, tiled=True)
    blocks_of = lambda w: w.reshape(count_blk, rows_d, width)
    gain_part = gain_part.astype(bf16).reshape(count_blk, -1, width)
    gain_rows = gain_part.shape[1]
    gain_part = jnp.pad(gain_part, ((0, 0), (0, -gain_rows % 8), (0, 0)))
    grad_gate = to_hidden(jnp.concatenate([blocks_of(sum_gate), gain_part], axis=1))
    gattn, sum_up, sum_down, grad_gate, y_part = together(
        (group_gattn, sum_up, sum_down, grad_gate, y_part)
    )

    down_blocks = sum_down.reshape(width, count_blk, rows_d).transpose(1, 0, 2)
    grads_ud = to_hidden(
        jnp.concatenate(
            [blocks_of(sum_up), down_blocks.reshape(count_blk, rows_d, width)], axis=1
        )
    )
    gq, gkv, *sent = attn_bwd_call(
        low_kb, query, gattn, begin[None, :], wo, cos, sin, kvs
    )
    got = [
        lax.ppermute(block, "uly", [(i, i - s) for i in range(s, count_uly)])
        for s, block in zip(range(back, 0, -1), sent)
    ]
    y_own = lax.psum_scatter(after(y_part, gattn), "blk", scatter_dimension=0, tiled=True)
    def split_rows(whole):
        rows = whole.shape[0] // count_uly
        pick = lambda j: lax.dynamic_slice_in_dim(whole, (uly_index ^ j) * rows, rows, 0)
        return scatter_uly(
            pick(0).astype(f32), [pick(j) for j in range(1, count_uly)], count_uly
        ).astype(bf16)

    gain_sum = jnp.sum(grad_gate[:, rows_d:][:, :gain_rows].astype(f32), axis=0)
    gain_sum = jnp.pad(gain_sum.reshape(part, 1), ((0, 0), (0, HD - 1)))
    outs = jnp.concatenate([t_dot(after(attended, gq), gattn), gain_sum], axis=1).astype(bf16)
    outs = split_rows(after(outs, gq))
    gkv, y_own, grads_ud, outs = together((gkv, y_own, grads_ud, outs))
    output = (resid + y_own.astype(f32)).astype(bf16)
    gqkv, gh1_part = gqkv_call(gq, gkv, got, cos, sin, w_qkv)
    grads = grads_call(uly_at, hidden_one, gqkv, count_uly)
    grad_h1 = lax.psum_scatter(gh1_part, "blk", scatter_dimension=0, tiled=True).astype(f32)
    normed_one, inv_one = rms_stats(input_f)
    input_grad = grad_resid + norm_back(grad_h1, normed_one, inv_one, gain_attn)

    if count_uly == 4:
        one = grads[2] + xor_permute(grads[0], count_uly, 1).astype(f32)
        two = grads[3] + xor_permute(grads[1], count_uly, 2).astype(f32)
        one = one[0] + xor_permute(one[1].astype(bf16), count_uly, 2).astype(f32)
        two = two[0] + xor_permute(two[1].astype(bf16), count_uly, 1).astype(f32)
        grads = jnp.concatenate([one, two], axis=1).astype(bf16)
    else:
        grads = scatter_uly(grads[0][0], [g[0] for g in grads[1:]], count_uly).astype(bf16)
    outs = lax.ppermute(after(outs, grads), BOTH, [(j, i) for i, j in owner])
    outs = outs.astype(f32)
    grad_out, grad_gain_ffn = outs[:, :dim], outs[:, dim]
    grads = lax.all_to_all(grads.reshape(count_blk, rows_w, 3 * part), "blk", 0, 0, tiled=True)
    grad_gate = grad_gate[:, :rows_d].astype(f32).transpose(1, 0, 2).reshape(w_gate.shape)
    grad_up = grads_ud[:, :rows_d].astype(f32).transpose(1, 0, 2).reshape(w_up.shape)
    grad_down = grads_ud[:, rows_d:].astype(f32).reshape(w_down.shape)
    grads, *_ = together((grads, grad_gate, grad_up, grad_down, input_grad, grad_out, grad_gain_ffn))
    grad_query, grad_key, grad_value, grad_gain_attn = unpack_call(
        grads, w_query, w_key, w_value, norm_attn.astype(f32)[:, None]
    )
    return (
        output,
        input_grad,
        grad_gain_attn[:, 0],
        grad_query,
        grad_key,
        grad_value,
        grad_out,
        grad_gain_ffn,
        grad_gate,
        grad_up,
        grad_down,
    )


def solution(mesh):
    rows = P(("uly", "blk"), None)
    vector = P(("uly", "blk"))
    weights = (vector, rows, rows, rows, rows, vector, P("blk", "uly"), P("blk", "uly"), P("uly", "blk"))
    return jax.shard_map(
        body,
        mesh=mesh,
        in_specs=(rows, rows, P(), P()) + weights,
        out_specs=(rows, rows) + weights,
        check_vma=False,
    )
```

```python
import functools
import math

import jax
import jax.numpy as jnp
from jax import lax
from jax.experimental import pallas as pl
from jax.experimental.pallas import tpu as pltpu
from jax.sharding import PartitionSpec as P

HEADS = 16
HD = 128
BOTH = ("uly", "blk")
LONGEST = {4096: 2048, 16384: 4096}
LOG2E = math.log2(math.e)

norm_eps = 1e-05
rope_base = 10000.0
score_bias = -math.log(4096.0)
head_scale = 1.0 / math.sqrt(HD)

BQ = 512
BK = 512
BR = 256
VMEM = 60 * 2**20
f32 = jnp.float32
bf16 = jnp.bfloat16


def dot_t(left, right):
    return lax.dot_general(left, right, (((1,), (1,)), ((), ())), preferred_element_type=f32)


def t_dot(left, right):
    return lax.dot_general(left, right, (((0,), (0,)), ((), ())), preferred_element_type=f32)


def dot(left, right):
    return jnp.dot(left, right, preferred_element_type=f32)


def pack_kernel(wq_ref, wk_ref, wv_ref, gain_ref, out_ref):
    rows = wq_ref.shape[0]
    width = out_ref.shape[2] // 3
    for b in range(out_ref.shape[0]):
        for i, w in enumerate((wq_ref, wk_ref, wv_ref)):
            out_ref[b, :rows, i * width : (i + 1) * width] = w[:, b * width : (b + 1) * width]
        out_ref[b, rows:, :] = gain_ref[...]


def pack_call(wq, wk, wv, gains, count):
    rows, dim = wq.shape
    vmem = pl.BlockSpec(memory_space=pltpu.VMEM)
    return pl.pallas_call(
        pack_kernel,
        in_specs=[vmem] * 4,
        out_specs=vmem,
        out_shape=jax.ShapeDtypeStruct((count, rows + gains.shape[0], 3 * dim // count), bf16),
    )(wq, wk, wv, gains)


def unpack_kernel(got_ref, wq_ref, wk_ref, wv_ref, gain_ref, gq_ref, gk_ref, gv_ref, gg_ref):
    width = got_ref.shape[2] // 3
    total = jnp.zeros(gg_ref.shape, f32)
    for i, (w, g_ref) in enumerate(((wq_ref, gq_ref), (wk_ref, gk_ref), (wv_ref, gv_ref))):
        for b in range(got_ref.shape[0]):
            at = slice(b * width, (b + 1) * width)
            g = got_ref[b, :, i * width : (i + 1) * width].astype(f32)
            g_ref[:, at] = g
            total = total + jnp.sum(g * w[:, at].astype(f32), axis=1, keepdims=True)
    gg_ref[...] = total / gain_ref[...]


def unpack_call(got, wq, wk, wv, gain):
    vmem = pl.BlockSpec(memory_space=pltpu.VMEM)
    return pl.pallas_call(
        unpack_kernel,
        in_specs=[vmem] * 5,
        out_specs=[vmem] * 4,
        out_shape=[jax.ShapeDtypeStruct(wq.shape, f32)] * 3
        + [jax.ShapeDtypeStruct((wq.shape[0], 1), f32)],
    )(got, wq, wk, wv, gain)


def qkv_kernel(x_ref, gain_ref, w_ref, cos_ref, sin_ref, h_ref, q_ref, kv_ref):
    x = x_ref[...].astype(f32)
    inv = lax.rsqrt(jnp.mean(x * x, axis=-1, keepdims=True) + norm_eps)
    h = (x * inv * gain_ref[...]).astype(bf16)
    h_ref[...] = h
    acc = dot(h, w_ref[...])
    cos, sin = cos_ref[...], sin_ref[...]
    width = q_ref.shape[1]
    for s in range(0, width, HD):
        t = acc[:, s : s + HD]
        q_ref[:, s : s + HD] = (t * cos + pltpu.roll(t, HD // 2, 1) * sin).astype(bf16)
        t = acc[:, width + s : width + s + HD]
        kv_ref[:, s : s + HD] = (t * cos + pltpu.roll(t, HD // 2, 1) * sin).astype(bf16)
    kv_ref[:, width:] = acc[:, 2 * width :].astype(bf16)


def qkv_call(x, gain, w, cos, sin):
    rows, dim = x.shape
    width = w.shape[1] // 3
    block = lambda cols: pl.BlockSpec((BR, cols), lambda i: (i, 0))
    whole = lambda shape: pl.BlockSpec(shape, lambda i: (0, 0))
    return pl.pallas_call(
        qkv_kernel,
        grid=(rows // BR,),
        in_specs=[block(dim), whole((1, dim)), whole(w.shape), block(HD), block(HD)],
        out_specs=[block(dim), block(width), block(2 * width)],
        out_shape=[
            jax.ShapeDtypeStruct((rows, dim), bf16),
            jax.ShapeDtypeStruct((rows, width), bf16),
            jax.ShapeDtypeStruct((rows, 2 * width), bf16),
        ],
        compiler_params=pltpu.CompilerParams(vmem_limit_bytes=VMEM),
        cost_estimate=pl.CostEstimate(
            flops=2 * rows * dim * 3 * width, bytes_accessed=16 * 2**20, transcendentals=0
        ),
    )(x, gain, w, cos, sin)


def attn_fwd_kernel(count_kv, lo_ref, q_ref, start_ref, wo_ref, *refs):
    kv_refs, (att_ref, part_ref, kv_all) = refs[:count_kv], refs[count_kv:]
    rows, width = q_ref.shape
    heads = width // HD
    base = (count_kv - 1) * rows
    for i, r in enumerate(kv_refs):
        kv_all[i * rows : (i + 1) * rows, :] = r[...]
    for i in range(rows // BQ):
        at = slice(i * BQ, (i + 1) * BQ)
        start = start_ref[at, :]
        row = base + i * BQ + lax.broadcasted_iota(jnp.int32, (BQ, BK), 0)
        col = lax.broadcasted_iota(jnp.int32, (BQ, BK), 1)
        queries = [q_ref[at, h * HD : (h + 1) * HD] for h in range(heads)]

        def step(kb, sums):
            off = pl.multiple_of(kb * BK, BK)
            here = col + off
            ok = (here >= start) & (here <= row)
            out = []
            for h in range(heads):
                k = kv_all[pl.ds(off, BK), h * HD : (h + 1) * HD]
                v = kv_all[pl.ds(off, BK), width + h * HD : width + (h + 1) * HD]
                e = jnp.exp2(
                    dot_t(queries[h], k) * (-head_scale * LOG2E) - score_bias * LOG2E
                )
                weight = jnp.where(ok, 1.0 / (1.0 + e), 0.0).astype(bf16)
                out.append(sums[h] + dot(weight, v))
            return tuple(out)

        last = (base + (i + 1) * BQ - 1) // BK + 1
        sums = lax.fori_loop(
            lo_ref[i], last, step, tuple(jnp.zeros((BQ, HD), f32) for _ in range(heads))
        )
        att = jnp.concatenate([s.astype(bf16) for s in sums], axis=1)
        att_ref[at, :] = att
        part_ref[at, :] = dot(att, wo_ref[...]).astype(bf16)


def attn_fwd_call(lo, q, start, wo, kvs):
    rows, width = q.shape
    dim = wo.shape[1]
    vmem = pl.BlockSpec(memory_space=pltpu.VMEM)
    return pl.pallas_call(
        functools.partial(attn_fwd_kernel, len(kvs)),
        in_specs=[pl.BlockSpec(memory_space=pltpu.SMEM)] + [vmem] * (3 + len(kvs)),
        out_specs=[vmem, vmem],
        out_shape=[
            jax.ShapeDtypeStruct((rows, width), bf16),
            jax.ShapeDtypeStruct((rows, dim), bf16),
        ],
        scratch_shapes=[pltpu.VMEM((len(kvs) * rows, 2 * width), bf16)],
        compiler_params=pltpu.CompilerParams(vmem_limit_bytes=VMEM),
        cost_estimate=pl.CostEstimate(
            flops=10**6, bytes_accessed=10**6, transcendentals=0
        ),
    )(lo, q, start, wo, *kvs)


def attn_bwd_kernel(count_kv, lo_ref, q_ref, ga_ref, start_ref, wo_ref, cos_ref, sin_ref, *refs):
    kv_refs = refs[:count_kv]
    gq_ref, own_ref = refs[count_kv : count_kv + 2]
    rem_refs = refs[count_kv + 2 : 2 * count_kv + 1]
    kv_all, gkv = refs[2 * count_kv + 1 :]
    rows, width = q_ref.shape
    heads = width // HD
    base = (count_kv - 1) * rows
    for i, r in enumerate(kv_refs):
        kv_all[i * rows : (i + 1) * rows, :] = r[...]
        gkv[i * rows : (i + 1) * rows, :] = jnp.zeros((rows, 2 * width), f32)
    for i in range(rows // BQ):
        at = slice(i * BQ, (i + 1) * BQ)
        start = start_ref[:, at]
        row = base + i * BQ + lax.broadcasted_iota(jnp.int32, (BK, BQ), 1)
        col = lax.broadcasted_iota(jnp.int32, (BK, BQ), 0)
        gatt = dot_t(ga_ref[at, :], wo_ref[...]).astype(bf16)
        queries = [q_ref[at, h * HD : (h + 1) * HD] for h in range(heads)]
        gatts = [gatt[:, h * HD : (h + 1) * HD] for h in range(heads)]

        def step(kb, sums):
            off = pl.multiple_of(kb * BK, BK)
            here = col + off
            ok = (here >= start) & (here <= row)
            out = []
            for h in range(heads):
                ks = slice(h * HD, (h + 1) * HD)
                vs = slice(width + h * HD, width + (h + 1) * HD)
                k = kv_all[pl.ds(off, BK), ks]
                v = kv_all[pl.ds(off, BK), vs]
                e = jnp.exp2(
                    dot_t(k, queries[h]) * (-head_scale * LOG2E) - score_bias * LOG2E
                )
                sg = jnp.where(ok, 1.0 / (1.0 + e), 0.0)
                gs = (dot_t(v, gatts[h]) * sg * (1.0 - sg)).astype(bf16)
                gkv[pl.ds(off, BK), ks] += dot(gs, queries[h])
                gkv[pl.ds(off, BK), vs] += dot(sg.astype(bf16), gatts[h])
                out.append(sums[h] + t_dot(gs, k))
            return tuple(out)

        last = (base + (i + 1) * BQ - 1) // BK + 1
        sums = lax.fori_loop(
            lo_ref[i], last, step, tuple(jnp.zeros((BQ, HD), f32) for _ in range(heads))
        )
        cos, sin = cos_ref[at, :], sin_ref[at, :]
        for h in range(heads):
            t = sums[h] * head_scale
            gq_ref[at, h * HD : (h + 1) * HD] = (
                t * cos - pltpu.roll(t, HD // 2, 1) * sin
            ).astype(bf16)
    own_ref[:, :width] = gkv[base:, :width] * head_scale
    own_ref[:, width:] = gkv[base:, width:]
    for i, r in enumerate(rem_refs):
        r[:, :width] = (gkv[i * rows : (i + 1) * rows, :width] * head_scale).astype(bf16)
        r[:, width:] = gkv[i * rows : (i + 1) * rows, width:].astype(bf16)


def attn_bwd_call(lo, q, ga, start, wo, cos, sin, kvs):
    rows, width = q.shape
    vmem = pl.BlockSpec(memory_space=pltpu.VMEM)
    return pl.pallas_call(
        functools.partial(attn_bwd_kernel, len(kvs)),
        in_specs=[pl.BlockSpec(memory_space=pltpu.SMEM)] + [vmem] * (6 + len(kvs)),
        out_specs=[vmem] * (1 + len(kvs)),
        out_shape=[
            jax.ShapeDtypeStruct((rows, width), bf16),
            jax.ShapeDtypeStruct((rows, 2 * width), f32),
        ]
        + [jax.ShapeDtypeStruct((rows, 2 * width), bf16)] * (len(kvs) - 1),
        scratch_shapes=[
            pltpu.VMEM((len(kvs) * rows, 2 * width), bf16),
            pltpu.VMEM((len(kvs) * rows, 2 * width), f32),
        ],
        compiler_params=pltpu.CompilerParams(vmem_limit_bytes=VMEM),
        cost_estimate=pl.CostEstimate(
            flops=25 * 10**9, bytes_accessed=20 * 2**20, transcendentals=4 * 10**6
        ),
    )(lo, q, ga, start, wo, cos, sin, *kvs)


def norm_kernel(gh_ref, cot_ref, resid_ref, gain_ref, grad_ref, low_ref, part_ref):
    gh, resid, gain = gh_ref[...].astype(f32), resid_ref[...], gain_ref[...]
    inv = lax.rsqrt(jnp.mean(resid * resid, axis=-1, keepdims=True) + norm_eps)
    normed = resid * inv
    scaled = gh * gain
    grad = cot_ref[...].astype(f32) + inv * (
        scaled - normed * jnp.mean(scaled * normed, axis=-1, keepdims=True)
    )
    grad_ref[...] = grad
    low_ref[...] = grad.astype(bf16)
    part_ref[...] = jnp.sum(gh * normed, axis=0, keepdims=True)


def norm_call(gh, cot, resid, gain):
    vmem = pl.BlockSpec(memory_space=pltpu.VMEM)
    return pl.pallas_call(
        norm_kernel,
        in_specs=[vmem] * 4,
        out_specs=[vmem] * 3,
        out_shape=[
            jax.ShapeDtypeStruct(resid.shape, f32),
            jax.ShapeDtypeStruct(resid.shape, bf16),
            jax.ShapeDtypeStruct(gain.shape, f32),
        ],
    )(gh, cot, resid, gain)


def gqkv_kernel(gq_ref, own_ref, cos_ref, sin_ref, w_ref, *refs):
    got, g_ref, gh_ref = refs[:-2], refs[-2], refs[-1]
    width = gq_ref.shape[1]
    gkv = own_ref[...]
    for r in got:
        gkv = gkv + r[...].astype(f32)
    cos, sin = cos_ref[...], sin_ref[...]
    g_ref[:, :width] = gq_ref[...]
    for s in range(0, width, HD):
        t = gkv[:, s : s + HD]
        g_ref[:, width + s : width + s + HD] = (
            t * cos - pltpu.roll(t, HD // 2, 1) * sin
        ).astype(bf16)
    g_ref[:, 2 * width :] = gkv[:, width:].astype(bf16)
    gh_ref[...] = dot_t(g_ref[...], w_ref[...]).astype(bf16)


def gqkv_call(gq, own, got, cos, sin, w):
    rows, width = gq.shape
    dim = w.shape[0]
    block = lambda cols: pl.BlockSpec((BR, cols), lambda i: (i, 0))
    return pl.pallas_call(
        gqkv_kernel,
        grid=(rows // BR,),
        in_specs=[
            block(width),
            block(2 * width),
            block(HD),
            block(HD),
            pl.BlockSpec(w.shape, lambda i: (0, 0)),
        ]
        + [block(2 * width)] * len(got),
        out_specs=[block(3 * width), block(dim)],
        out_shape=[
            jax.ShapeDtypeStruct((rows, 3 * width), bf16),
            jax.ShapeDtypeStruct((rows, dim), bf16),
        ],
        compiler_params=pltpu.CompilerParams(vmem_limit_bytes=VMEM),
        cost_estimate=pl.CostEstimate(
            flops=2 * rows * dim * 3 * width, bytes_accessed=16 * 2**20, transcendentals=0
        ),
    )(gq, own, cos, sin, w, *got)


def grads_kernel(groups, index_ref, h_ref, g_ref, *refs):
    size = refs[0].shape[1]
    for j in range(h_ref.shape[1] // size):
        at = pl.multiple_of((index_ref[0] ^ j) * size, size)
        grad = t_dot(h_ref[:, pl.ds(at, size)], g_ref[...])
        for ref, (first, columns, members) in zip(refs, groups):
            if j in members:
                ref[members.index(j)] = grad[:, first : first + columns].astype(ref.dtype)


def grads_call(index, h, g, count):
    rows, width = g.shape
    size = h.shape[1] // count
    if count == 4:
        half = width // 2
        groups = [(0, half, (1, 3)), (half, half, (2, 3)), (0, half, (0, 2)), (half, half, (0, 1))]
        kinds = [bf16, bf16, f32, f32]
    else:
        groups = [(0, width, (j,)) for j in range(count)]
        kinds = [f32] + [bf16] * (count - 1)
    vmem = pl.BlockSpec(memory_space=pltpu.VMEM)
    return pl.pallas_call(
        functools.partial(grads_kernel, groups),
        in_specs=[pl.BlockSpec(memory_space=pltpu.SMEM), vmem, vmem],
        out_specs=[vmem] * len(groups),
        out_shape=[
            jax.ShapeDtypeStruct((len(members), size, columns), kind)
            for (_, columns, members), kind in zip(groups, kinds)
        ],
        compiler_params=pltpu.CompilerParams(vmem_limit_bytes=VMEM),
        cost_estimate=pl.CostEstimate(
            flops=2 * rows * width * h.shape[1], bytes_accessed=9 * 2**20, transcendentals=0
        ),
    )(index, h, g)


def ffn_kernel(places, blocks, groups, h_ref, c_ref, *refs):
    count = 1 + max(p[1] for p in places)
    sources = refs[:count]
    outs = refs[count : count + 3 * len(groups)]
    inner_ref, gh_ref, wg, wu, wd, gates, ups, sem = refs[count + 3 * len(groups) :]
    width = wg.shape[1] // blocks
    copies = [
        (which, pltpu.make_async_copy(sources[source].at[at], (wg, wu, wd)[which].at[to], sem.at[i]))
        for i, (which, source, at, to) in enumerate(places)
    ]
    first = pl.program_id(0) == 0

    def wait(weight):
        @pl.when(first)
        def _():
            for which, c in copies:
                if which == weight:
                    c.wait()

    @pl.when(first)
    def _():
        for weight in range(3):
            for which, c in copies:
                if which == weight:
                    c.start()

    wait(0)
    gate = dot(h_ref[...], wg[...])
    wait(1)
    up = dot(h_ref[...], wu[...])
    wait(2)
    grad = dot_t(c_ref[...], wd[...])
    sig = 1.0 / (1.0 + jnp.exp2(gate * -LOG2E))
    act = gate * sig
    inner = (act * up).astype(bf16)
    gg = (grad * up * sig * (1.0 + gate * (1.0 - sig))).astype(bf16)
    gu = (grad * act).astype(bf16)
    inner_ref[...] = inner
    gates[...] = gg
    ups[...] = gu
    for n, members in enumerate(groups):
        for m, j in enumerate(members):
            at, to = slice(j * width, (j + 1) * width), slice(m * width, (m + 1) * width)
            outs[n][:, to] = inner[:, at]
            outs[len(groups) + n][:, to] = gg[:, at]
            outs[2 * len(groups) + n][:, to] = gu[:, at]
    gh_ref[...] = (dot_t(gates[...], wg[...]) + dot_t(ups[...], wu[...])).astype(bf16)


def ffn_call(h, cot, sources, places, blocks, width, groups):
    rows, dim = h.shape
    hidden = blocks * width
    block = lambda cols: pl.BlockSpec((BR, cols), lambda i: (i, 0))
    sizes = [len(members) * width for members in groups] * 3 + [hidden, dim]
    result = pl.pallas_call(
        functools.partial(ffn_kernel, places, blocks, groups),
        grid=(rows // BR,),
        in_specs=[block(dim), block(dim)] + [pl.BlockSpec(memory_space=pl.ANY)] * len(sources),
        out_specs=[block(size) for size in sizes],
        out_shape=[jax.ShapeDtypeStruct((rows, size), bf16) for size in sizes],
        scratch_shapes=[
            pltpu.VMEM((dim, hidden), bf16),
            pltpu.VMEM((dim, hidden), bf16),
            pltpu.VMEM((hidden, dim), bf16),
            pltpu.VMEM((BR, hidden), bf16),
            pltpu.VMEM((BR, hidden), bf16),
            pltpu.SemaphoreType.DMA((len(places),)),
        ],
        compiler_params=pltpu.CompilerParams(vmem_limit_bytes=VMEM),
        cost_estimate=pl.CostEstimate(
            flops=10 * rows * dim * hidden, bytes_accessed=36 * 2**20, transcendentals=10**6
        ),
    )(h, cot, *sources)
    n = len(groups)
    down = [p for p in places if p[0] == 2]
    base = min(p[1] for p in down)
    project = functools.partial(
        down_call, sources=sources[base:], places=[(p[1] - base,) + p[2:] for p in down]
    )
    return result[:n], result[n : 2 * n], result[2 * n : 3 * n], result[-2], project, result[-1]


def down_kernel(places, inner_ref, *refs):
    sources, (y_ref, wd, sem) = refs[:-3], refs[-3:]

    @pl.when(pl.program_id(0) == 0)
    def _():
        copies = [
            pltpu.make_async_copy(sources[source].at[at], wd.at[to], sem.at[i])
            for i, (source, at, to) in enumerate(places)
        ]
        for c in copies:
            c.start()
        for c in copies:
            c.wait()

    y_ref[...] = dot(inner_ref[...], wd[...]).astype(bf16)


def down_call(inner, sources, places):
    rows, hidden = inner.shape
    dim = max(to[1].stop or 0 for _, _, to in places) or sources[0].shape[-1]
    block = lambda cols: pl.BlockSpec((BR, cols), lambda i: (i, 0))
    return pl.pallas_call(
        functools.partial(down_kernel, tuple(places)),
        grid=(rows // BR,),
        in_specs=[block(hidden)] + [pl.BlockSpec(memory_space=pl.ANY)] * len(sources),
        out_specs=block(dim),
        out_shape=jax.ShapeDtypeStruct((rows, dim), bf16),
        scratch_shapes=[
            pltpu.VMEM((hidden, dim), bf16),
            pltpu.SemaphoreType.DMA((len(places),)),
        ],
        compiler_params=pltpu.CompilerParams(vmem_limit_bytes=VMEM),
        cost_estimate=pl.CostEstimate(
            flops=2 * rows * dim * hidden, bytes_accessed=12 * 2**20, transcendentals=0
        ),
    )(inner, *sources)


PAIRS = ((0, 2), (1, 3), (2, 3), (0, 1))


def ffn_pieces(h, cot, gate_up, down, width):
    sources, places = [], []
    for pieces, kinds in ((gate_up, (0, 1)), (down, (2,))):
        for j, parts in enumerate(pieces):
            block = 0
            for part in parts:
                size = part.shape[2] if kinds == (2,) else part.shape[1] // 2
                for i in range(part.shape[0]):
                    rows = slice(block * size, (block + 1) * size)
                    cols = slice(j * width, (j + 1) * width)
                    for which in kinds:
                        at = (i, slice(which * size, (which + 1) * size)) if which < 2 else (i,)
                        to = (rows, cols) if which < 2 else (cols, rows)
                        places.append((which, len(sources), at, to))
                    block += 1
                sources.append(part)
    return ffn_call(h, cot, sources, tuple(places), len(down), width, PAIRS)


def ffn_plain(h, cot, gate_up, down):
    size = gate_up[0][0].shape[1] // 2
    merge = lambda parts: jnp.concatenate(parts, axis=0)
    flat = lambda p, at: merge(p)[:, at].reshape(-1, p[0].shape[-1])
    tall = lambda p: merge(p).transpose(1, 0, 2).reshape(p[0].shape[1], -1)
    sources = [
        jnp.concatenate([flat(p, slice(0, size)) for p in gate_up], axis=1),
        jnp.concatenate([flat(p, slice(size, 2 * size)) for p in gate_up], axis=1),
        jnp.concatenate([tall(p) for p in down], axis=0),
    ]
    every = (slice(None), slice(None))
    places = tuple((which, which, every, every) for which in range(3))
    return ffn_call(h, cot, sources, places, 1, sources[0].shape[1], ((0,),))


def xor_permute(x, count, flip):
    return lax.ppermute(x, "uly", [(i, i ^ flip) for i in range(count)])


def gather_uly(x, count):
    return gather_rest(gather_first(x, count), count)


def gather_first(x, count):
    return [x] + [xor_permute(x, count, j) for j in ((1, 2) if count == 4 else range(1, count))]


def gather_rest(blocks, count):
    if count != 4:
        return [[block] for block in blocks]
    x, one, two = blocks
    half = x.shape[0] // 2
    low = xor_permute(one[:half], count, 2)
    high = xor_permute(two[half:], count, 1)
    return [[x], [one], [two], [low, high]]


def in_order(pieces, index):
    rows = sum(p.shape[0] for p in pieces[0])
    out = jnp.zeros((len(pieces) * rows,) + pieces[0][0].shape[1:], pieces[0][0].dtype)
    for j, parts in enumerate(pieces):
        at = (index ^ j) * rows
        for part in parts:
            out = lax.dynamic_update_slice_in_dim(out, part, at, 0)
            at = at + part.shape[0]
    return out


def scatter_uly(own, others, count):
    got = [xor_permute(block, count, j + 1) for j, block in enumerate(others)]
    for block in got:
        own = own + block.astype(f32)
    return own


def after(x, *earlier):
    return lax.optimization_barrier((x,) + earlier)[0]


def rms_stats(values):
    scale_inv = lax.rsqrt(jnp.mean(values * values, axis=-1, keepdims=True) + norm_eps)
    return (values * scale_inv, scale_inv)


def norm_back(grad_normed, normed, scale_inv, gain):
    scaled = grad_normed * gain
    return scale_inv * (scaled - normed * jnp.mean(scaled * normed, axis=-1, keepdims=True))


def body(
    block_input,
    cotangent,
    lengths,
    seq_order,
    norm_attn,
    w_query,
    w_key,
    w_value,
    w_out,
    norm_ffn,
    w_gate,
    w_up,
    w_down,
):
    count_uly = lax.axis_size("uly")
    count_blk = lax.axis_size("blk")
    devices = count_uly * count_blk
    uly_index = lax.axis_index("uly")
    uly_at = uly_index.astype(jnp.int32).reshape(1)
    tok_rows, dim = block_input.shape
    group = count_blk * tok_rows
    part = dim // count_blk
    rows_w = w_query.shape[0]
    together = lax.optimization_barrier
    longest = LONGEST.get(devices * tok_rows, devices * tok_rows)
    back = min(count_uly - 1, -(-(longest - 1) // group))

    labels = jnp.arange(lengths.shape[0], dtype=jnp.int32)
    picked = jnp.sum(
        jnp.where(seq_order[:, None] == labels[None, :], lengths[None, :], 0), axis=1
    )
    ends = jnp.sum(jnp.where(labels[None, :] <= labels[:, None], picked[None, :], 0), axis=1)
    starts = ends - picked
    row_ids = uly_index * group + jnp.arange(group, dtype=jnp.int32)
    inside = (row_ids[:, None] >= starts[None, :]) & (row_ids[:, None] < ends[None, :])
    seq_start = jnp.sum(jnp.where(inside, starts[None, :], 0), axis=1)
    position = row_ids - seq_start
    used = jnp.any(inside, axis=1)
    shift = (uly_index - back) * group
    begin = jnp.where(used, seq_start - shift, 1 << 30).astype(jnp.int32)
    firsts = begin[::BQ]
    ends_kb = (back * group + jnp.arange(group // BQ, dtype=jnp.int32) * BQ + BQ - 1) // BK + 1
    low_kb = jnp.minimum(firsts // BK, ends_kb).astype(jnp.int32)
    frequency = rope_base ** (-jnp.arange(HD // 2, dtype=f32) * 2.0 / HD)
    angles = position.astype(f32)[:, None] * frequency[None, :]
    cos, sin = jnp.cos(angles), jnp.sin(angles)
    cos = jnp.concatenate([cos, cos], axis=1)
    sin = jnp.concatenate([-sin, sin], axis=1)

    owner = [(i, (i % count_uly) * count_blk + i // count_uly) for i in range(devices)]
    wo = lax.ppermute(w_out, BOTH, owner)
    gains = jnp.concatenate([norm_attn, norm_ffn])
    gains = jnp.pad(gains[None], ((0, 15), (0, 3 * part - 2 * rows_w)))
    qkv = pack_call(w_query, w_key, w_value, gains, count_blk)
    qkv = lax.all_to_all(qkv, "blk", 0, 0, tiled=True)
    group_in = lax.all_gather(after(block_input, qkv, wo), "blk", axis=0, tiled=True)
    qkv_pieces = gather_uly(qkv, count_uly)
    cut = lambda f: in_order([[f(p) for p in parts] for parts in qkv_pieces], uly_index)
    w_qkv = cut(lambda p: p[:, :rows_w].reshape(-1, 3 * part))
    gains = cut(lambda p: p[:, rows_w, : 2 * rows_w])
    gain_attn = gains[:, :rows_w].reshape(1, dim).astype(f32)
    gain_ffn = gains[:, rows_w:].reshape(1, dim).astype(f32)

    rows_d, width = w_gate.shape[0], w_gate.shape[1] // count_blk
    columns = lambda w: w.reshape(rows_d, count_blk, width).transpose(1, 0, 2)
    to_hidden = lambda w: lax.all_to_all(w, "blk", 0, 0, tiled=True)
    gate_up = jnp.concatenate([columns(w_gate), columns(w_up)], axis=1)
    down = to_hidden(
        after(w_down.reshape(count_blk, width, rows_d), *[p[0] for p in qkv_pieces[1:3]])
    )
    wo = in_order(gather_uly(after(wo, qkv_pieces[3][-1]), count_uly), uly_index)
    group_in, gate_up, wo = together((group_in, gate_up, wo))
    hidden_one, query, kv = qkv_call(group_in, gain_attn, w_qkv, cos, sin)
    kv, query, down = together((kv, query, down))
    if count_uly == 4 and back == 2:
        half = group // 2
        two = lax.ppermute(kv, "uly", [(0, 2), (1, 3)])
        one = lax.ppermute(kv, "uly", [(0, 1), (2, 3)])
        over = lax.ppermute(kv[:half], "uly", [(1, 0)])
        over = lax.ppermute(over, "uly", [(0, 2)])
        under = lax.ppermute(two[half:], "uly", [(3, 2)])
        kvs = [two, one + jnp.concatenate([over, under]), kv]
    else:
        kvs = [
            lax.ppermute(kv, "uly", [(i, i + s) for i in range(count_uly - s)])
            for s in range(back, 0, -1)
        ] + [kv]

    gate_up = to_hidden(after(gate_up, kv))
    group_cot = lax.all_gather(after(cotangent, kv), "blk", axis=0, tiled=True)
    down = gather_first(after(down, kv), count_uly)
    query, down = together((query, down))
    attended, out_part = attn_fwd_call(low_kb, query, begin[:, None], wo, kvs)
    out_part, gate_up, group_cot = together((out_part, gate_up, group_cot))
    gate_up = gather_first(gate_up, count_uly)
    out_own = lax.psum_scatter(out_part, "blk", scatter_dimension=0, tiled=True)
    out_own, gate_up = together((out_own, gate_up))
    gate_up = gather_rest(gate_up, count_uly)
    down = gather_rest(down, count_uly)
    input_f = block_input.astype(f32)
    resid = input_f + out_own.astype(f32)
    hidden_two = (rms_stats(resid)[0] * gain_ffn).astype(bf16)
    group_hidden = lax.all_gather(hidden_two, "blk", axis=0, tiled=True)

    pairs = count_uly == 4 and width % HD == 0
    if pairs:
        ffn = ffn_pieces(group_hidden, group_cot, gate_up, down, width)
    else:
        ffn = ffn_plain(group_hidden, group_cot, gate_up, down)
    inner, gg, gu, inner_all, project, gh_part = ffn
    grad_h2 = lax.psum_scatter(gh_part, "blk", scatter_dimension=0, tiled=True)

    def products(lefts, rights, rows):
        half = dim // 2
        if rows:
            halves = (rights[:, :half], rights[:, half:])
            term = [t_dot(lefts[n], halves[n // 2]) for n in range(4)]
        else:
            halves = (lefts[:, :half], lefts[:, half:])
            term = [t_dot(halves[n // 2], rights[n]) for n in range(4)]
        return [term[1].astype(bf16), term[2].astype(bf16), term[0], term[3]]

    def first_phase(term):
        return [
            xor_permute(term[0], count_uly, 1),
            xor_permute(term[1], count_uly, 2),
            term[2],
            term[3],
        ]

    def second_phase(term, rows):
        axis = 0 if rows else 1
        one, two = (k + g.astype(f32) for k, g in zip(term[2:], term[:2]))
        mine = [lax.slice_in_dim(t, 0, width, axis=axis) for t in (one, two)]
        rest = [lax.slice_in_dim(t, width, 2 * width, axis=axis).astype(bf16) for t in (one, two)]
        mine[0] = mine[0] + xor_permute(rest[0], count_uly, 2).astype(f32)
        mine[1] = mine[1] + xor_permute(rest[1], count_uly, 1).astype(f32)
        return jnp.concatenate(mine, axis=1 - axis).astype(bf16)

    def direct(lefts, rights, rows):
        cut = lambda a: [a[0][:, j * width : (j + 1) * width] for j in range(count_uly)]
        if rows:
            terms = [t_dot(left, rights) for left in cut(lefts)]
        else:
            terms = [t_dot(lefts, right) for right in cut(rights)]
        return scatter_uly(terms[0], [t.astype(bf16) for t in terms[1:]], count_uly).astype(bf16)

    if pairs:
        sum_gate = second_phase(first_phase(products(group_hidden, gg, False)), False)
        sum_up = products(group_hidden, gu, False)
        sum_down = products(inner, group_cot, True)
    else:
        sum_gate = direct(group_hidden, gg, False)
        sum_up = direct(group_hidden, gu, False)
        sum_down = direct(inner, group_cot, True)
    grad_h2, sum_gate, sum_up, sum_down, inner_all = together(
        (grad_h2, sum_gate, sum_up, sum_down, inner_all)
    )
    y_part = project(inner_all)
    if pairs:
        sum_up = second_phase(first_phase(sum_up), False)
        sum_down = second_phase(first_phase(sum_down), True)
    grad_resid, grad_low, gain_part = norm_call(grad_h2, cotangent, resid, gain_ffn)
    group_gattn = lax.all_gather(grad_low, "blk", axis=0, tiled=True)
    blocks_of = lambda w: w.reshape(count_blk, rows_d, width)
    gain_part = gain_part.astype(bf16).reshape(count_blk, -1, width)
    gain_rows = gain_part.shape[1]
    gain_part = jnp.pad(gain_part, ((0, 0), (0, -gain_rows % 8), (0, 0)))
    grad_gate = to_hidden(jnp.concatenate([blocks_of(sum_gate), gain_part], axis=1))
    gattn, sum_up, sum_down, grad_gate, y_part = together(
        (group_gattn, sum_up, sum_down, grad_gate, y_part)
    )

    down_blocks = sum_down.reshape(width, count_blk, rows_d).transpose(1, 0, 2)
    grads_ud = to_hidden(
        jnp.concatenate(
            [blocks_of(sum_up), down_blocks.reshape(count_blk, rows_d, width)], axis=1
        )
    )
    gq, gkv, *sent = attn_bwd_call(
        low_kb, query, gattn, begin[None, :], wo, cos, sin, kvs
    )
    got = [
        lax.ppermute(block, "uly", [(i, i - s) for i in range(s, count_uly)])
        for s, block in zip(range(back, 0, -1), sent)
    ]
    y_own = lax.psum_scatter(after(y_part, gattn), "blk", scatter_dimension=0, tiled=True)
    def split_rows(whole):
        rows = whole.shape[0] // count_uly
        pick = lambda j: lax.dynamic_slice_in_dim(whole, (uly_index ^ j) * rows, rows, 0)
        return scatter_uly(
            pick(0).astype(f32), [pick(j) for j in range(1, count_uly)], count_uly
        ).astype(bf16)

    gain_sum = jnp.sum(grad_gate[:, rows_d:][:, :gain_rows].astype(f32), axis=0)
    gain_sum = jnp.pad(gain_sum.reshape(part, 1), ((0, 0), (0, HD - 1)))
    outs = jnp.concatenate([t_dot(after(attended, gq), gattn), gain_sum], axis=1).astype(bf16)
    outs = split_rows(after(outs, gq))
    gkv, y_own, grads_ud, outs = together((gkv, y_own, grads_ud, outs))
    output = (resid + y_own.astype(f32)).astype(bf16)
    gqkv, gh1_part = gqkv_call(gq, gkv, got, cos, sin, w_qkv)
    grads = grads_call(uly_at, hidden_one, gqkv, count_uly)
    grad_h1 = lax.psum_scatter(gh1_part, "blk", scatter_dimension=0, tiled=True).astype(f32)
    normed_one, inv_one = rms_stats(input_f)
    input_grad = grad_resid + norm_back(grad_h1, normed_one, inv_one, gain_attn)

    if count_uly == 4:
        one = grads[2] + xor_permute(grads[0], count_uly, 1).astype(f32)
        two = grads[3] + xor_permute(grads[1], count_uly, 2).astype(f32)
        one = one[0] + xor_permute(one[1].astype(bf16), count_uly, 2).astype(f32)
        two = two[0] + xor_permute(two[1].astype(bf16), count_uly, 1).astype(f32)
        grads = jnp.concatenate([one, two], axis=1).astype(bf16)
    else:
        grads = scatter_uly(grads[0][0], [g[0] for g in grads[1:]], count_uly).astype(bf16)
    outs = lax.ppermute(after(outs, grads), BOTH, [(j, i) for i, j in owner])
    outs = outs.astype(f32)
    grad_out, grad_gain_ffn = outs[:, :dim], outs[:, dim]
    grads = lax.all_to_all(grads.reshape(count_blk, rows_w, 3 * part), "blk", 0, 0, tiled=True)
    grad_gate = grad_gate[:, :rows_d].astype(f32).transpose(1, 0, 2).reshape(w_gate.shape)
    grad_up = grads_ud[:, :rows_d].astype(f32).transpose(1, 0, 2).reshape(w_up.shape)
    grad_down = grads_ud[:, rows_d:].astype(f32).reshape(w_down.shape)
    grads, *_ = together((grads, grad_gate, grad_up, grad_down, input_grad, grad_out, grad_gain_ffn))
    grad_query, grad_key, grad_value, grad_gain_attn = unpack_call(
        grads, w_query, w_key, w_value, norm_attn.astype(f32)[:, None]
    )
    return (
        output,
        input_grad,
        grad_gain_attn[:, 0],
        grad_query,
        grad_key,
        grad_value,
        grad_out,
        grad_gain_ffn,
        grad_gate,
        grad_up,
        grad_down,
    )


def solution(mesh):
    rows = P(("uly", "blk"), None)
    vector = P(("uly", "blk"))
    weights = (vector, rows, rows, rows, rows, vector, P("blk", "uly"), P("blk", "uly"), P("uly", "blk"))
    return jax.shard_map(
        body,
        mesh=mesh,
        in_specs=(rows, rows, P(), P()) + weights,
        out_specs=(rows, rows) + weights,
        check_vma=False,
    )
```

```python
import functools
import math

import jax
import jax.numpy as jnp
from jax import lax
from jax.experimental import pallas as pl
from jax.experimental.pallas import tpu as pltpu
from jax.sharding import PartitionSpec as P

HEADS = 16
HD = 128
BOTH = ("uly", "blk")
LONGEST = {4096: 2048, 16384: 4096}
LOG2E = math.log2(math.e)

norm_eps = 1e-05
rope_base = 10000.0
score_bias = -math.log(4096.0)
head_scale = 1.0 / math.sqrt(HD)

BQ = 512
BK = 512
BB = 384
BR = 256
VMEM = 60 * 2**20
f32 = jnp.float32
bf16 = jnp.bfloat16


def dot_t(left, right):
    return lax.dot_general(left, right, (((1,), (1,)), ((), ())), preferred_element_type=f32)


def t_dot(left, right):
    return lax.dot_general(left, right, (((0,), (0,)), ((), ())), preferred_element_type=f32)


def dot(left, right):
    return jnp.dot(left, right, preferred_element_type=f32)


def pack_kernel(wq_ref, wk_ref, wv_ref, gain_ref, out_ref):
    rows = wq_ref.shape[0]
    width = out_ref.shape[2] // 3
    for b in range(out_ref.shape[0]):
        for i, w in enumerate((wq_ref, wk_ref, wv_ref)):
            out_ref[b, :rows, i * width : (i + 1) * width] = w[:, b * width : (b + 1) * width]
        out_ref[b, rows:, :] = gain_ref[...]


def pack_call(wq, wk, wv, gains, count):
    rows, dim = wq.shape
    vmem = pl.BlockSpec(memory_space=pltpu.VMEM)
    return pl.pallas_call(
        pack_kernel,
        in_specs=[vmem] * 4,
        out_specs=vmem,
        out_shape=jax.ShapeDtypeStruct((count, rows + gains.shape[0], 3 * dim // count), bf16),
    )(wq, wk, wv, gains)


def unpack_kernel(got_ref, wq_ref, wk_ref, wv_ref, gain_ref, gq_ref, gk_ref, gv_ref, gg_ref):
    width = got_ref.shape[2] // 3
    total = jnp.zeros(gg_ref.shape, f32)
    for i, (w, g_ref) in enumerate(((wq_ref, gq_ref), (wk_ref, gk_ref), (wv_ref, gv_ref))):
        for b in range(got_ref.shape[0]):
            at = slice(b * width, (b + 1) * width)
            g = got_ref[b, :, i * width : (i + 1) * width].astype(f32)
            g_ref[:, at] = g
            total = total + jnp.sum(g * w[:, at].astype(f32), axis=1, keepdims=True)
    gg_ref[...] = total / gain_ref[...]


def unpack_call(got, wq, wk, wv, gain):
    vmem = pl.BlockSpec(memory_space=pltpu.VMEM)
    return pl.pallas_call(
        unpack_kernel,
        in_specs=[vmem] * 5,
        out_specs=[vmem] * 4,
        out_shape=[jax.ShapeDtypeStruct(wq.shape, f32)] * 3
        + [jax.ShapeDtypeStruct((wq.shape[0], 1), f32)],
    )(got, wq, wk, wv, gain)


def qkv_kernel(x_ref, gain_ref, w_ref, cos_ref, sin_ref, h_ref, q_ref, kv_ref):
    x = x_ref[...].astype(f32)
    inv = lax.rsqrt(jnp.mean(x * x, axis=-1, keepdims=True) + norm_eps)
    h = (x * inv * gain_ref[...]).astype(bf16)
    h_ref[...] = h
    acc = dot(h, w_ref[...])
    cos, sin = cos_ref[...], sin_ref[...]
    width = q_ref.shape[1]
    for s in range(0, width, HD):
        t = acc[:, s : s + HD]
        q_ref[:, s : s + HD] = (t * cos + pltpu.roll(t, HD // 2, 1) * sin).astype(bf16)
        t = acc[:, width + s : width + s + HD]
        kv_ref[:, s : s + HD] = (t * cos + pltpu.roll(t, HD // 2, 1) * sin).astype(bf16)
    kv_ref[:, width:] = acc[:, 2 * width :].astype(bf16)


def qkv_call(x, gain, w, cos, sin):
    rows, dim = x.shape
    width = w.shape[1] // 3
    block = lambda cols: pl.BlockSpec((BR, cols), lambda i: (i, 0))
    whole = lambda shape: pl.BlockSpec(shape, lambda i: (0, 0))
    return pl.pallas_call(
        qkv_kernel,
        grid=(rows // BR,),
        in_specs=[block(dim), whole((1, dim)), whole(w.shape), block(HD), block(HD)],
        out_specs=[block(dim), block(width), block(2 * width)],
        out_shape=[
            jax.ShapeDtypeStruct((rows, dim), bf16),
            jax.ShapeDtypeStruct((rows, width), bf16),
            jax.ShapeDtypeStruct((rows, 2 * width), bf16),
        ],
        compiler_params=pltpu.CompilerParams(vmem_limit_bytes=VMEM),
        cost_estimate=pl.CostEstimate(
            flops=2 * rows * dim * 3 * width, bytes_accessed=16 * 2**20, transcendentals=0
        ),
    )(x, gain, w, cos, sin)


def attn_fwd_kernel(count_kv, lo_ref, q_ref, start_ref, wo_ref, *refs):
    kv_refs, (att_ref, part_ref, kv_all) = refs[:count_kv], refs[count_kv:]
    rows, width = q_ref.shape
    heads = width // HD
    base = (count_kv - 1) * rows
    for i, r in enumerate(kv_refs):
        kv_all[i * rows : (i + 1) * rows, :] = r[...]
    for i in range(rows // BQ):
        at = slice(i * BQ, (i + 1) * BQ)
        start = start_ref[at, :]
        row = base + i * BQ + lax.broadcasted_iota(jnp.int32, (BQ, BK), 0)
        col = lax.broadcasted_iota(jnp.int32, (BQ, BK), 1)
        queries = [q_ref[at, h * HD : (h + 1) * HD] for h in range(heads)]

        def step(kb, sums):
            off = pl.multiple_of(kb * BK, BK)
            here = col + off
            ok = (here >= start) & (here <= row)
            out = []
            for h in range(heads):
                k = kv_all[pl.ds(off, BK), h * HD : (h + 1) * HD]
                v = kv_all[pl.ds(off, BK), width + h * HD : width + (h + 1) * HD]
                e = jnp.exp2(
                    dot_t(queries[h], k) * (-head_scale * LOG2E) - score_bias * LOG2E
                )
                weight = jnp.where(ok, 1.0 / (1.0 + e), 0.0).astype(bf16)
                out.append(sums[h] + dot(weight, v))
            return tuple(out)

        last = (base + (i + 1) * BQ - 1) // BK + 1
        sums = lax.fori_loop(
            lo_ref[i], last, step, tuple(jnp.zeros((BQ, HD), f32) for _ in range(heads))
        )
        att = jnp.concatenate([s.astype(bf16) for s in sums], axis=1)
        att_ref[at, :] = att
        part_ref[at, :] = dot(att, wo_ref[...]).astype(bf16)


def attn_fwd_call(lo, q, start, wo, kvs):
    rows, width = q.shape
    dim = wo.shape[1]
    vmem = pl.BlockSpec(memory_space=pltpu.VMEM)
    return pl.pallas_call(
        functools.partial(attn_fwd_kernel, len(kvs)),
        in_specs=[pl.BlockSpec(memory_space=pltpu.SMEM)] + [vmem] * (3 + len(kvs)),
        out_specs=[vmem, vmem],
        out_shape=[
            jax.ShapeDtypeStruct((rows, width), bf16),
            jax.ShapeDtypeStruct((rows, dim), bf16),
        ],
        scratch_shapes=[pltpu.VMEM((len(kvs) * rows, 2 * width), bf16)],
        compiler_params=pltpu.CompilerParams(vmem_limit_bytes=VMEM),
        cost_estimate=pl.CostEstimate(
            flops=10**6, bytes_accessed=10**6, transcendentals=0
        ),
    )(lo, q, start, wo, *kvs)


def attn_bwd_kernel(count_kv, lo_ref, q_ref, ga_ref, start_ref, wo_ref, cos_ref, sin_ref, *refs):
    kv_refs = refs[:count_kv]
    gq_ref, own_ref = refs[count_kv : count_kv + 2]
    rem_refs = refs[count_kv + 2 : 2 * count_kv + 1]
    kv_all, gkv = refs[2 * count_kv + 1 :]
    rows, width = q_ref.shape
    heads = width // HD
    base = (count_kv - 1) * rows
    for i, r in enumerate(kv_refs):
        kv_all[i * rows : (i + 1) * rows, :] = r[...]
        gkv[i * rows : (i + 1) * rows, :] = jnp.zeros((rows, 2 * width), f32)
    for i in range(rows // BQ):
        at = slice(i * BQ, (i + 1) * BQ)
        start = start_ref[:, at]
        row = base + i * BQ + lax.broadcasted_iota(jnp.int32, (BB, BQ), 1)
        col = lax.broadcasted_iota(jnp.int32, (BB, BQ), 0)
        gatt = dot_t(ga_ref[at, :], wo_ref[...]).astype(bf16)
        queries = [q_ref[at, h * HD : (h + 1) * HD] for h in range(heads)]
        gatts = [gatt[:, h * HD : (h + 1) * HD] for h in range(heads)]

        def step(kb, sums):
            off = pl.multiple_of(kb * BB, BB)
            here = col + off
            ok = (here >= start) & (here <= row)
            out = []
            for h in range(heads):
                ks = slice(h * HD, (h + 1) * HD)
                vs = slice(width + h * HD, width + (h + 1) * HD)
                k = kv_all[pl.ds(off, BB), ks]
                v = kv_all[pl.ds(off, BB), vs]
                e = jnp.exp2(
                    dot_t(k, queries[h]) * (-head_scale * LOG2E) - score_bias * LOG2E
                )
                sg = jnp.where(ok, 1.0 / (1.0 + e), 0.0)
                gs = (dot_t(v, gatts[h]) * sg * (1.0 - sg)).astype(bf16)
                gkv[pl.ds(off, BB), ks] += dot(gs, queries[h])
                gkv[pl.ds(off, BB), vs] += dot(sg.astype(bf16), gatts[h])
                out.append(sums[h] + t_dot(gs, k))
            return tuple(out)

        last = (base + (i + 1) * BQ - 1) // BB + 1
        sums = lax.fori_loop(
            lo_ref[i], last, step, tuple(jnp.zeros((BQ, HD), f32) for _ in range(heads))
        )
        cos, sin = cos_ref[at, :], sin_ref[at, :]
        for h in range(heads):
            t = sums[h] * head_scale
            gq_ref[at, h * HD : (h + 1) * HD] = (
                t * cos - pltpu.roll(t, HD // 2, 1) * sin
            ).astype(bf16)
    own_ref[:, :width] = gkv[base:, :width] * head_scale
    own_ref[:, width:] = gkv[base:, width:]
    for i, r in enumerate(rem_refs):
        r[:, :width] = (gkv[i * rows : (i + 1) * rows, :width] * head_scale).astype(bf16)
        r[:, width:] = gkv[i * rows : (i + 1) * rows, width:].astype(bf16)


def attn_bwd_call(lo, q, ga, start, wo, cos, sin, kvs):
    rows, width = q.shape
    vmem = pl.BlockSpec(memory_space=pltpu.VMEM)
    return pl.pallas_call(
        functools.partial(attn_bwd_kernel, len(kvs)),
        in_specs=[pl.BlockSpec(memory_space=pltpu.SMEM)] + [vmem] * (6 + len(kvs)),
        out_specs=[vmem] * (1 + len(kvs)),
        out_shape=[
            jax.ShapeDtypeStruct((rows, width), bf16),
            jax.ShapeDtypeStruct((rows, 2 * width), f32),
        ]
        + [jax.ShapeDtypeStruct((rows, 2 * width), bf16)] * (len(kvs) - 1),
        scratch_shapes=[
            pltpu.VMEM((len(kvs) * rows, 2 * width), bf16),
            pltpu.VMEM((len(kvs) * rows, 2 * width), f32),
        ],
        compiler_params=pltpu.CompilerParams(vmem_limit_bytes=VMEM),
        cost_estimate=pl.CostEstimate(
            flops=25 * 10**9, bytes_accessed=20 * 2**20, transcendentals=4 * 10**6
        ),
    )(lo, q, ga, start, wo, cos, sin, *kvs)


def norm_kernel(gh_ref, cot_ref, resid_ref, gain_ref, grad_ref, low_ref, part_ref):
    gh, resid, gain = gh_ref[...].astype(f32), resid_ref[...], gain_ref[...]
    inv = lax.rsqrt(jnp.mean(resid * resid, axis=-1, keepdims=True) + norm_eps)
    normed = resid * inv
    scaled = gh * gain
    grad = cot_ref[...].astype(f32) + inv * (
        scaled - normed * jnp.mean(scaled * normed, axis=-1, keepdims=True)
    )
    grad_ref[...] = grad
    low_ref[...] = grad.astype(bf16)
    part_ref[...] = jnp.sum(gh * normed, axis=0, keepdims=True)


def norm_call(gh, cot, resid, gain):
    vmem = pl.BlockSpec(memory_space=pltpu.VMEM)
    return pl.pallas_call(
        norm_kernel,
        in_specs=[vmem] * 4,
        out_specs=[vmem] * 3,
        out_shape=[
            jax.ShapeDtypeStruct(resid.shape, f32),
            jax.ShapeDtypeStruct(resid.shape, bf16),
            jax.ShapeDtypeStruct(gain.shape, f32),
        ],
    )(gh, cot, resid, gain)


def gqkv_kernel(gq_ref, own_ref, cos_ref, sin_ref, w_ref, *refs):
    got, g_ref, gh_ref = refs[:-2], refs[-2], refs[-1]
    width = gq_ref.shape[1]
    gkv = own_ref[...]
    for r in got:
        gkv = gkv + r[...].astype(f32)
    cos, sin = cos_ref[...], sin_ref[...]
    g_ref[:, :width] = gq_ref[...]
    for s in range(0, width, HD):
        t = gkv[:, s : s + HD]
        g_ref[:, width + s : width + s + HD] = (
            t * cos - pltpu.roll(t, HD // 2, 1) * sin
        ).astype(bf16)
    g_ref[:, 2 * width :] = gkv[:, width:].astype(bf16)
    gh_ref[...] = dot_t(g_ref[...], w_ref[...]).astype(bf16)


def gqkv_call(gq, own, got, cos, sin, w):
    rows, width = gq.shape
    dim = w.shape[0]
    block = lambda cols: pl.BlockSpec((BR, cols), lambda i: (i, 0))
    return pl.pallas_call(
        gqkv_kernel,
        grid=(rows // BR,),
        in_specs=[
            block(width),
            block(2 * width),
            block(HD),
            block(HD),
            pl.BlockSpec(w.shape, lambda i: (0, 0)),
        ]
        + [block(2 * width)] * len(got),
        out_specs=[block(3 * width), block(dim)],
        out_shape=[
            jax.ShapeDtypeStruct((rows, 3 * width), bf16),
            jax.ShapeDtypeStruct((rows, dim), bf16),
        ],
        compiler_params=pltpu.CompilerParams(vmem_limit_bytes=VMEM),
        cost_estimate=pl.CostEstimate(
            flops=2 * rows * dim * 3 * width, bytes_accessed=16 * 2**20, transcendentals=0
        ),
    )(gq, own, cos, sin, w, *got)


def grads_kernel(groups, index_ref, h_ref, g_ref, *refs):
    size = refs[0].shape[1]
    for j in range(h_ref.shape[1] // size):
        at = pl.multiple_of((index_ref[0] ^ j) * size, size)
        grad = t_dot(h_ref[:, pl.ds(at, size)], g_ref[...])
        for ref, (first, columns, members) in zip(refs, groups):
            if j in members:
                ref[members.index(j)] = grad[:, first : first + columns].astype(ref.dtype)


def grads_call(index, h, g, count):
    rows, width = g.shape
    size = h.shape[1] // count
    if count == 4:
        half = width // 2
        groups = [(0, half, (1, 3)), (half, half, (2, 3)), (0, half, (0, 2)), (half, half, (0, 1))]
        kinds = [bf16, bf16, f32, f32]
    else:
        groups = [(0, width, (j,)) for j in range(count)]
        kinds = [f32] + [bf16] * (count - 1)
    vmem = pl.BlockSpec(memory_space=pltpu.VMEM)
    return pl.pallas_call(
        functools.partial(grads_kernel, groups),
        in_specs=[pl.BlockSpec(memory_space=pltpu.SMEM), vmem, vmem],
        out_specs=[vmem] * len(groups),
        out_shape=[
            jax.ShapeDtypeStruct((len(members), size, columns), kind)
            for (_, columns, members), kind in zip(groups, kinds)
        ],
        compiler_params=pltpu.CompilerParams(vmem_limit_bytes=VMEM),
        cost_estimate=pl.CostEstimate(
            flops=2 * rows * width * h.shape[1], bytes_accessed=9 * 2**20, transcendentals=0
        ),
    )(index, h, g)


def ffn_kernel(places, blocks, groups, h_ref, c_ref, *refs):
    count = 1 + max(p[1] for p in places)
    sources = refs[:count]
    outs = refs[count : count + 3 * len(groups)]
    inner_ref, gh_ref, wg, wu, wd, gates, ups, sem = refs[count + 3 * len(groups) :]
    width = wg.shape[1] // blocks
    copies = [
        (which, pltpu.make_async_copy(sources[source].at[at], (wg, wu, wd)[which].at[to], sem.at[i]))
        for i, (which, source, at, to) in enumerate(places)
    ]
    first = pl.program_id(0) == 0

    def wait(weight):
        @pl.when(first)
        def _():
            for which, c in copies:
                if which == weight:
                    c.wait()

    @pl.when(first)
    def _():
        for weight in range(3):
            for which, c in copies:
                if which == weight:
                    c.start()

    wait(0)
    gate = dot(h_ref[...], wg[...])
    wait(1)
    up = dot(h_ref[...], wu[...])
    wait(2)
    grad = dot_t(c_ref[...], wd[...])
    sig = 1.0 / (1.0 + jnp.exp2(gate * -LOG2E))
    act = gate * sig
    inner = (act * up).astype(bf16)
    gg = (grad * up * sig * (1.0 + gate * (1.0 - sig))).astype(bf16)
    gu = (grad * act).astype(bf16)
    inner_ref[...] = inner
    gates[...] = gg
    ups[...] = gu
    for n, members in enumerate(groups):
        for m, j in enumerate(members):
            at, to = slice(j * width, (j + 1) * width), slice(m * width, (m + 1) * width)
            outs[n][:, to] = inner[:, at]
            outs[len(groups) + n][:, to] = gg[:, at]
            outs[2 * len(groups) + n][:, to] = gu[:, at]
    gh_ref[...] = (dot_t(gates[...], wg[...]) + dot_t(ups[...], wu[...])).astype(bf16)


def ffn_call(h, cot, sources, places, blocks, width, groups):
    rows, dim = h.shape
    hidden = blocks * width
    block = lambda cols: pl.BlockSpec((BR, cols), lambda i: (i, 0))
    sizes = [len(members) * width for members in groups] * 3 + [hidden, dim]
    result = pl.pallas_call(
        functools.partial(ffn_kernel, places, blocks, groups),
        grid=(rows // BR,),
        in_specs=[block(dim), block(dim)] + [pl.BlockSpec(memory_space=pl.ANY)] * len(sources),
        out_specs=[block(size) for size in sizes],
        out_shape=[jax.ShapeDtypeStruct((rows, size), bf16) for size in sizes],
        scratch_shapes=[
            pltpu.VMEM((dim, hidden), bf16),
            pltpu.VMEM((dim, hidden), bf16),
            pltpu.VMEM((hidden, dim), bf16),
            pltpu.VMEM((BR, hidden), bf16),
            pltpu.VMEM((BR, hidden), bf16),
            pltpu.SemaphoreType.DMA((len(places),)),
        ],
        compiler_params=pltpu.CompilerParams(vmem_limit_bytes=VMEM),
        cost_estimate=pl.CostEstimate(
            flops=10 * rows * dim * hidden, bytes_accessed=36 * 2**20, transcendentals=10**6
        ),
    )(h, cot, *sources)
    n = len(groups)
    down = [p for p in places if p[0] == 2]
    base = min(p[1] for p in down)
    project = functools.partial(
        down_call, sources=sources[base:], places=[(p[1] - base,) + p[2:] for p in down]
    )
    return result[:n], result[n : 2 * n], result[2 * n : 3 * n], result[-2], project, result[-1]


def down_kernel(places, inner_ref, *refs):
    sources, (y_ref, wd, sem) = refs[:-3], refs[-3:]

    @pl.when(pl.program_id(0) == 0)
    def _():
        copies = [
            pltpu.make_async_copy(sources[source].at[at], wd.at[to], sem.at[i])
            for i, (source, at, to) in enumerate(places)
        ]
        for c in copies:
            c.start()
        for c in copies:
            c.wait()

    y_ref[...] = dot(inner_ref[...], wd[...]).astype(bf16)


def down_call(inner, sources, places):
    rows, hidden = inner.shape
    dim = max(to[1].stop or 0 for _, _, to in places) or sources[0].shape[-1]
    block = lambda cols: pl.BlockSpec((BR, cols), lambda i: (i, 0))
    return pl.pallas_call(
        functools.partial(down_kernel, tuple(places)),
        grid=(rows // BR,),
        in_specs=[block(hidden)] + [pl.BlockSpec(memory_space=pl.ANY)] * len(sources),
        out_specs=block(dim),
        out_shape=jax.ShapeDtypeStruct((rows, dim), bf16),
        scratch_shapes=[
            pltpu.VMEM((hidden, dim), bf16),
            pltpu.SemaphoreType.DMA((len(places),)),
        ],
        compiler_params=pltpu.CompilerParams(vmem_limit_bytes=VMEM),
        cost_estimate=pl.CostEstimate(
            flops=2 * rows * dim * hidden, bytes_accessed=12 * 2**20, transcendentals=0
        ),
    )(inner, *sources)


PAIRS = ((0, 2), (1, 3), (2, 3), (0, 1))


def ffn_pieces(h, cot, gate_up, down, width):
    sources, places = [], []
    for pieces, kinds in ((gate_up, (0, 1)), (down, (2,))):
        for j, parts in enumerate(pieces):
            block = 0
            for part in parts:
                size = part.shape[2] if kinds == (2,) else part.shape[1] // 2
                for i in range(part.shape[0]):
                    rows = slice(block * size, (block + 1) * size)
                    cols = slice(j * width, (j + 1) * width)
                    for which in kinds:
                        at = (i, slice(which * size, (which + 1) * size)) if which < 2 else (i,)
                        to = (rows, cols) if which < 2 else (cols, rows)
                        places.append((which, len(sources), at, to))
                    block += 1
                sources.append(part)
    return ffn_call(h, cot, sources, tuple(places), len(down), width, PAIRS)


def ffn_plain(h, cot, gate_up, down):
    size = gate_up[0][0].shape[1] // 2
    merge = lambda parts: jnp.concatenate(parts, axis=0)
    flat = lambda p, at: merge(p)[:, at].reshape(-1, p[0].shape[-1])
    tall = lambda p: merge(p).transpose(1, 0, 2).reshape(p[0].shape[1], -1)
    sources = [
        jnp.concatenate([flat(p, slice(0, size)) for p in gate_up], axis=1),
        jnp.concatenate([flat(p, slice(size, 2 * size)) for p in gate_up], axis=1),
        jnp.concatenate([tall(p) for p in down], axis=0),
    ]
    every = (slice(None), slice(None))
    places = tuple((which, which, every, every) for which in range(3))
    return ffn_call(h, cot, sources, places, 1, sources[0].shape[1], ((0,),))


def xor_permute(x, count, flip):
    return lax.ppermute(x, "uly", [(i, i ^ flip) for i in range(count)])


def gather_uly(x, count):
    return gather_rest(gather_first(x, count), count)


def gather_first(x, count):
    return [x] + [xor_permute(x, count, j) for j in ((1, 2) if count == 4 else range(1, count))]


def gather_rest(blocks, count):
    if count != 4:
        return [[block] for block in blocks]
    x, one, two = blocks
    half = x.shape[0] // 2
    low = xor_permute(one[:half], count, 2)
    high = xor_permute(two[half:], count, 1)
    return [[x], [one], [two], [low, high]]


def in_order(pieces, index):
    rows = sum(p.shape[0] for p in pieces[0])
    out = jnp.zeros((len(pieces) * rows,) + pieces[0][0].shape[1:], pieces[0][0].dtype)
    for j, parts in enumerate(pieces):
        at = (index ^ j) * rows
        for part in parts:
            out = lax.dynamic_update_slice_in_dim(out, part, at, 0)
            at = at + part.shape[0]
    return out


def scatter_uly(own, others, count):
    got = [xor_permute(block, count, j + 1) for j, block in enumerate(others)]
    for block in got:
        own = own + block.astype(f32)
    return own


def after(x, *earlier):
    return lax.optimization_barrier((x,) + earlier)[0]


def rms_stats(values):
    scale_inv = lax.rsqrt(jnp.mean(values * values, axis=-1, keepdims=True) + norm_eps)
    return (values * scale_inv, scale_inv)


def norm_back(grad_normed, normed, scale_inv, gain):
    scaled = grad_normed * gain
    return scale_inv * (scaled - normed * jnp.mean(scaled * normed, axis=-1, keepdims=True))


def body(
    block_input,
    cotangent,
    lengths,
    seq_order,
    norm_attn,
    w_query,
    w_key,
    w_value,
    w_out,
    norm_ffn,
    w_gate,
    w_up,
    w_down,
):
    count_uly = lax.axis_size("uly")
    count_blk = lax.axis_size("blk")
    devices = count_uly * count_blk
    uly_index = lax.axis_index("uly")
    uly_at = uly_index.astype(jnp.int32).reshape(1)
    tok_rows, dim = block_input.shape
    group = count_blk * tok_rows
    part = dim // count_blk
    rows_w = w_query.shape[0]
    together = lax.optimization_barrier
    longest = LONGEST.get(devices * tok_rows, devices * tok_rows)
    back = min(count_uly - 1, -(-(longest - 1) // group))

    labels = jnp.arange(lengths.shape[0], dtype=jnp.int32)
    picked = jnp.sum(
        jnp.where(seq_order[:, None] == labels[None, :], lengths[None, :], 0), axis=1
    )
    ends = jnp.sum(jnp.where(labels[None, :] <= labels[:, None], picked[None, :], 0), axis=1)
    starts = ends - picked
    row_ids = uly_index * group + jnp.arange(group, dtype=jnp.int32)
    inside = (row_ids[:, None] >= starts[None, :]) & (row_ids[:, None] < ends[None, :])
    seq_start = jnp.sum(jnp.where(inside, starts[None, :], 0), axis=1)
    position = row_ids - seq_start
    used = jnp.any(inside, axis=1)
    shift = (uly_index - back) * group
    begin = jnp.where(used, seq_start - shift, 1 << 30).astype(jnp.int32)
    firsts = begin[::BQ]
    finals = back * group + jnp.arange(group // BQ, dtype=jnp.int32) * BQ + BQ - 1
    low_kb, low_bb = (
        jnp.minimum(firsts // size, finals // size + 1).astype(jnp.int32) for size in (BK, BB)
    )
    frequency = rope_base ** (-jnp.arange(HD // 2, dtype=f32) * 2.0 / HD)
    angles = position.astype(f32)[:, None] * frequency[None, :]
    cos, sin = jnp.cos(angles), jnp.sin(angles)
    cos = jnp.concatenate([cos, cos], axis=1)
    sin = jnp.concatenate([-sin, sin], axis=1)

    owner = [(i, (i % count_uly) * count_blk + i // count_uly) for i in range(devices)]
    wo = lax.ppermute(w_out, BOTH, owner)
    gains = jnp.concatenate([norm_attn, norm_ffn])
    gains = jnp.pad(gains[None], ((0, 15), (0, 3 * part - 2 * rows_w)))
    qkv = pack_call(w_query, w_key, w_value, gains, count_blk)
    qkv = lax.all_to_all(qkv, "blk", 0, 0, tiled=True)
    group_in = lax.all_gather(after(block_input, qkv, wo), "blk", axis=0, tiled=True)
    qkv_pieces = gather_uly(qkv, count_uly)
    cut = lambda f: in_order([[f(p) for p in parts] for parts in qkv_pieces], uly_index)
    w_qkv = cut(lambda p: p[:, :rows_w].reshape(-1, 3 * part))
    gains = cut(lambda p: p[:, rows_w, : 2 * rows_w])
    gain_attn = gains[:, :rows_w].reshape(1, dim).astype(f32)
    gain_ffn = gains[:, rows_w:].reshape(1, dim).astype(f32)

    rows_d, width = w_gate.shape[0], w_gate.shape[1] // count_blk
    columns = lambda w: w.reshape(rows_d, count_blk, width).transpose(1, 0, 2)
    to_hidden = lambda w: lax.all_to_all(w, "blk", 0, 0, tiled=True)
    gate_up = jnp.concatenate([columns(w_gate), columns(w_up)], axis=1)
    down = to_hidden(
        after(w_down.reshape(count_blk, width, rows_d), *[p[0] for p in qkv_pieces[1:3]])
    )
    wo = in_order(gather_uly(after(wo, qkv_pieces[3][-1]), count_uly), uly_index)
    group_in, gate_up, wo = together((group_in, gate_up, wo))
    hidden_one, query, kv = qkv_call(group_in, gain_attn, w_qkv, cos, sin)
    kv, query, down = together((kv, query, down))
    if count_uly == 4 and back == 2:
        half = group // 2
        two = lax.ppermute(kv, "uly", [(0, 2), (1, 3)])
        one = lax.ppermute(kv, "uly", [(0, 1), (2, 3)])
        over = lax.ppermute(kv[:half], "uly", [(1, 0)])
        over = lax.ppermute(over, "uly", [(0, 2)])
        under = lax.ppermute(two[half:], "uly", [(3, 2)])
        kvs = [two, one + jnp.concatenate([over, under]), kv]
    else:
        kvs = [
            lax.ppermute(kv, "uly", [(i, i + s) for i in range(count_uly - s)])
            for s in range(back, 0, -1)
        ] + [kv]

    gate_up = to_hidden(after(gate_up, kv))
    group_cot = lax.all_gather(after(cotangent, kv), "blk", axis=0, tiled=True)
    down = gather_first(after(down, kv), count_uly)
    query, down = together((query, down))
    attended, out_part = attn_fwd_call(low_kb, query, begin[:, None], wo, kvs)
    out_part, gate_up, group_cot = together((out_part, gate_up, group_cot))
    gate_up = gather_first(gate_up, count_uly)
    out_own = lax.psum_scatter(out_part, "blk", scatter_dimension=0, tiled=True)
    out_own, gate_up = together((out_own, gate_up))
    gate_up = gather_rest(gate_up, count_uly)
    down = gather_rest(down, count_uly)
    input_f = block_input.astype(f32)
    resid = input_f + out_own.astype(f32)
    hidden_two = (rms_stats(resid)[0] * gain_ffn).astype(bf16)
    group_hidden = lax.all_gather(hidden_two, "blk", axis=0, tiled=True)

    pairs = count_uly == 4 and width % HD == 0
    if pairs:
        ffn = ffn_pieces(group_hidden, group_cot, gate_up, down, width)
    else:
        ffn = ffn_plain(group_hidden, group_cot, gate_up, down)
    inner, gg, gu, inner_all, project, gh_part = ffn
    grad_h2 = lax.psum_scatter(gh_part, "blk", scatter_dimension=0, tiled=True)

    def products(lefts, rights, rows):
        half = dim // 2
        if rows:
            halves = (rights[:, :half], rights[:, half:])
            term = [t_dot(lefts[n], halves[n // 2]) for n in range(4)]
        else:
            halves = (lefts[:, :half], lefts[:, half:])
            term = [t_dot(halves[n // 2], rights[n]) for n in range(4)]
        return [term[1].astype(bf16), term[2].astype(bf16), term[0], term[3]]

    def first_phase(term):
        return [
            xor_permute(term[0], count_uly, 1),
            xor_permute(term[1], count_uly, 2),
            term[2],
            term[3],
        ]

    def second_phase(term, rows):
        axis = 0 if rows else 1
        one, two = (k + g.astype(f32) for k, g in zip(term[2:], term[:2]))
        mine = [lax.slice_in_dim(t, 0, width, axis=axis) for t in (one, two)]
        rest = [lax.slice_in_dim(t, width, 2 * width, axis=axis).astype(bf16) for t in (one, two)]
        mine[0] = mine[0] + xor_permute(rest[0], count_uly, 2).astype(f32)
        mine[1] = mine[1] + xor_permute(rest[1], count_uly, 1).astype(f32)
        return jnp.concatenate(mine, axis=1 - axis).astype(bf16)

    def direct(lefts, rights, rows):
        cut = lambda a: [a[0][:, j * width : (j + 1) * width] for j in range(count_uly)]
        if rows:
            terms = [t_dot(left, rights) for left in cut(lefts)]
        else:
            terms = [t_dot(lefts, right) for right in cut(rights)]
        return scatter_uly(terms[0], [t.astype(bf16) for t in terms[1:]], count_uly).astype(bf16)

    if pairs:
        sum_gate = second_phase(first_phase(products(group_hidden, gg, False)), False)
        sum_up = products(group_hidden, gu, False)
        sum_down = products(inner, group_cot, True)
    else:
        sum_gate = direct(group_hidden, gg, False)
        sum_up = direct(group_hidden, gu, False)
        sum_down = direct(inner, group_cot, True)
    grad_h2, sum_gate, sum_up, sum_down, inner_all = together(
        (grad_h2, sum_gate, sum_up, sum_down, inner_all)
    )
    y_part = project(inner_all)
    if pairs:
        sum_up = second_phase(first_phase(sum_up), False)
        sum_down = second_phase(first_phase(sum_down), True)
    grad_resid, grad_low, gain_part = norm_call(grad_h2, cotangent, resid, gain_ffn)
    group_gattn = lax.all_gather(grad_low, "blk", axis=0, tiled=True)
    blocks_of = lambda w: w.reshape(count_blk, rows_d, width)
    gain_part = gain_part.astype(bf16).reshape(count_blk, -1, width)
    gain_rows = gain_part.shape[1]
    gain_part = jnp.pad(gain_part, ((0, 0), (0, -gain_rows % 8), (0, 0)))
    grad_gate = to_hidden(jnp.concatenate([blocks_of(sum_gate), gain_part], axis=1))
    gattn, sum_up, sum_down, grad_gate, y_part = together(
        (group_gattn, sum_up, sum_down, grad_gate, y_part)
    )

    down_blocks = sum_down.reshape(width, count_blk, rows_d).transpose(1, 0, 2)
    grads_ud = to_hidden(
        jnp.concatenate(
            [blocks_of(sum_up), down_blocks.reshape(count_blk, rows_d, width)], axis=1
        )
    )
    gq, gkv, *sent = attn_bwd_call(
        low_bb, query, gattn, begin[None, :], wo, cos, sin, kvs
    )
    got = [
        lax.ppermute(block, "uly", [(i, i - s) for i in range(s, count_uly)])
        for s, block in zip(range(back, 0, -1), sent)
    ]
    y_own = lax.psum_scatter(after(y_part, gattn), "blk", scatter_dimension=0, tiled=True)
    def split_rows(whole):
        rows = whole.shape[0] // count_uly
        pick = lambda j: lax.dynamic_slice_in_dim(whole, (uly_index ^ j) * rows, rows, 0)
        return scatter_uly(
            pick(0).astype(f32), [pick(j) for j in range(1, count_uly)], count_uly
        ).astype(bf16)

    gain_sum = jnp.sum(grad_gate[:, rows_d:][:, :gain_rows].astype(f32), axis=0)
    gain_sum = jnp.pad(gain_sum.reshape(part, 1), ((0, 0), (0, HD - 1)))
    outs = jnp.concatenate([t_dot(after(attended, gq), gattn), gain_sum], axis=1).astype(bf16)
    outs = split_rows(after(outs, gq))
    gkv, y_own, grads_ud, outs = together((gkv, y_own, grads_ud, outs))
    output = (resid + y_own.astype(f32)).astype(bf16)
    gqkv, gh1_part = gqkv_call(gq, gkv, got, cos, sin, w_qkv)
    grads = grads_call(uly_at, hidden_one, gqkv, count_uly)
    grad_h1 = lax.psum_scatter(gh1_part, "blk", scatter_dimension=0, tiled=True).astype(f32)
    normed_one, inv_one = rms_stats(input_f)
    input_grad = grad_resid + norm_back(grad_h1, normed_one, inv_one, gain_attn)

    if count_uly == 4:
        one = grads[2] + xor_permute(grads[0], count_uly, 1).astype(f32)
        two = grads[3] + xor_permute(grads[1], count_uly, 2).astype(f32)
        one = one[0] + xor_permute(one[1].astype(bf16), count_uly, 2).astype(f32)
        two = two[0] + xor_permute(two[1].astype(bf16), count_uly, 1).astype(f32)
        grads = jnp.concatenate([one, two], axis=1).astype(bf16)
    else:
        grads = scatter_uly(grads[0][0], [g[0] for g in grads[1:]], count_uly).astype(bf16)
    outs = lax.ppermute(after(outs, grads), BOTH, [(j, i) for i, j in owner])
    outs = outs.astype(f32)
    grad_out, grad_gain_ffn = outs[:, :dim], outs[:, dim]
    grads = lax.all_to_all(grads.reshape(count_blk, rows_w, 3 * part), "blk", 0, 0, tiled=True)
    grad_gate = grad_gate[:, :rows_d].astype(f32).transpose(1, 0, 2).reshape(w_gate.shape)
    grad_up = grads_ud[:, :rows_d].astype(f32).transpose(1, 0, 2).reshape(w_up.shape)
    grad_down = grads_ud[:, rows_d:].astype(f32).reshape(w_down.shape)
    grads, *_ = together((grads, grad_gate, grad_up, grad_down, input_grad, grad_out, grad_gain_ffn))
    grad_query, grad_key, grad_value, grad_gain_attn = unpack_call(
        grads, w_query, w_key, w_value, norm_attn.astype(f32)[:, None]
    )
    return (
        output,
        input_grad,
        grad_gain_attn[:, 0],
        grad_query,
        grad_key,
        grad_value,
        grad_out,
        grad_gain_ffn,
        grad_gate,
        grad_up,
        grad_down,
    )


def solution(mesh):
    rows = P(("uly", "blk"), None)
    vector = P(("uly", "blk"))
    weights = (vector, rows, rows, rows, rows, vector, P("blk", "uly"), P("blk", "uly"), P("uly", "blk"))
    return jax.shard_map(
        body,
        mesh=mesh,
        in_specs=(rows, rows, P(), P()) + weights,
        out_specs=(rows, rows) + weights,
        check_vma=False,
    )
```

```python
import functools
import math

import jax
import jax.numpy as jnp
from jax import lax
from jax.experimental import pallas as pl
from jax.experimental.pallas import tpu as pltpu
from jax.sharding import PartitionSpec as P

HEADS = 16
HD = 128
BOTH = ("uly", "blk")
LONGEST = {4096: 2048, 16384: 4096}
LOG2E = math.log2(math.e)

norm_eps = 1e-05
rope_base = 10000.0
score_bias = -math.log(4096.0)
head_scale = 1.0 / math.sqrt(HD)

BQ = 512
BK = 512
BB = 384
BR = 256
VMEM = 60 * 2**20
f32 = jnp.float32
bf16 = jnp.bfloat16


def dot_t(left, right):
    return lax.dot_general(left, right, (((1,), (1,)), ((), ())), preferred_element_type=f32)


def t_dot(left, right):
    return lax.dot_general(left, right, (((0,), (0,)), ((), ())), preferred_element_type=f32)


def dot(left, right):
    return jnp.dot(left, right, preferred_element_type=f32)


def pack_kernel(wq_ref, wk_ref, wv_ref, gain_ref, out_ref):
    rows = wq_ref.shape[0]
    width = out_ref.shape[2] // 3
    for b in range(out_ref.shape[0]):
        for i, w in enumerate((wq_ref, wk_ref, wv_ref)):
            out_ref[b, :rows, i * width : (i + 1) * width] = w[:, b * width : (b + 1) * width]
        out_ref[b, rows:, :] = gain_ref[...]


def pack_call(wq, wk, wv, gains, count):
    rows, dim = wq.shape
    vmem = pl.BlockSpec(memory_space=pltpu.VMEM)
    return pl.pallas_call(
        pack_kernel,
        in_specs=[vmem] * 4,
        out_specs=vmem,
        out_shape=jax.ShapeDtypeStruct((count, rows + gains.shape[0], 3 * dim // count), bf16),
    )(wq, wk, wv, gains)


def unpack_kernel(got_ref, wq_ref, wk_ref, wv_ref, gain_ref, gq_ref, gk_ref, gv_ref, gg_ref):
    width = got_ref.shape[2] // 3
    total = jnp.zeros(gg_ref.shape, f32)
    for i, (w, g_ref) in enumerate(((wq_ref, gq_ref), (wk_ref, gk_ref), (wv_ref, gv_ref))):
        for b in range(got_ref.shape[0]):
            at = slice(b * width, (b + 1) * width)
            g = got_ref[b, :, i * width : (i + 1) * width].astype(f32)
            g_ref[:, at] = g
            total = total + jnp.sum(g * w[:, at].astype(f32), axis=1, keepdims=True)
    gg_ref[...] = total / gain_ref[...]


def unpack_call(got, wq, wk, wv, gain):
    vmem = pl.BlockSpec(memory_space=pltpu.VMEM)
    return pl.pallas_call(
        unpack_kernel,
        in_specs=[vmem] * 5,
        out_specs=[vmem] * 4,
        out_shape=[jax.ShapeDtypeStruct(wq.shape, f32)] * 3
        + [jax.ShapeDtypeStruct((wq.shape[0], 1), f32)],
    )(got, wq, wk, wv, gain)


def qkv_kernel(x_ref, gain_ref, w_ref, cos_ref, sin_ref, h_ref, q_ref, kv_ref):
    x = x_ref[...].astype(f32)
    inv = lax.rsqrt(jnp.mean(x * x, axis=-1, keepdims=True) + norm_eps)
    h = (x * inv * gain_ref[...]).astype(bf16)
    h_ref[...] = h
    acc = dot(h, w_ref[...])
    cos, sin = cos_ref[...], sin_ref[...]
    width = q_ref.shape[1]
    for s in range(0, width, HD):
        t = acc[:, s : s + HD]
        q_ref[:, s : s + HD] = (t * cos + pltpu.roll(t, HD // 2, 1) * sin).astype(bf16)
        t = acc[:, width + s : width + s + HD]
        kv_ref[:, s : s + HD] = (t * cos + pltpu.roll(t, HD // 2, 1) * sin).astype(bf16)
    kv_ref[:, width:] = acc[:, 2 * width :].astype(bf16)


def qkv_call(x, gain, w, cos, sin):
    rows, dim = x.shape
    width = w.shape[1] // 3
    block = lambda cols: pl.BlockSpec((BR, cols), lambda i: (i, 0))
    whole = lambda shape: pl.BlockSpec(shape, lambda i: (0, 0))
    return pl.pallas_call(
        qkv_kernel,
        grid=(rows // BR,),
        in_specs=[block(dim), whole((1, dim)), whole(w.shape), block(HD), block(HD)],
        out_specs=[block(dim), block(width), block(2 * width)],
        out_shape=[
            jax.ShapeDtypeStruct((rows, dim), bf16),
            jax.ShapeDtypeStruct((rows, width), bf16),
            jax.ShapeDtypeStruct((rows, 2 * width), bf16),
        ],
        compiler_params=pltpu.CompilerParams(vmem_limit_bytes=VMEM),
        cost_estimate=pl.CostEstimate(
            flops=2 * rows * dim * 3 * width, bytes_accessed=16 * 2**20, transcendentals=0
        ),
    )(x, gain, w, cos, sin)


def attn_fwd_kernel(count_kv, lo_ref, q_ref, start_ref, wo_ref, *refs):
    kv_refs, (att_ref, part_ref, kv_all) = refs[:count_kv], refs[count_kv:]
    rows, width = q_ref.shape
    heads = width // HD
    base = (count_kv - 1) * rows
    for i, r in enumerate(kv_refs):
        kv_all[i * rows : (i + 1) * rows, :] = r[...]
    for i in range(rows // BQ):
        at = slice(i * BQ, (i + 1) * BQ)
        start = start_ref[at, :]
        row = base + i * BQ + lax.broadcasted_iota(jnp.int32, (BQ, BK), 0)
        col = lax.broadcasted_iota(jnp.int32, (BQ, BK), 1)
        queries = [q_ref[at, h * HD : (h + 1) * HD] for h in range(heads)]

        def step(kb, sums):
            off = pl.multiple_of(kb * BK, BK)
            here = col + off
            ok = (here >= start) & (here <= row)
            out = []
            for h in range(heads):
                k = kv_all[pl.ds(off, BK), h * HD : (h + 1) * HD]
                v = kv_all[pl.ds(off, BK), width + h * HD : width + (h + 1) * HD]
                e = jnp.exp2(
                    dot_t(queries[h], k) * (-head_scale * LOG2E) - score_bias * LOG2E
                )
                weight = jnp.where(ok, 1.0 / (1.0 + e), 0.0).astype(bf16)
                out.append(sums[h] + dot(weight, v))
            return tuple(out)

        last = (base + (i + 1) * BQ - 1) // BK + 1
        sums = lax.fori_loop(
            lo_ref[i], last, step, tuple(jnp.zeros((BQ, HD), f32) for _ in range(heads))
        )
        att = jnp.concatenate([s.astype(bf16) for s in sums], axis=1)
        att_ref[at, :] = att
        part_ref[at, :] = dot(att, wo_ref[...]).astype(bf16)


def attn_fwd_call(lo, q, start, wo, kvs):
    rows, width = q.shape
    dim = wo.shape[1]
    vmem = pl.BlockSpec(memory_space=pltpu.VMEM)
    return pl.pallas_call(
        functools.partial(attn_fwd_kernel, len(kvs)),
        in_specs=[pl.BlockSpec(memory_space=pltpu.SMEM)] + [vmem] * (3 + len(kvs)),
        out_specs=[vmem, vmem],
        out_shape=[
            jax.ShapeDtypeStruct((rows, width), bf16),
            jax.ShapeDtypeStruct((rows, dim), bf16),
        ],
        scratch_shapes=[pltpu.VMEM((len(kvs) * rows, 2 * width), bf16)],
        compiler_params=pltpu.CompilerParams(vmem_limit_bytes=VMEM),
        cost_estimate=pl.CostEstimate(
            flops=10**6, bytes_accessed=10**6, transcendentals=0
        ),
    )(lo, q, start, wo, *kvs)


def attn_bwd_kernel(count_kv, lo_ref, q_ref, ga_ref, start_ref, wo_ref, cos_ref, sin_ref, *refs):
    kv_refs = refs[:count_kv]
    gq_ref, own_ref = refs[count_kv : count_kv + 2]
    rem_refs = refs[count_kv + 2 : 2 * count_kv + 1]
    kv_all, gkv = refs[2 * count_kv + 1 :]
    rows, width = q_ref.shape
    heads = width // HD
    base = (count_kv - 1) * rows
    for i, r in enumerate(kv_refs):
        kv_all[i * rows : (i + 1) * rows, :] = r[...]
        gkv[i * rows : (i + 1) * rows, :] = jnp.zeros((rows, 2 * width), f32)
    for i in range(rows // BQ):
        at = slice(i * BQ, (i + 1) * BQ)
        start = start_ref[:, at]
        row = base + i * BQ + lax.broadcasted_iota(jnp.int32, (BB, BQ), 1)
        col = lax.broadcasted_iota(jnp.int32, (BB, BQ), 0)
        gatt = dot_t(ga_ref[at, :], wo_ref[...]).astype(bf16)
        queries = [q_ref[at, h * HD : (h + 1) * HD] for h in range(heads)]
        gatts = [gatt[:, h * HD : (h + 1) * HD] for h in range(heads)]

        def step(kb, sums):
            off = pl.multiple_of(kb * BB, BB)
            here = col + off
            ok = (here >= start) & (here <= row)
            out = []
            for h in range(heads):
                ks = slice(h * HD, (h + 1) * HD)
                vs = slice(width + h * HD, width + (h + 1) * HD)
                k = kv_all[pl.ds(off, BB), ks]
                v = kv_all[pl.ds(off, BB), vs]
                e = jnp.exp2(
                    dot_t(k, queries[h]) * (-head_scale * LOG2E) - score_bias * LOG2E
                )
                sg = jnp.where(ok, 1.0 / (1.0 + e), 0.0)
                gs = (dot_t(v, gatts[h]) * sg * (1.0 - sg)).astype(bf16)
                gkv[pl.ds(off, BB), ks] += dot(gs, queries[h])
                gkv[pl.ds(off, BB), vs] += dot(sg.astype(bf16), gatts[h])
                out.append(sums[h] + t_dot(gs, k))
            return tuple(out)

        last = (base + (i + 1) * BQ - 1) // BB + 1
        sums = lax.fori_loop(
            lo_ref[i], last, step, tuple(jnp.zeros((BQ, HD), f32) for _ in range(heads))
        )
        cos, sin = cos_ref[at, :], sin_ref[at, :]
        for h in range(heads):
            t = sums[h] * head_scale
            gq_ref[at, h * HD : (h + 1) * HD] = (
                t * cos - pltpu.roll(t, HD // 2, 1) * sin
            ).astype(bf16)
    own_ref[:, :width] = gkv[base:, :width] * head_scale
    own_ref[:, width:] = gkv[base:, width:]
    for i, r in enumerate(rem_refs):
        r[:, :width] = (gkv[i * rows : (i + 1) * rows, :width] * head_scale).astype(bf16)
        r[:, width:] = gkv[i * rows : (i + 1) * rows, width:].astype(bf16)


def attn_bwd_call(lo, q, ga, start, wo, cos, sin, kvs):
    rows, width = q.shape
    vmem = pl.BlockSpec(memory_space=pltpu.VMEM)
    return pl.pallas_call(
        functools.partial(attn_bwd_kernel, len(kvs)),
        in_specs=[pl.BlockSpec(memory_space=pltpu.SMEM)] + [vmem] * (6 + len(kvs)),
        out_specs=[vmem] * (1 + len(kvs)),
        out_shape=[
            jax.ShapeDtypeStruct((rows, width), bf16),
            jax.ShapeDtypeStruct((rows, 2 * width), f32),
        ]
        + [jax.ShapeDtypeStruct((rows, 2 * width), bf16)] * (len(kvs) - 1),
        scratch_shapes=[
            pltpu.VMEM((len(kvs) * rows, 2 * width), bf16),
            pltpu.VMEM((len(kvs) * rows, 2 * width), f32),
        ],
        compiler_params=pltpu.CompilerParams(vmem_limit_bytes=VMEM),
        cost_estimate=pl.CostEstimate(
            flops=10**6, bytes_accessed=10**6, transcendentals=0
        ),
    )(lo, q, ga, start, wo, cos, sin, *kvs)


def norm_kernel(gh_ref, cot_ref, resid_ref, gain_ref, grad_ref, low_ref, part_ref):
    gh, resid, gain = gh_ref[...].astype(f32), resid_ref[...], gain_ref[...]
    inv = lax.rsqrt(jnp.mean(resid * resid, axis=-1, keepdims=True) + norm_eps)
    normed = resid * inv
    scaled = gh * gain
    grad = cot_ref[...].astype(f32) + inv * (
        scaled - normed * jnp.mean(scaled * normed, axis=-1, keepdims=True)
    )
    grad_ref[...] = grad
    low_ref[...] = grad.astype(bf16)
    part_ref[...] = jnp.sum(gh * normed, axis=0, keepdims=True)


def norm_call(gh, cot, resid, gain):
    vmem = pl.BlockSpec(memory_space=pltpu.VMEM)
    return pl.pallas_call(
        norm_kernel,
        in_specs=[vmem] * 4,
        out_specs=[vmem] * 3,
        out_shape=[
            jax.ShapeDtypeStruct(resid.shape, f32),
            jax.ShapeDtypeStruct(resid.shape, bf16),
            jax.ShapeDtypeStruct(gain.shape, f32),
        ],
    )(gh, cot, resid, gain)


def gqkv_kernel(gq_ref, own_ref, cos_ref, sin_ref, w_ref, *refs):
    got, g_ref, gh_ref = refs[:-2], refs[-2], refs[-1]
    width = gq_ref.shape[1]
    gkv = own_ref[...]
    for r in got:
        gkv = gkv + r[...].astype(f32)
    cos, sin = cos_ref[...], sin_ref[...]
    g_ref[:, :width] = gq_ref[...]
    for s in range(0, width, HD):
        t = gkv[:, s : s + HD]
        g_ref[:, width + s : width + s + HD] = (
            t * cos - pltpu.roll(t, HD // 2, 1) * sin
        ).astype(bf16)
    g_ref[:, 2 * width :] = gkv[:, width:].astype(bf16)
    gh_ref[...] = dot_t(g_ref[...], w_ref[...]).astype(bf16)


def gqkv_call(gq, own, got, cos, sin, w):
    rows, width = gq.shape
    dim = w.shape[0]
    block = lambda cols: pl.BlockSpec((BR, cols), lambda i: (i, 0))
    return pl.pallas_call(
        gqkv_kernel,
        grid=(rows // BR,),
        in_specs=[
            block(width),
            block(2 * width),
            block(HD),
            block(HD),
            pl.BlockSpec(w.shape, lambda i: (0, 0)),
        ]
        + [block(2 * width)] * len(got),
        out_specs=[block(3 * width), block(dim)],
        out_shape=[
            jax.ShapeDtypeStruct((rows, 3 * width), bf16),
            jax.ShapeDtypeStruct((rows, dim), bf16),
        ],
        compiler_params=pltpu.CompilerParams(vmem_limit_bytes=VMEM),
        cost_estimate=pl.CostEstimate(
            flops=2 * rows * dim * 3 * width, bytes_accessed=16 * 2**20, transcendentals=0
        ),
    )(gq, own, cos, sin, w, *got)


def grads_kernel(groups, index_ref, h_ref, g_ref, *refs):
    size = refs[0].shape[1]
    for j in range(h_ref.shape[1] // size):
        at = pl.multiple_of((index_ref[0] ^ j) * size, size)
        grad = t_dot(h_ref[:, pl.ds(at, size)], g_ref[...])
        for ref, (first, columns, members) in zip(refs, groups):
            if j in members:
                ref[members.index(j)] = grad[:, first : first + columns].astype(ref.dtype)


def grads_call(index, h, g, count):
    rows, width = g.shape
    size = h.shape[1] // count
    if count == 4:
        half = width // 2
        groups = [(0, half, (1, 3)), (half, half, (2, 3)), (0, half, (0, 2)), (half, half, (0, 1))]
        kinds = [bf16, bf16, f32, f32]
    else:
        groups = [(0, width, (j,)) for j in range(count)]
        kinds = [f32] + [bf16] * (count - 1)
    vmem = pl.BlockSpec(memory_space=pltpu.VMEM)
    return pl.pallas_call(
        functools.partial(grads_kernel, groups),
        in_specs=[pl.BlockSpec(memory_space=pltpu.SMEM), vmem, vmem],
        out_specs=[vmem] * len(groups),
        out_shape=[
            jax.ShapeDtypeStruct((len(members), size, columns), kind)
            for (_, columns, members), kind in zip(groups, kinds)
        ],
        compiler_params=pltpu.CompilerParams(vmem_limit_bytes=VMEM),
        cost_estimate=pl.CostEstimate(
            flops=2 * rows * width * h.shape[1], bytes_accessed=9 * 2**20, transcendentals=0
        ),
    )(index, h, g)


def ffn_kernel(places, blocks, groups, h_ref, c_ref, *refs):
    count = 1 + max(p[1] for p in places)
    sources = refs[:count]
    outs = refs[count : count + 3 * len(groups)]
    inner_ref, gh_ref, wg, wu, wd, gates, ups, sem = refs[count + 3 * len(groups) :]
    width = wg.shape[1] // blocks
    copies = [
        (which, pltpu.make_async_copy(sources[source].at[at], (wg, wu, wd)[which].at[to], sem.at[i]))
        for i, (which, source, at, to) in enumerate(places)
    ]
    first = pl.program_id(0) == 0

    def wait(weight):
        @pl.when(first)
        def _():
            for which, c in copies:
                if which == weight:
                    c.wait()

    @pl.when(first)
    def _():
        for weight in range(3):
            for which, c in copies:
                if which == weight:
                    c.start()

    wait(0)
    gate = dot(h_ref[...], wg[...])
    wait(1)
    up = dot(h_ref[...], wu[...])
    wait(2)
    grad = dot_t(c_ref[...], wd[...])
    sig = 1.0 / (1.0 + jnp.exp2(gate * -LOG2E))
    act = gate * sig
    inner = (act * up).astype(bf16)
    gg = (grad * up * sig * (1.0 + gate * (1.0 - sig))).astype(bf16)
    gu = (grad * act).astype(bf16)
    inner_ref[...] = inner
    gates[...] = gg
    ups[...] = gu
    for n, members in enumerate(groups):
        for m, j in enumerate(members):
            at, to = slice(j * width, (j + 1) * width), slice(m * width, (m + 1) * width)
            outs[n][:, to] = inner[:, at]
            outs[len(groups) + n][:, to] = gg[:, at]
            outs[2 * len(groups) + n][:, to] = gu[:, at]
    gh_ref[...] = (dot_t(gates[...], wg[...]) + dot_t(ups[...], wu[...])).astype(bf16)


def ffn_call(h, cot, sources, places, blocks, width, groups):
    rows, dim = h.shape
    hidden = blocks * width
    block = lambda cols: pl.BlockSpec((BR, cols), lambda i: (i, 0))
    sizes = [len(members) * width for members in groups] * 3 + [hidden, dim]
    result = pl.pallas_call(
        functools.partial(ffn_kernel, places, blocks, groups),
        grid=(rows // BR,),
        in_specs=[block(dim), block(dim)] + [pl.BlockSpec(memory_space=pl.ANY)] * len(sources),
        out_specs=[block(size) for size in sizes],
        out_shape=[jax.ShapeDtypeStruct((rows, size), bf16) for size in sizes],
        scratch_shapes=[
            pltpu.VMEM((dim, hidden), bf16),
            pltpu.VMEM((dim, hidden), bf16),
            pltpu.VMEM((hidden, dim), bf16),
            pltpu.VMEM((BR, hidden), bf16),
            pltpu.VMEM((BR, hidden), bf16),
            pltpu.SemaphoreType.DMA((len(places),)),
        ],
        compiler_params=pltpu.CompilerParams(vmem_limit_bytes=VMEM),
        cost_estimate=pl.CostEstimate(
            flops=10 * rows * dim * hidden, bytes_accessed=36 * 2**20, transcendentals=10**6
        ),
    )(h, cot, *sources)
    n = len(groups)
    down = [p for p in places if p[0] == 2]
    base = min(p[1] for p in down)
    project = functools.partial(
        down_call, sources=sources[base:], places=[(p[1] - base,) + p[2:] for p in down]
    )
    return result[:n], result[n : 2 * n], result[2 * n : 3 * n], result[-2], project, result[-1]


def down_kernel(places, inner_ref, *refs):
    sources, (y_ref, wd, sem) = refs[:-3], refs[-3:]

    @pl.when(pl.program_id(0) == 0)
    def _():
        copies = [
            pltpu.make_async_copy(sources[source].at[at], wd.at[to], sem.at[i])
            for i, (source, at, to) in enumerate(places)
        ]
        for c in copies:
            c.start()
        for c in copies:
            c.wait()

    y_ref[...] = dot(inner_ref[...], wd[...]).astype(bf16)


def down_call(inner, sources, places):
    rows, hidden = inner.shape
    dim = max(to[1].stop or 0 for _, _, to in places) or sources[0].shape[-1]
    block = lambda cols: pl.BlockSpec((BR, cols), lambda i: (i, 0))
    return pl.pallas_call(
        functools.partial(down_kernel, tuple(places)),
        grid=(rows // BR,),
        in_specs=[block(hidden)] + [pl.BlockSpec(memory_space=pl.ANY)] * len(sources),
        out_specs=block(dim),
        out_shape=jax.ShapeDtypeStruct((rows, dim), bf16),
        scratch_shapes=[
            pltpu.VMEM((hidden, dim), bf16),
            pltpu.SemaphoreType.DMA((len(places),)),
        ],
        compiler_params=pltpu.CompilerParams(vmem_limit_bytes=VMEM),
        cost_estimate=pl.CostEstimate(
            flops=2 * rows * dim * hidden, bytes_accessed=12 * 2**20, transcendentals=0
        ),
    )(inner, *sources)


PAIRS = ((0, 2), (1, 3), (2, 3), (0, 1))


def ffn_pieces(h, cot, gate_up, down, width):
    sources, places = [], []
    for pieces, kinds in ((gate_up, (0, 1)), (down, (2,))):
        for j, parts in enumerate(pieces):
            block = 0
            for part in parts:
                size = part.shape[2] if kinds == (2,) else part.shape[1] // 2
                for i in range(part.shape[0]):
                    rows = slice(block * size, (block + 1) * size)
                    cols = slice(j * width, (j + 1) * width)
                    for which in kinds:
                        at = (i, slice(which * size, (which + 1) * size)) if which < 2 else (i,)
                        to = (rows, cols) if which < 2 else (cols, rows)
                        places.append((which, len(sources), at, to))
                    block += 1
                sources.append(part)
    return ffn_call(h, cot, sources, tuple(places), len(down), width, PAIRS)


def ffn_plain(h, cot, gate_up, down):
    size = gate_up[0][0].shape[1] // 2
    merge = lambda parts: jnp.concatenate(parts, axis=0)
    flat = lambda p, at: merge(p)[:, at].reshape(-1, p[0].shape[-1])
    tall = lambda p: merge(p).transpose(1, 0, 2).reshape(p[0].shape[1], -1)
    sources = [
        jnp.concatenate([flat(p, slice(0, size)) for p in gate_up], axis=1),
        jnp.concatenate([flat(p, slice(size, 2 * size)) for p in gate_up], axis=1),
        jnp.concatenate([tall(p) for p in down], axis=0),
    ]
    every = (slice(None), slice(None))
    places = tuple((which, which, every, every) for which in range(3))
    return ffn_call(h, cot, sources, places, 1, sources[0].shape[1], ((0,),))


def xor_permute(x, count, flip):
    return lax.ppermute(x, "uly", [(i, i ^ flip) for i in range(count)])


def gather_uly(x, count):
    return gather_rest(gather_first(x, count), count)


def gather_first(x, count):
    return [x] + [xor_permute(x, count, j) for j in ((1, 2) if count == 4 else range(1, count))]


def gather_rest(blocks, count):
    if count != 4:
        return [[block] for block in blocks]
    x, one, two = blocks
    half = x.shape[0] // 2
    low = xor_permute(one[:half], count, 2)
    high = xor_permute(two[half:], count, 1)
    return [[x], [one], [two], [low, high]]


def in_order(pieces, index):
    rows = sum(p.shape[0] for p in pieces[0])
    out = jnp.zeros((len(pieces) * rows,) + pieces[0][0].shape[1:], pieces[0][0].dtype)
    for j, parts in enumerate(pieces):
        at = (index ^ j) * rows
        for part in parts:
            out = lax.dynamic_update_slice_in_dim(out, part, at, 0)
            at = at + part.shape[0]
    return out


def scatter_uly(own, others, count):
    got = [xor_permute(block, count, j + 1) for j, block in enumerate(others)]
    for block in got:
        own = own + block.astype(f32)
    return own


def after(x, *earlier):
    return lax.optimization_barrier((x,) + earlier)[0]


def rms_stats(values):
    scale_inv = lax.rsqrt(jnp.mean(values * values, axis=-1, keepdims=True) + norm_eps)
    return (values * scale_inv, scale_inv)


def norm_back(grad_normed, normed, scale_inv, gain):
    scaled = grad_normed * gain
    return scale_inv * (scaled - normed * jnp.mean(scaled * normed, axis=-1, keepdims=True))


def body(
    block_input,
    cotangent,
    lengths,
    seq_order,
    norm_attn,
    w_query,
    w_key,
    w_value,
    w_out,
    norm_ffn,
    w_gate,
    w_up,
    w_down,
):
    count_uly = lax.axis_size("uly")
    count_blk = lax.axis_size("blk")
    devices = count_uly * count_blk
    uly_index = lax.axis_index("uly")
    uly_at = uly_index.astype(jnp.int32).reshape(1)
    tok_rows, dim = block_input.shape
    group = count_blk * tok_rows
    part = dim // count_blk
    rows_w = w_query.shape[0]
    together = lax.optimization_barrier
    longest = LONGEST.get(devices * tok_rows, devices * tok_rows)
    back = min(count_uly - 1, -(-(longest - 1) // group))

    labels = jnp.arange(lengths.shape[0], dtype=jnp.int32)
    picked = jnp.sum(
        jnp.where(seq_order[:, None] == labels[None, :], lengths[None, :], 0), axis=1
    )
    ends = jnp.sum(jnp.where(labels[None, :] <= labels[:, None], picked[None, :], 0), axis=1)
    starts = ends - picked
    row_ids = uly_index * group + jnp.arange(group, dtype=jnp.int32)
    inside = (row_ids[:, None] >= starts[None, :]) & (row_ids[:, None] < ends[None, :])
    seq_start = jnp.sum(jnp.where(inside, starts[None, :], 0), axis=1)
    position = row_ids - seq_start
    used = jnp.any(inside, axis=1)
    shift = (uly_index - back) * group
    begin = jnp.where(used, seq_start - shift, 1 << 30).astype(jnp.int32)
    firsts = begin[::BQ]
    finals = back * group + jnp.arange(group // BQ, dtype=jnp.int32) * BQ + BQ - 1
    low_kb, low_bb = (
        jnp.minimum(firsts // size, finals // size + 1).astype(jnp.int32) for size in (BK, BB)
    )
    frequency = rope_base ** (-jnp.arange(HD // 2, dtype=f32) * 2.0 / HD)
    angles = position.astype(f32)[:, None] * frequency[None, :]
    cos, sin = jnp.cos(angles), jnp.sin(angles)
    cos = jnp.concatenate([cos, cos], axis=1)
    sin = jnp.concatenate([-sin, sin], axis=1)

    owner = [(i, (i % count_uly) * count_blk + i // count_uly) for i in range(devices)]
    wo = lax.ppermute(w_out, BOTH, owner)
    gains = jnp.concatenate([norm_attn, norm_ffn])
    gains = jnp.pad(gains[None], ((0, 15), (0, 3 * part - 2 * rows_w)))
    qkv = pack_call(w_query, w_key, w_value, gains, count_blk)
    qkv = lax.all_to_all(qkv, "blk", 0, 0, tiled=True)
    group_in = lax.all_gather(after(block_input, qkv, wo), "blk", axis=0, tiled=True)
    qkv_pieces = gather_uly(qkv, count_uly)
    cut = lambda f: in_order([[f(p) for p in parts] for parts in qkv_pieces], uly_index)
    w_qkv = cut(lambda p: p[:, :rows_w].reshape(-1, 3 * part))
    gains = cut(lambda p: p[:, rows_w, : 2 * rows_w])
    gain_attn = gains[:, :rows_w].reshape(1, dim).astype(f32)
    gain_ffn = gains[:, rows_w:].reshape(1, dim).astype(f32)

    rows_d, width = w_gate.shape[0], w_gate.shape[1] // count_blk
    columns = lambda w: w.reshape(rows_d, count_blk, width).transpose(1, 0, 2)
    to_hidden = lambda w: lax.all_to_all(w, "blk", 0, 0, tiled=True)
    gate_up = jnp.concatenate([columns(w_gate), columns(w_up)], axis=1)
    down = to_hidden(
        after(w_down.reshape(count_blk, width, rows_d), *[p[0] for p in qkv_pieces[1:3]])
    )
    wo = in_order(gather_uly(after(wo, qkv_pieces[3][-1]), count_uly), uly_index)
    group_in, gate_up, wo = together((group_in, gate_up, wo))
    hidden_one, query, kv = qkv_call(group_in, gain_attn, w_qkv, cos, sin)
    kv, query, down = together((kv, query, down))
    if count_uly == 4 and back == 2:
        half = group // 2
        two = lax.ppermute(kv, "uly", [(0, 2), (1, 3)])
        one = lax.ppermute(kv, "uly", [(0, 1), (2, 3)])
        over = lax.ppermute(kv[:half], "uly", [(1, 0)])
        over = lax.ppermute(over, "uly", [(0, 2)])
        under = lax.ppermute(two[half:], "uly", [(3, 2)])
        kvs = [two, one + jnp.concatenate([over, under]), kv]
    else:
        kvs = [
            lax.ppermute(kv, "uly", [(i, i + s) for i in range(count_uly - s)])
            for s in range(back, 0, -1)
        ] + [kv]

    gate_up = to_hidden(after(gate_up, kv))
    group_cot = lax.all_gather(after(cotangent, kv), "blk", axis=0, tiled=True)
    down = gather_first(after(down, kv), count_uly)
    query, down = together((query, down))
    attended, out_part = attn_fwd_call(low_kb, query, begin[:, None], wo, kvs)
    out_part, gate_up, group_cot = together((out_part, gate_up, group_cot))
    gate_up = gather_first(gate_up, count_uly)
    out_own = lax.psum_scatter(out_part, "blk", scatter_dimension=0, tiled=True)
    out_own, gate_up = together((out_own, gate_up))
    gate_up = gather_rest(gate_up, count_uly)
    down = gather_rest(down, count_uly)
    input_f = block_input.astype(f32)
    resid = input_f + out_own.astype(f32)
    hidden_two = (rms_stats(resid)[0] * gain_ffn).astype(bf16)
    group_hidden = lax.all_gather(hidden_two, "blk", axis=0, tiled=True)

    pairs = count_uly == 4 and width % HD == 0
    if pairs:
        ffn = ffn_pieces(group_hidden, group_cot, gate_up, down, width)
    else:
        ffn = ffn_plain(group_hidden, group_cot, gate_up, down)
    inner, gg, gu, inner_all, project, gh_part = ffn
    grad_h2 = lax.psum_scatter(gh_part, "blk", scatter_dimension=0, tiled=True)

    def products(lefts, rights, rows):
        half = dim // 2
        if rows:
            halves = (rights[:, :half], rights[:, half:])
            term = [t_dot(lefts[n], halves[n // 2]) for n in range(4)]
        else:
            halves = (lefts[:, :half], lefts[:, half:])
            term = [t_dot(halves[n // 2], rights[n]) for n in range(4)]
        return [term[1].astype(bf16), term[2].astype(bf16), term[0], term[3]]

    def first_phase(term):
        return [
            xor_permute(term[0], count_uly, 1),
            xor_permute(term[1], count_uly, 2),
            term[2],
            term[3],
        ]

    def second_phase(term, rows):
        axis = 0 if rows else 1
        one, two = (k + g.astype(f32) for k, g in zip(term[2:], term[:2]))
        mine = [lax.slice_in_dim(t, 0, width, axis=axis) for t in (one, two)]
        rest = [lax.slice_in_dim(t, width, 2 * width, axis=axis).astype(bf16) for t in (one, two)]
        mine[0] = mine[0] + xor_permute(rest[0], count_uly, 2).astype(f32)
        mine[1] = mine[1] + xor_permute(rest[1], count_uly, 1).astype(f32)
        return jnp.concatenate(mine, axis=1 - axis).astype(bf16)

    def direct(lefts, rights, rows):
        cut = lambda a: [a[0][:, j * width : (j + 1) * width] for j in range(count_uly)]
        if rows:
            terms = [t_dot(left, rights) for left in cut(lefts)]
        else:
            terms = [t_dot(lefts, right) for right in cut(rights)]
        return scatter_uly(terms[0], [t.astype(bf16) for t in terms[1:]], count_uly).astype(bf16)

    if pairs:
        sum_gate = second_phase(first_phase(products(group_hidden, gg, False)), False)
        sum_up = products(group_hidden, gu, False)
        sum_down = products(inner, group_cot, True)
    else:
        sum_gate = direct(group_hidden, gg, False)
        sum_up = direct(group_hidden, gu, False)
        sum_down = direct(inner, group_cot, True)
    grad_h2, sum_gate, sum_up, sum_down, inner_all = together(
        (grad_h2, sum_gate, sum_up, sum_down, inner_all)
    )
    y_part = project(inner_all)
    if pairs:
        sum_up = second_phase(first_phase(sum_up), False)
        sum_down = second_phase(first_phase(sum_down), True)
    grad_resid, grad_low, gain_part = norm_call(grad_h2, cotangent, resid, gain_ffn)
    group_gattn = lax.all_gather(grad_low, "blk", axis=0, tiled=True)
    blocks_of = lambda w: w.reshape(count_blk, rows_d, width)
    gain_part = gain_part.astype(bf16).reshape(count_blk, -1, width)
    gain_rows = gain_part.shape[1]
    gain_part = jnp.pad(gain_part, ((0, 0), (0, -gain_rows % 8), (0, 0)))
    grad_gate = to_hidden(jnp.concatenate([blocks_of(sum_gate), gain_part], axis=1))
    gattn, sum_up, sum_down, grad_gate, y_part = together(
        (group_gattn, sum_up, sum_down, grad_gate, y_part)
    )

    down_blocks = sum_down.reshape(width, count_blk, rows_d).transpose(1, 0, 2)
    grads_ud = to_hidden(
        jnp.concatenate(
            [blocks_of(sum_up), down_blocks.reshape(count_blk, rows_d, width)], axis=1
        )
    )
    gq, gkv, *sent = attn_bwd_call(
        low_bb, query, gattn, begin[None, :], wo, cos, sin, kvs
    )
    got = [
        lax.ppermute(block, "uly", [(i, i - s) for i in range(s, count_uly)])
        for s, block in zip(range(back, 0, -1), sent)
    ]
    y_own = lax.psum_scatter(after(y_part, gattn), "blk", scatter_dimension=0, tiled=True)
    def split_rows(whole):
        rows = whole.shape[0] // count_uly
        pick = lambda j: lax.dynamic_slice_in_dim(whole, (uly_index ^ j) * rows, rows, 0)
        return scatter_uly(
            pick(0).astype(f32), [pick(j) for j in range(1, count_uly)], count_uly
        ).astype(bf16)

    gain_sum = jnp.sum(grad_gate[:, rows_d:][:, :gain_rows].astype(f32), axis=0)
    gain_sum = jnp.pad(gain_sum.reshape(part, 1), ((0, 0), (0, HD - 1)))
    outs = jnp.concatenate([t_dot(after(attended, gq), gattn), gain_sum], axis=1).astype(bf16)
    outs = split_rows(after(outs, gq))
    gkv, y_own, grads_ud, outs = together((gkv, y_own, grads_ud, outs))
    output = (resid + y_own.astype(f32)).astype(bf16)
    gqkv, gh1_part = gqkv_call(gq, gkv, got, cos, sin, w_qkv)
    grads = grads_call(uly_at, hidden_one, gqkv, count_uly)
    grad_h1 = lax.psum_scatter(gh1_part, "blk", scatter_dimension=0, tiled=True).astype(f32)
    normed_one, inv_one = rms_stats(input_f)
    input_grad = grad_resid + norm_back(grad_h1, normed_one, inv_one, gain_attn)

    if count_uly == 4:
        one = grads[2] + xor_permute(grads[0], count_uly, 1).astype(f32)
        two = grads[3] + xor_permute(grads[1], count_uly, 2).astype(f32)
        one = one[0] + xor_permute(one[1].astype(bf16), count_uly, 2).astype(f32)
        two = two[0] + xor_permute(two[1].astype(bf16), count_uly, 1).astype(f32)
        grads = jnp.concatenate([one, two], axis=1).astype(bf16)
    else:
        grads = scatter_uly(grads[0][0], [g[0] for g in grads[1:]], count_uly).astype(bf16)
    outs = lax.ppermute(after(outs, grads), BOTH, [(j, i) for i, j in owner])
    outs = outs.astype(f32)
    grad_out, grad_gain_ffn = outs[:, :dim], outs[:, dim]
    grads = lax.all_to_all(grads.reshape(count_blk, rows_w, 3 * part), "blk", 0, 0, tiled=True)
    grad_gate = grad_gate[:, :rows_d].astype(f32).transpose(1, 0, 2).reshape(w_gate.shape)
    grad_up = grads_ud[:, :rows_d].astype(f32).transpose(1, 0, 2).reshape(w_up.shape)
    grad_down = grads_ud[:, rows_d:].astype(f32).reshape(w_down.shape)
    grads, *_ = together((grads, grad_gate, grad_up, grad_down, input_grad, grad_out, grad_gain_ffn))
    grad_query, grad_key, grad_value, grad_gain_attn = unpack_call(
        grads, w_query, w_key, w_value, norm_attn.astype(f32)[:, None]
    )
    return (
        output,
        input_grad,
        grad_gain_attn[:, 0],
        grad_query,
        grad_key,
        grad_value,
        grad_out,
        grad_gain_ffn,
        grad_gate,
        grad_up,
        grad_down,
    )


def solution(mesh):
    rows = P(("uly", "blk"), None)
    vector = P(("uly", "blk"))
    weights = (vector, rows, rows, rows, rows, vector, P("blk", "uly"), P("blk", "uly"), P("uly", "blk"))
    return jax.shard_map(
        body,
        mesh=mesh,
        in_specs=(rows, rows, P(), P()) + weights,
        out_specs=(rows, rows) + weights,
        check_vma=False,
    )
```
